128 devices in a mesh: pb: 32 (over x, y, core), pa: 4 (over z).
Axes of the slice: x: 4, y: 4, z: 4, core: 2. Of those that a mesh axis runs over, the one named last changes fastest.
Arguments:
- queries: bfloat16 [4096, 4096], P(('pb', 'pa')), may hold values from -4 to 4
- passages: bfloat16 [16384, 4096], P(('pb', 'pa')), may hold values from -4 to 4
- query_cluster: int32 [4096], P(('pb', 'pa')), may hold values from 0 to 255, as said below
- passage_cluster: int32 [16384], P(('pb', 'pa')), may hold values from 0 to 511, as said below
- allowed: int32 [256, 16], replicated, may hold values from 0 to 1, as said below
- positive: int32 [4096], P(('pb', 'pa')), may hold values from 0 to 16383, as said below
Outputs:
- grad_queries: bfloat16 [4096, 4096], P(('pb', 'pa'))
- grad_passages: bfloat16 [16384, 4096], P(('pb', 'pa'))
The draws below stay inside these ranges and needn't reach their ends.
Inputs may be any that keep to these rules, and one draw needn't show every extreme that they name: `query_cluster`: on each device's rows, at most 2 queries have a cluster in any one block of 8 consecutive clusters, and some block has exactly 2. `passage_cluster`: on each device's rows, at most 2 passages have a cluster in any one block of 4 consecutive clusters, and some block has exactly 2. allowed[query_cluster[i], passage_cluster[positive[i]] - (query_cluster[i] // 8) * 16] == 1 for every query i. passage_cluster[positive[i]] // 16 == query_cluster[i] // 8 for every query i.
All inputs are finite; a program needn't handle non-finite values.
Results may differ from the reference program's by a relative error of at most 0.012.
Values may be sent and summed in bfloat16 or wider, within the bound.
A program may use at most 64 MiB of HBM per device.

```python
import math
import jax
import jax.numpy as jnp
from jax import lax

D = 4096
Q_DEV = 32
QCL = 8
PCL = 4
P_DEV = 128
QCAP = 2
PCAP = 2
MCOL = 16
NQC = 256
TOTQ = 4096
TOTP = 16384
N_PB = 32
N_PA = 4
DEVICES = 128


def pick_targets(key, per_device, capacity, num_targets):
    total_slots = capacity * num_targets
    key_perm, key_full, key_mix = jax.random.split(key, 3)
    priority = jax.vmap(lambda subkey: jax.random.permutation(subkey, total_slots))(jax.random.split(key_perm, DEVICES))
    priority = priority.astype(jnp.int32)
    filled = jax.random.randint(key_full, (DEVICES, 1), 0, num_targets)
    slot_ids = jnp.arange(total_slots, dtype=jnp.int32)[None, :]
    priority = jnp.where(slot_ids // capacity == filled, -1 - slot_ids, priority)
    chosen = jnp.argsort(priority, axis=1, stable=True)[:, :per_device]
    shuffle = jax.vmap(lambda subkey: jax.random.permutation(subkey, per_device))(jax.random.split(key_mix, DEVICES))
    chosen = jnp.take_along_axis(chosen, shuffle, axis=1)
    return (chosen // capacity).astype(jnp.int32).reshape(-1)


def integer_tables(key):
    key_q, key_p, key_qc, key_pc, key_pos, key_mask, key_riv = jax.random.split(jax.random.fold_in(key, 11), 7)
    query_rows = pick_targets(key_q, Q_DEV, QCAP, N_PB)
    passage_owners = pick_targets(key_p, P_DEV, PCAP, DEVICES)
    query_cl = query_rows * QCL + jax.random.randint(key_qc, (TOTQ,), 0, QCL)
    passage_cl = passage_owners * PCL + jax.random.randint(key_pc, (TOTP,), 0, PCL)
    passage_rows = passage_cl // MCOL
    by_row = jnp.argsort(passage_rows, stable=True).astype(jnp.int32)
    row_counts = jnp.sum((passage_rows[None, :] == jnp.arange(N_PB, dtype=jnp.int32)[:, None]).astype(jnp.int32), axis=1)
    row_starts = jnp.cumsum(row_counts) - row_counts
    offsets = jax.random.randint(key_pos, (TOTQ,), 0, 1 << 20)
    row_count = jnp.maximum(row_counts[query_rows], 1)
    first = offsets % row_count
    onward = 1 + jax.random.randint(key_riv, (TOTQ,), 0, 1 << 20) % jnp.maximum(row_count - 1, 1)
    positive = by_row[row_starts[query_rows] + first]
    rival = by_row[row_starts[query_rows] + (first + onward) % row_count]
    marked = (jnp.arange(TOTQ, dtype=jnp.int32) % 61 == 7).astype(jnp.int32)
    pair_mask = jax.random.randint(key_mask, (NQC, MCOL), 0, 2)
    pair_mask = pair_mask.at[query_cl, passage_cl[positive] - query_rows * MCOL].set(1)
    pair_mask = pair_mask.at[query_cl, passage_cl[rival] - query_rows * MCOL].max(marked)
    return (query_cl.astype(jnp.int32), passage_cl.astype(jnp.int32), pair_mask.astype(jnp.int32), positive.astype(jnp.int32), rival.astype(jnp.int32))


def passage_matrix(key):
    key_normal = jax.random.fold_in(jax.random.fold_in(key, 21), 0)
    key_scale = jax.random.fold_in(jax.random.fold_in(key, 21), 2)
    values = jax.random.normal(key_normal, (TOTP, D))
    scales = jnp.exp(jax.random.uniform(key_scale, (TOTP, 1), minval=math.log(0.3), maxval=math.log(3.0)))
    return values * scales / math.sqrt(D)


def draw_query_cluster(key, part):
    tables = integer_tables(key)
    return tables[0]


def draw_passage_cluster(key, part):
    tables = integer_tables(key)
    return tables[1]


def draw_allowed(key, part):
    tables = integer_tables(key)
    return tables[2]


def draw_positive(key, part):
    tables = integer_tables(key)
    return tables[3]


def draw_passages(key, part):
    values = passage_matrix(key)
    return values.astype(jnp.bfloat16)


def draw_queries(key, part):
    key = jax.random.fold_in(key, 6)
    key_normal = jax.random.fold_in(key, 0)
    key_scale = jax.random.fold_in(key, 2)
    row_scale = jnp.exp(jax.random.uniform(key_scale, (TOTQ, 1), minval=math.log(0.3), maxval=math.log(3.0)))
    return (jax.random.normal(key_normal, (TOTQ, D)) * row_scale / math.sqrt(D)).astype(jnp.bfloat16)


def setup_inputs(seed: int = 0) -> dict:
    keys = jax.random.split(jax.random.key(seed), 7)
    return {
        "queries": draw_queries(jax.random.fold_in(keys[6], 71), 0),
        "passages": draw_passages(jax.random.fold_in(keys[6], 71), 0),
        "query_cluster": draw_query_cluster(jax.random.fold_in(keys[6], 71), 0),
        "passage_cluster": draw_passage_cluster(jax.random.fold_in(keys[6], 71), 0),
        "allowed": draw_allowed(jax.random.fold_in(keys[6], 71), 0),
        "positive": draw_positive(jax.random.fold_in(keys[6], 71), 0),
    }


inv_temp = 50.0
neg_fill = -1e30


def slot_ranks(targets, num_targets):
    one_hot = (targets[..., None] == jnp.arange(num_targets, dtype=jnp.int32)).astype(jnp.int32)
    return jnp.sum((jnp.cumsum(one_hot, axis=-2) - one_hot) * one_hot, axis=-1)


def block_grads(query_block, query_ids, passage_block, passage_ids, row_index, query_cluster, passage_cluster, allowed, positive):
    query_live = query_ids >= 0
    query_safe = jnp.where(query_live, query_ids, 0)
    query_local = jnp.where(query_live, query_cluster[query_safe] % QCL, -1)
    wanted = jnp.where(query_live, positive[query_safe], -2)
    passage_live = passage_ids >= 0
    passage_safe = jnp.where(passage_live, passage_ids, 0)
    passage_local = jnp.where(passage_live, passage_cluster[passage_safe] - row_index * MCOL, -1)
    pair_table = lax.dynamic_slice_in_dim(allowed, (row_index * QCL).astype(jnp.int32), QCL, 0).astype(jnp.float32)
    query_onehot = (query_local[:, None] == jnp.arange(QCL, dtype=jnp.int32)[None, :]).astype(jnp.float32)
    passage_onehot = (passage_local[:, None] == jnp.arange(MCOL, dtype=jnp.int32)[None, :]).astype(jnp.float32)
    reach = jnp.dot(query_onehot, pair_table, precision=lax.Precision.HIGHEST)
    permitted = jnp.dot(reach, passage_onehot.T, precision=lax.Precision.HIGHEST) > 0.5
    targets = ((wanted[:, None] == passage_ids[None, :]) & passage_live[None, :]).astype(jnp.float32)
    scores = jnp.dot(query_block, passage_block.T, preferred_element_type=jnp.float32) * inv_temp
    row_top = jnp.max(jnp.where(permitted, scores, neg_fill), axis=1)
    exp_terms = jnp.where(permitted, jnp.exp(scores - row_top[:, None]), 0.0)
    row_total = jnp.sum(exp_terms, axis=1)
    softmax_p = exp_terms / jnp.where(row_total > 0.0, row_total, 1.0)[:, None]
    grad_scores = ((softmax_p - targets) * inv_temp).astype(jnp.bfloat16)
    column_slots = passage_block.shape[0] // N_PA
    query_sum = jnp.zeros((query_block.shape[0], D), jnp.float32)
    for column in range(N_PA):
        column_part = jnp.dot(grad_scores[:, column * column_slots:(column + 1) * column_slots],
                              passage_block[column * column_slots:(column + 1) * column_slots],
                              preferred_element_type=jnp.float32)
        query_sum = query_sum + lax.optimization_barrier(column_part.astype(jnp.bfloat16)).astype(jnp.float32)
    passage_grad = jnp.dot(grad_scores.T, query_block, preferred_element_type=jnp.float32).astype(jnp.bfloat16)
    return query_sum.astype(jnp.bfloat16), passage_grad


def reference(queries, passages, query_cluster, passage_cluster, allowed, positive):
    source = jnp.arange(DEVICES, dtype=jnp.int32)[:, None]
    query_dest = (query_cluster // QCL).reshape(DEVICES, Q_DEV)
    query_rank = slot_ranks(query_dest, N_PB)
    query_slots = DEVICES * QCAP
    query_pos = (query_dest * query_slots + source * QCAP + query_rank).reshape(-1)
    query_buffer = jnp.zeros((N_PB * query_slots, D), jnp.bfloat16).at[query_pos].set(queries)
    query_ids = jnp.full((N_PB * query_slots,), -1, jnp.int32).at[query_pos].set(jnp.arange(TOTQ, dtype=jnp.int32))
    passage_dest = (passage_cluster // PCL).reshape(DEVICES, P_DEV)
    passage_rank = slot_ranks(passage_dest, DEVICES)
    passage_slots = DEVICES * PCAP
    passage_pos = (passage_dest * passage_slots + source * PCAP + passage_rank).reshape(-1)
    passage_buffer = jnp.zeros((DEVICES * passage_slots, D), jnp.bfloat16).at[passage_pos].set(passages)
    passage_ids = jnp.full((DEVICES * passage_slots,), -1, jnp.int32).at[passage_pos].set(jnp.arange(TOTP, dtype=jnp.int32))
    row_slots = N_PA * passage_slots

    def one_row(row_index):
        query_block = lax.dynamic_slice_in_dim(query_buffer, (row_index * query_slots).astype(jnp.int32), query_slots, 0)
        query_block_ids = lax.dynamic_slice_in_dim(query_ids, (row_index * query_slots).astype(jnp.int32), query_slots, 0)
        passage_block = lax.dynamic_slice_in_dim(passage_buffer, (row_index * row_slots).astype(jnp.int32), row_slots, 0)
        passage_block_ids = lax.dynamic_slice_in_dim(passage_ids, (row_index * row_slots).astype(jnp.int32), row_slots, 0)
        return block_grads(query_block, query_block_ids, passage_block, passage_block_ids, row_index,
                           query_cluster, passage_cluster, allowed, positive)

    query_grads, passage_grads = lax.map(one_row, jnp.arange(N_PB, dtype=jnp.int32))
    grad_queries = query_grads.reshape(-1, D)[query_pos]
    grad_passages = passage_grads.reshape(-1, D)[passage_pos]
    return grad_queries, grad_passages
```

```python
import functools

import jax
import jax.numpy as jnp
from jax import lax
from jax.experimental import pallas as pl
from jax.experimental.pallas import tpu as pltpu
from jax.sharding import PartitionSpec as P

MESH = pl.DeviceIdType.MESH
F32, BF16, I32 = jnp.float32, jnp.bfloat16, jnp.int32
D = 4096
NB = 32
NZ = 4
QW = 512
PW = 2048
CT = 512
SCALE = 50.0
FILL = -1e30


def iota(shape, dim):
    return lax.broadcasted_iota(I32, shape, dim)


def shr(a, n):
    return lax.shift_right_logical(a, jnp.full(a.shape, n, I32))


def hot(cond):
    return jnp.where(cond, 1.0, 0.0).astype(BF16)


def nn(a, b):
    return lax.dot_general(a, b, (((1,), (0,)), ((), ())), preferred_element_type=F32)


def nt(a, b):
    return lax.dot_general(a, b, (((1,), (1,)), ((), ())), preferred_element_type=F32)


def tn(a, b):
    return lax.dot_general(a, b, (((0,), (0,)), ((), ())), preferred_element_type=F32)


def cols(j, width=CT):
    return pl.ds(pl.multiple_of(j * width, width), width)


def rows16(i):
    return pl.ds(pl.multiple_of(i * 16, 16), 16)


def kernel(
    q_ref, p_ref, ints_ref, allowed_ref, outq_ref, outp_ref,
    a_send, a_recv, b_send, b_recv, a_ret, a_back, b_ret, b_back,
    q_stack, p_stack, gq_stack, g_q, g_p, sel_q, allow_buf, q_meta, p_meta,
    q_all, p_all, score, part, part_in, gq_own, stat, stat_in,
    as_s, as_r, bs_s, bs_r, ar_s, ar_r, br_s, br_r, zq_s, zq_r, zs_s, zs_r, zg_s, zg_r,
):
    me = lax.axis_index("pb")
    z = lax.axis_index("pa")
    x, y, c = me // 8, (me // 2) % 4, me % 2

    def partner(i):
        dc, j = i // 16, i % 16
        g, dx = j // 4, j % 4
        dy = (dx + 4 - g) % 4
        return ((x + dx) % 4) * 8 + ((y + dy) % 4) * 2 + (c + dc) % 2

    barrier = pltpu.get_barrier_semaphore()

    def greet(i, carry):
        pl.semaphore_signal(barrier, inc=1, device_id=(partner(i), z), device_id_type=MESH)
        return carry

    lax.fori_loop(1, NB, greet, 0)
    for dz in range(1, NZ):
        pl.semaphore_signal(barrier, inc=1, device_id=(me, (z + dz) % NZ), device_id_type=MESH)

    ints = ints_ref[...]
    qc_row, pos_row, pc_row = ints[0:1, :], ints[1:2, :], ints[2:3, :]
    lane32, sub32 = iota((32, 256), 1), iota((32, 256), 0)
    qc_col = jnp.sum(jnp.where(lane32 == sub32, qc_row, 0), axis=1, keepdims=True)
    pos_col = jnp.sum(jnp.where(lane32 == sub32, pos_row, 0), axis=1, keepdims=True)
    qb_row, qb_col = shr(qc_row, 3), shr(qc_col, 3)
    q_before = jnp.where((qb_col == qb_row) & (sub32 < (lane32 & 31)), 1, 0)
    q_slot = qb_row * 2 + jnp.sum(q_before, axis=0, keepdims=True)
    lane128, sub128 = iota((128, 256), 1), iota((128, 256), 0)
    pc_col = jnp.sum(jnp.where(lane128 == sub128, pc_row, 0), axis=1, keepdims=True)
    pb_row, pb_col = shr(pc_row, 2), shr(pc_col, 2)
    p_before = jnp.where((pb_col == pb_row) & (sub128 < (lane128 & 127)), 1, 0)
    p_slot = pb_row * 2 + jnp.sum(p_before, axis=0, keepdims=True)

    big_r, big_c = iota((512, 256), 0), iota((512, 256), 1)
    g_q[...] = hot((q_slot == shr(big_r, 3)) & (shr(big_c, 5) == (big_r & 7)))
    g_p[...] = hot(
        (p_slot == shr(big_r, 4) * 8 + (big_r & 7)) & (shr(big_c, 7) == (shr(big_r, 3) & 1))
    )

    allow_buf[...] = jnp.zeros_like(allow_buf)
    allow_buf[:, 0:16] = allowed_ref[...].astype(F32).astype(BF16)
    reach = nn(hot(lane32 == qc_col), allow_buf[...])
    l32 = iota((32, 128), 1)
    q_num = jnp.where(l32 < 16, reach, 0.0)
    q_num = jnp.where(l32 == 16, (pos_col & 127).astype(F32) + 1.0, q_num)
    q_num = jnp.where(l32 == 17, shr(pos_col, 7).astype(F32), q_num).astype(BF16)
    l128, s128 = iota((128, 128), 1), iota((128, 128), 0)
    p_num = jnp.where((l128 < 16) & ((pc_col & 15) == l128), 1.0, 0.0)
    p_num = jnp.where(l128 == 16, s128.astype(F32) + 1.0, p_num).astype(BF16)
    mr_p, mr_q = iota((512, 128), 0), iota((512, 32), 0)
    gm_p = hot((p_slot[:, 0:128] == shr(mr_p, 4) * 8 + (mr_p & 15)) & ((mr_p & 15) < 8))
    gm_q = hot((q_slot[:, 0:32] == shr(mr_q, 4) * 2 + (mr_q & 15) - 8) & (shr(mr_q & 15, 1) == 4))
    a_send[:, QW:] = (nn(gm_p, p_num) + nn(gm_q, q_num)).astype(BF16)
    for e in range(8):
        q_stack[e * 32 : (e + 1) * 32, :] = q_ref[:, e * QW : (e + 1) * QW]
    a_send[:, 0:QW] = nn(g_q[...], q_stack[...]).astype(BF16)

    pl.semaphore_wait(barrier, NB - 1 + NZ - 1)

    def plane_copy(src, dst, send, recv, i, outgoing):
        d = partner(i)
        return pltpu.make_async_remote_copy(
            src_ref=src.at[rows16(d), :],
            dst_ref=dst.at[rows16(me if outgoing else d), :],
            send_sem=send.at[i],
            recv_sem=recv.at[me if outgoing else d],
            device_id=(d, z),
            device_id_type=MESH,
        )

    def start_all(src, dst, send, recv):
        def body(i, carry):
            plane_copy(src, dst, send, recv, i, True).start()
            return carry

        lax.fori_loop(1, NB, body, 0)

    def await_recv(src, dst, send, recv):
        def body(i, carry):
            plane_copy(src, dst, send, recv, i, False).wait_recv()
            return carry

        lax.fori_loop(1, NB, body, 0)

    def await_send(src, dst, send, recv):
        def body(i, carry):
            plane_copy(src, dst, send, recv, i, True).wait_send()
            return carry

        lax.fori_loop(1, NB, body, 0)

    def z_copy(src, dst, send, recv, dz):
        return pltpu.make_async_remote_copy(
            src_ref=src,
            dst_ref=dst,
            send_sem=send.at[dz - 1],
            recv_sem=recv.at[dz - 1],
            device_id=(me, (z + dz) % NZ),
            device_id_type=MESH,
        )

    mine = rows16(me)
    start_all(a_send, a_recv, as_s, as_r)
    a_recv[mine, :] = a_send[mine, :]

    p_stack[0:128, :] = p_ref[:, 0:PW]
    p_stack[128:256, :] = p_ref[:, PW:]

    def pack_p(j, carry):
        b_send[:, cols(j)] = nn(g_p[...], p_stack[:, cols(j)]).astype(BF16)
        return carry

    lax.fori_loop(0, PW // CT, pack_p, 0)
    start_all(b_send, b_recv, bs_s, bs_r)
    b_recv[mine, :] = b_send[mine, :]

    sr, sc = iota((512, 512), 0), iota((512, 512), 1)
    sel_q[...] = hot((shr(sr, 6) == (sc & 7)) & ((sr & 63) == shr(sc, 3)))
    hr, hc = iota((256, 512), 0), iota((256, 512), 1)
    half = (shr(hr, 3) == shr(hc, 4)) & ((hr & 7) == (hc & 7))
    sel_p0 = hot(half & ((hc & 8) == 0))
    sel_p1 = hot(half & ((hc & 8) == 8))
    nr, nc = iota((64, 512), 0), iota((64, 512), 1)
    sel_n = hot((shr(nr, 1) == shr(nc, 4)) & ((nc & 15) == 8 + (nr & 1)))

    await_recv(a_send, a_recv, as_s, as_r)
    zrows = pl.ds(pl.multiple_of(z * 64, 64), 64)
    whole = nn(sel_q[...], a_recv[:, 0:QW]).astype(BF16)
    for e in range(8):
        q_all[zrows, e * QW : (e + 1) * QW] = whole[e * 64 : (e + 1) * 64, :]
    q_all[zrows, D:] = nn(sel_n, a_recv[:, QW:]).astype(BF16)
    q_block = q_all.at[zrows, :]
    q_out = {dz: z_copy(q_block, q_block, zq_s, zq_r, dz) for dz in (1, 3, 2)}
    for dz in (1, 3, 2):
        q_out[dz].start()
    p_meta[...] = nn(sel_p0, a_recv[:, QW:]).astype(BF16)

    await_recv(b_send, b_recv, bs_s, bs_r)

    def unpack_p(j, carry):
        got = b_recv[:, cols(j)]
        p_all[:, cols(j)] = nn(sel_p0, got).astype(BF16)
        p_all[:, pl.ds(pl.multiple_of(PW + j * CT, CT), CT)] = nn(sel_p1, got).astype(BF16)
        return carry

    lax.fori_loop(0, PW // CT, unpack_p, 0)

    def z_from(dz):
        return (z + NZ - dz) % NZ

    for dz in (1, 3, 2):
        block = q_all.at[pl.ds(pl.multiple_of(z_from(dz) * 64, 64), 64), :]
        z_copy(block, block, zq_s, zq_r, dz).wait_recv()

    score[...] = jnp.zeros_like(score)

    def score_step(j, carry):
        score[...] += nt(p_all[:, cols(j)], q_all[:, cols(j)])
        return carry

    lax.fori_loop(0, D // CT, score_step, 0)
    qm, pm = q_all[:, D:], p_meta[...]
    l256 = iota((256, 128), 1)
    permitted = nt(jnp.where(l256 < 16, pm.astype(F32), 0.0).astype(BF16), qm) > 0.5
    er, el = iota((8, 128), 0), iota((8, 128), 1)
    q_dig = nt(hot((er < 2) & (el == 16 + er)), qm)
    q_lo, q_hi = q_dig[0:1, :], q_dig[1:2, :]
    q_code = jnp.where(q_lo > 0.5, q_hi * 256.0 + q_lo, -2.0)
    p_lo = pm[:, 16:17].astype(F32)
    p_dev = (shr(iota((256, 1), 0), 3) * NZ + z).astype(F32)
    p_code = jnp.where(p_lo > 0.5, p_dev * 256.0 + p_lo, -1.0)
    target = jnp.where(p_code == q_code, 1.0, 0.0)

    s = score[...] * SCALE
    top = jnp.max(jnp.where(permitted, s, FILL), axis=0, keepdims=True)
    total = jnp.sum(jnp.where(permitted, jnp.exp(s - top), 0.0), axis=0, keepdims=True)
    stat[0:1, :] = top
    stat[1:2, :] = total
    stat[2:8, :] = jnp.zeros((6, 256), F32)
    st_out = {dz: z_copy(stat, stat_in.at[dz - 1], zs_s, zs_r, dz) for dz in (1, 3, 2)}
    for dz in (1, 3, 2):
        st_out[dz].start()
    for dz in (1, 3, 2):
        st_out[dz].wait_recv()
    tops = [top] + [stat_in[i, 0:1, :] for i in range(3)]
    sums = [total] + [stat_in[i, 1:2, :] for i in range(3)]
    row_top = jnp.maximum(jnp.maximum(tops[0], tops[1]), jnp.maximum(tops[2], tops[3]))
    row_total = sum(l * jnp.exp(m - row_top) for m, l in zip(tops, sums))
    prob = jnp.where(permitted, jnp.exp(s - row_top), 0.0)
    prob = prob / jnp.where(row_total > 0.0, row_total, 1.0)
    gs = ((prob - target) * SCALE).astype(BF16)

    gs_t = jnp.transpose(gs.astype(F32)).astype(BF16)

    def part_step(j, carry):
        part[:, cols(j)] = nn(gs_t, p_all[:, cols(j)]).astype(BF16)
        return carry

    lax.fori_loop(0, D // CT, part_step, 0)
    pt_out = {}
    for dz in (1, 3, 2):
        rows = pl.ds(pl.multiple_of(((z + dz) % NZ) * 64, 64), 64)
        pt_out[dz] = z_copy(part.at[rows, :], part_in.at[dz - 1], zg_s, zg_r, dz)
        pt_out[dz].start()

    dr, dc_ = iota((512, 256), 0), iota((512, 256), 1)
    same = (shr(dr, 4) == shr(dc_, 3)) & ((dr & 7) == (dc_ & 7))
    gs0 = nn(hot(same & ((dr & 8) == 0)), gs).astype(BF16)
    gs1 = nn(hot(same & ((dr & 8) == 8)), gs).astype(BF16)

    def ret_step(j, carry):
        right = pl.ds(pl.multiple_of(PW + j * CT, CT), CT)
        b_ret[:, cols(j)] = (nn(gs0, q_all[:, cols(j)]) + nn(gs1, q_all[:, right])).astype(BF16)
        return carry

    lax.fori_loop(0, PW // CT, ret_step, 0)
    start_all(b_ret, b_back, br_s, br_r)
    b_back[mine, :] = b_ret[mine, :]

    for dz in (1, 3, 2):
        pt_out[dz].wait_recv()
    for e in range(8):
        ec = slice(e * QW, (e + 1) * QW)
        acc = part[zrows, ec].astype(F32)
        for i in range(3):
            acc = acc + part_in[i, :, ec].astype(F32)
        gq_stack[e * 64 : (e + 1) * 64, :] = acc.astype(BF16)
    a_ret[...] = tn(sel_q[...], gq_stack[...]).astype(BF16)
    start_all(a_ret, a_back, ar_s, ar_r)
    a_back[mine, :] = a_ret[mine, :]

    await_recv(b_ret, b_back, br_s, br_r)

    def out_p(j, carry):
        got = tn(g_p[...], b_back[:, cols(j)]).astype(BF16)
        outp_ref[:, cols(j)] = got[0:128, :]
        outp_ref[:, pl.ds(pl.multiple_of(PW + j * CT, CT), CT)] = got[128:256, :]
        return carry

    lax.fori_loop(0, PW // CT, out_p, 0)

    await_recv(a_ret, a_back, ar_s, ar_r)
    back = tn(g_q[...], a_back[...]).astype(BF16)
    for e in range(8):
        outq_ref[:, e * QW : (e + 1) * QW] = back[e * 32 : (e + 1) * 32, :]

    await_send(a_send, a_recv, as_s, as_r)
    await_send(b_send, b_recv, bs_s, bs_r)
    await_send(b_ret, b_back, br_s, br_r)
    await_send(a_ret, a_back, ar_s, ar_r)
    for dz in (1, 3, 2):
        q_out[dz].wait_send()
        st_out[dz].wait_send()
        pt_out[dz].wait_send()


def per_device(queries, passages, query_cluster, passage_cluster, allowed, positive):
    ints = jnp.concatenate(
        [
            jnp.tile(query_cluster, 8)[None],
            jnp.tile(positive, 8)[None],
            jnp.tile(passage_cluster, 2)[None],
            jnp.zeros((5, 256), I32),
        ],
        axis=0,
    )
    vm = pltpu.VMEM
    dma = pltpu.SemaphoreType.DMA
    return pl.pallas_call(
        kernel,
        out_shape=(
            jax.ShapeDtypeStruct(queries.shape, BF16),
            jax.ShapeDtypeStruct(passages.shape, BF16),
        ),
        in_specs=[pl.BlockSpec(memory_space=vm)] * 4,
        out_specs=(pl.BlockSpec(memory_space=vm),) * 2,
        scratch_shapes=[
            vm((512, QW + 128), BF16), vm((512, QW + 128), BF16),
            vm((512, PW), BF16), vm((512, PW), BF16),
            vm((512, QW), BF16), vm((512, QW), BF16),
            vm((512, PW), BF16), vm((512, PW), BF16),
            vm((256, QW), BF16), vm((256, PW), BF16), vm((512, QW), BF16),
            vm((512, 256), BF16), vm((512, 256), BF16), vm((512, 512), BF16),
            vm((256, 128), BF16), vm((64, 128), BF16), vm((256, 128), BF16),
            vm((256, D + 128), BF16), vm((256, D), BF16), vm((256, 256), F32),
            vm((256, D), BF16), vm((3, 64, D), BF16), vm((64, D), F32),
            vm((8, 256), F32), vm((3, 8, 256), F32),
        ]
        + [dma((NB,))] * 8
        + [dma((3,))] * 6,
        compiler_params=pltpu.CompilerParams(
            collective_id=0, has_side_effects=True, vmem_limit_bytes=56 * 1024 * 1024
        ),
        name="contrastive",
    )(queries, passages, ints, allowed)


def solution(mesh):
    rows = P(("pb", "pa"), None)
    flat = P(("pb", "pa"))
    return jax.shard_map(
        per_device,
        mesh=mesh,
        in_specs=(rows, rows, flat, flat, P(), flat),
        out_specs=(rows, rows),
        check_vma=False,
    )
```

```python
import functools

import jax
import jax.numpy as jnp
from jax import lax
from jax.experimental import pallas as pl
from jax.experimental.pallas import tpu as pltpu
from jax.sharding import PartitionSpec as P

MESH = pl.DeviceIdType.MESH
F32, BF16, I32 = jnp.float32, jnp.bfloat16, jnp.int32
D = 4096
NB = 32
NZ = 4
QW = 512
PW = 2048
CT = 512
SCALE = 50.0
FILL = -1e30


def iota(shape, dim):
    return lax.broadcasted_iota(I32, shape, dim)


def shr(a, n):
    return lax.shift_right_logical(a, jnp.full(a.shape, n, I32))


def hot(cond):
    return jnp.where(cond, 1.0, 0.0).astype(BF16)


def nn(a, b):
    return lax.dot_general(a, b, (((1,), (0,)), ((), ())), preferred_element_type=F32)


def nt(a, b):
    return lax.dot_general(a, b, (((1,), (1,)), ((), ())), preferred_element_type=F32)


def tn(a, b):
    return lax.dot_general(a, b, (((0,), (0,)), ((), ())), preferred_element_type=F32)


def cols(j, width=CT):
    return pl.ds(pl.multiple_of(j * width, width), width)


def rows16(i):
    return pl.ds(pl.multiple_of(i * 16, 16), 16)


def kernel(
    q_hbm, p_hbm, qc_hbm, pos_hbm, pc_hbm, allowed_hbm,
    a_back, b_back, g_q, g_p,
    a_send, a_recv, b_send, b_recv, a_ret, b_ret,
    q_stack, p_stack, gq_stack, sel_q, allow_int, allow_buf, qc_buf, pos_buf, pc_buf, p_meta,
    q_all, p_all, score, part, relay_in, part_in, stat, stat_in,
    as_s, as_r, bs_s, bs_r, ar_s, ar_r, br_s, br_r, zq_s, zq_r, zs_s, zs_r, zg_s, zg_r, in_sem,
):
    me = lax.axis_index("pb")
    z = lax.axis_index("pa")
    x, y, c = me // 8, (me // 2) % 4, me % 2

    def partner(i):
        dc, j = i // 16, i % 16
        g, dx = j // 4, j % 4
        dy = (dx + 4 - g) % 4
        return ((x + dx) % 4) * 8 + ((y + dy) % 4) * 2 + (c + dc) % 2

    loads = [
        pltpu.make_async_copy(qc_hbm, qc_buf, in_sem.at[0]),
        pltpu.make_async_copy(pos_hbm, pos_buf, in_sem.at[1]),
        pltpu.make_async_copy(pc_hbm, pc_buf, in_sem.at[2]),
        pltpu.make_async_copy(allowed_hbm, allow_int, in_sem.at[3]),
    ]
    for e in range(8):
        loads.append(
            pltpu.make_async_copy(
                q_hbm.at[:, e * QW : (e + 1) * QW],
                q_stack.at[e * 32 : (e + 1) * 32, :],
                in_sem.at[4 + e],
            )
        )
    for h in range(2):
        loads.append(
            pltpu.make_async_copy(
                p_hbm.at[:, h * PW : (h + 1) * PW],
                p_stack.at[h * 128 : (h + 1) * 128, :],
                in_sem.at[12 + h],
            )
        )
    for load in loads:
        load.start()

    barrier = pltpu.get_barrier_semaphore()

    def greet(i, carry):
        pl.semaphore_signal(barrier, inc=1, device_id=(partner(i), z), device_id_type=MESH)
        return carry

    lax.fori_loop(1, NB, greet, 0)
    for dz in range(1, NZ):
        pl.semaphore_signal(barrier, inc=1, device_id=(me, (z + dz) % NZ), device_id_type=MESH)

    for load in loads[:4]:
        load.wait()
    qc_row, pos_row, pc_row = qc_buf[...], pos_buf[...], pc_buf[...]
    lane32, sub32 = iota((32, 32), 1), iota((32, 32), 0)
    qc_col = jnp.sum(jnp.where(lane32 == sub32, qc_row, 0), axis=1, keepdims=True)
    pos_col = jnp.sum(jnp.where(lane32 == sub32, pos_row, 0), axis=1, keepdims=True)
    qb_row, qb_col = shr(qc_row, 3), shr(qc_col, 3)
    q_before = jnp.where((qb_col == qb_row) & (sub32 < lane32), 1, 0)
    q_slot = qb_row * 2 + jnp.sum(q_before, axis=0, keepdims=True)
    lane128, sub128 = iota((128, 128), 1), iota((128, 128), 0)
    pc_col = jnp.sum(jnp.where(lane128 == sub128, pc_row, 0), axis=1, keepdims=True)
    pb_row, pb_col = shr(pc_row, 2), shr(pc_col, 2)
    p_before = jnp.where((pb_col == pb_row) & (sub128 < lane128), 1, 0)
    p_slot = pb_row * 2 + jnp.sum(p_before, axis=0, keepdims=True)

    spread = hot(iota((32, 256), 0) == (iota((32, 256), 1) & 31))
    q_slot8 = nn(jnp.broadcast_to(q_slot, (8, 32)).astype(F32).astype(BF16), spread)[0:1, :]
    big_r, big_c = iota((512, 256), 0), iota((512, 256), 1)
    g_q[...] = hot(
        (q_slot8 == shr(big_r, 3).astype(F32)) & (shr(big_c, 5) == (big_r & 7))
    )
    half_r = iota((512, 128), 0)
    here = p_slot == shr(half_r, 4) * 8 + (half_r & 7)
    g_p[:, 0:128] = hot(here & ((half_r & 8) == 0))
    g_p[:, 128:256] = hot(here & ((half_r & 8) == 8))

    allow_buf[...] = jnp.zeros_like(allow_buf)
    allow_buf[0:16, :] = allow_int[...].astype(F32).astype(BF16)
    l256c = iota((32, 256), 1)
    reach = nt(hot(l256c == qc_col), allow_buf[...])
    l32 = iota((32, 128), 1)
    q_num = jnp.where(l32 < 16, reach, 0.0)
    q_num = jnp.where(l32 == 16, (pos_col & 127).astype(F32) + 1.0, q_num)
    q_num = jnp.where(l32 == 17, shr(pos_col, 7).astype(F32), q_num).astype(BF16)
    p_num = jnp.where((lane128 < 16) & ((pc_col & 15) == lane128), 1.0, 0.0)
    p_num = jnp.where(lane128 == 16, sub128.astype(F32) + 1.0, p_num).astype(BF16)
    mr_p, mr_q = iota((512, 128), 0), iota((512, 32), 0)
    gm_p = hot((p_slot == shr(mr_p, 4) * 8 + (mr_p & 15)) & ((mr_p & 15) < 8))
    gm_q = hot((q_slot == shr(mr_q, 4) * 2 + (mr_q & 15) - 8) & (shr(mr_q & 15, 1) == 4))
    a_send[:, QW:] = (nn(gm_p, p_num) + nn(gm_q, q_num)).astype(BF16)
    for load in loads[4:12]:
        load.wait()
    a_send[:, 0:QW] = nn(g_q[...], q_stack[...]).astype(BF16)

    pl.semaphore_wait(barrier, NB - 1 + NZ - 1)

    def plane_copy(src, dst, send, recv, i, outgoing):
        d = partner(i)
        return pltpu.make_async_remote_copy(
            src_ref=src.at[rows16(d), :],
            dst_ref=dst.at[rows16(me if outgoing else d), :],
            send_sem=send.at[i],
            recv_sem=recv.at[me if outgoing else d],
            device_id=(d, z),
            device_id_type=MESH,
        )

    def start_all(src, dst, send, recv):
        def body(i, carry):
            plane_copy(src, dst, send, recv, i, True).start()
            return carry

        lax.fori_loop(1, NB, body, 0)

    def await_recv(src, dst, send, recv):
        def body(i, carry):
            plane_copy(src, dst, send, recv, i, False).wait_recv()
            return carry

        lax.fori_loop(1, NB, body, 0)

    def await_send(src, dst, send, recv):
        def body(i, carry):
            plane_copy(src, dst, send, recv, i, True).wait_send()
            return carry

        lax.fori_loop(1, NB, body, 0)

    def z_copy(src, dst, send, recv, dz, k=None):
        k = dz - 1 if k is None else k
        return pltpu.make_async_remote_copy(
            src_ref=src,
            dst_ref=dst,
            send_sem=send.at[k],
            recv_sem=recv.at[k],
            device_id=(me, (z + dz) % NZ),
            device_id_type=MESH,
        )

    def block_rows(dz):
        return pl.ds(pl.multiple_of(((z + dz) % NZ) * 64, 64), 64)

    mine = rows16(me)
    start_all(a_send, a_recv, as_s, as_r)
    a_recv[mine, :] = a_send[mine, :]

    for load in loads[12:]:
        load.wait()

    def pack_p(j, carry):
        b_send[:, cols(j)] = nn(g_p[...], p_stack[:, cols(j)]).astype(BF16)
        return carry

    lax.fori_loop(0, PW // CT, pack_p, 0)
    start_all(b_send, b_recv, bs_s, bs_r)
    b_recv[mine, :] = b_send[mine, :]

    sr, sc = iota((512, 512), 0), iota((512, 512), 1)
    sel_q[...] = hot((shr(sr, 6) == (sc & 7)) & ((sr & 63) == shr(sc, 3)))
    hr, hc = iota((256, 512), 0), iota((256, 512), 1)
    half = (shr(hr, 3) == shr(hc, 4)) & ((hr & 7) == (hc & 7))
    sel_p0 = hot(half & ((hc & 8) == 0))
    sel_p1 = hot(half & ((hc & 8) == 8))
    nr, nc = iota((64, 512), 0), iota((64, 512), 1)
    sel_n = hot((shr(nr, 1) == shr(nc, 4)) & ((nc & 15) == 8 + (nr & 1)))

    await_recv(a_send, a_recv, as_s, as_r)
    zrows = pl.ds(pl.multiple_of(z * 64, 64), 64)
    whole = nn(sel_q[...], a_recv[:, 0:QW]).astype(BF16)
    for e in range(8):
        q_all[zrows, e * QW : (e + 1) * QW] = whole[e * 64 : (e + 1) * 64, :]
    q_all[zrows, D:] = nn(sel_n, a_recv[:, QW:]).astype(BF16)
    left, right = slice(0, PW), slice(PW, D + 128)

    def q_hop(dz_block, columns, dz, k):
        piece = q_all.at[block_rows(dz_block), columns]
        return z_copy(piece, piece, zq_s, zq_r, dz, k)

    q_out = [
        q_hop(0, left, 1, 0), q_hop(0, right, 3, 3), q_hop(0, right, 1, 1), q_hop(0, left, 3, 4),
        q_hop(3, left, 1, 2), q_hop(1, right, 3, 5),
    ]
    for copy in q_out[:4]:
        copy.start()
    p_meta[...] = nn(sel_p0, a_recv[:, QW:]).astype(BF16)
    q_hop(3, left, 1, 0).wait_recv()
    q_out[4].start()
    q_hop(1, right, 3, 3).wait_recv()
    q_out[5].start()

    await_recv(b_send, b_recv, bs_s, bs_r)

    def unpack_p(j, carry):
        got = b_recv[:, cols(j)]
        p_all[:, cols(j)] = nn(sel_p0, got).astype(BF16)
        p_all[:, pl.ds(pl.multiple_of(PW + j * CT, CT), CT)] = nn(sel_p1, got).astype(BF16)
        return carry

    lax.fori_loop(0, PW // CT, unpack_p, 0)

    q_hop(3, right, 1, 1).wait_recv()
    q_hop(1, left, 3, 4).wait_recv()
    q_hop(2, left, 1, 2).wait_recv()
    q_hop(2, right, 3, 5).wait_recv()

    score[...] = jnp.zeros_like(score)

    def score_step(j, carry):
        score[...] += nt(p_all[:, cols(j)], q_all[:, cols(j)])
        return carry

    lax.fori_loop(0, D // CT, score_step, 0)
    qm, pm = q_all[:, D:], p_meta[...]
    l256 = iota((256, 128), 1)
    permitted = nt(jnp.where(l256 < 16, pm.astype(F32), 0.0).astype(BF16), qm) > 0.5
    er, el = iota((8, 128), 0), iota((8, 128), 1)
    q_dig = nt(hot((er < 2) & (el == 16 + er)), qm)
    q_lo, q_hi = q_dig[0:1, :], q_dig[1:2, :]
    q_code = jnp.where(q_lo > 0.5, q_hi * 256.0 + q_lo, -2.0)
    p_lo = pm[:, 16:17].astype(F32)
    p_dev = (shr(iota((256, 1), 0), 3) * NZ + z).astype(F32)
    p_code = jnp.where(p_lo > 0.5, p_dev * 256.0 + p_lo, -1.0)
    target = jnp.where(p_code == q_code, 1.0, 0.0)

    s = score[...] * SCALE
    top = jnp.max(jnp.where(permitted, s, FILL), axis=0, keepdims=True)
    total = jnp.sum(jnp.where(permitted, jnp.exp(s - top), 0.0), axis=0, keepdims=True)
    stat[0:1, :] = top
    stat[1:2, :] = total
    stat[2:8, :] = jnp.zeros((6, 256), F32)
    st_out = {dz: z_copy(stat, stat_in.at[dz - 1], zs_s, zs_r, dz) for dz in (1, 3, 2)}
    for dz in (1, 3, 2):
        st_out[dz].start()
    for dz in (1, 3, 2):
        st_out[dz].wait_recv()
    tops = [top] + [stat_in[i, 0:1, :] for i in range(3)]
    sums = [total] + [stat_in[i, 1:2, :] for i in range(3)]
    row_top = jnp.maximum(jnp.maximum(tops[0], tops[1]), jnp.maximum(tops[2], tops[3]))
    row_total = sum(l * jnp.exp(m - row_top) for m, l in zip(tops, sums))
    prob = jnp.where(permitted, jnp.exp(s - row_top), 0.0)
    prob = prob / jnp.where(row_total > 0.0, row_total, 1.0)
    gs = ((prob - target) * SCALE).astype(BF16)

    dr, dc_ = iota((512, 256), 0), iota((512, 256), 1)
    same = (shr(dr, 4) == shr(dc_, 3)) & ((dr & 7) == (dc_ & 7))
    gs0 = nn(hot(same & ((dr & 8) == 0)), gs).astype(BF16)
    gs1 = nn(hot(same & ((dr & 8) == 8)), gs).astype(BF16)

    def ret_step(j, carry):
        right = pl.ds(pl.multiple_of(PW + j * CT, CT), CT)
        b_ret[:, cols(j)] = (nn(gs0, q_all[:, cols(j)]) + nn(gs1, q_all[:, right])).astype(BF16)
        return carry

    lax.fori_loop(0, PW // CT, ret_step, 0)
    start_all(b_ret, b_back, br_s, br_r)
    b_back[mine, :] = b_ret[mine, :]

    gs_t = jnp.transpose(gs.astype(F32)).astype(BF16)

    def part_step(j, carry):
        part[:, cols(j)] = nn(gs_t, p_all[:, cols(j)]).astype(BF16)
        return carry

    lax.fori_loop(0, D // CT, part_step, 0)
    low, high = slice(0, PW), slice(PW, D)

    def part_hop(dz_block, columns, dst, dz, k):
        return z_copy(part.at[block_rows(dz_block), columns], dst, zg_s, zg_r, dz, k)

    pt_out = [
        part_hop(2, low, relay_in.at[0], 1, 0),
        part_hop(2, high, relay_in.at[1], 3, 1),
        part_hop(1, high, part_in.at[0, :, high], 1, 2),
        part_hop(3, low, part_in.at[1, :, low], 3, 3),
        part_hop(1, low, part_in.at[0, :, low], 1, 4),
        part_hop(3, high, part_in.at[1, :, high], 3, 5),
    ]
    for copy in pt_out[:4]:
        copy.start()
    pt_out[0].wait_recv()
    up = part[block_rows(1), low].astype(F32) + relay_in[0].astype(F32)
    part[block_rows(1), low] = up.astype(BF16)
    pt_out[4].start()
    pt_out[1].wait_recv()
    down = part[block_rows(3), high].astype(F32) + relay_in[1].astype(F32)
    part[block_rows(3), high] = down.astype(BF16)
    pt_out[5].start()
    for copy in pt_out[2:]:
        copy.wait_recv()
    for e in range(8):
        ec = slice(e * QW, (e + 1) * QW)
        acc = part[zrows, ec].astype(F32)
        for i in range(2):
            acc = acc + part_in[i, :, ec].astype(F32)
        gq_stack[e * 64 : (e + 1) * 64, :] = acc.astype(BF16)
    a_ret[...] = tn(sel_q[...], gq_stack[...]).astype(BF16)
    start_all(a_ret, a_back, ar_s, ar_r)
    a_back[mine, :] = a_ret[mine, :]

    await_recv(b_ret, b_back, br_s, br_r)
    await_recv(a_ret, a_back, ar_s, ar_r)

    await_send(a_send, a_recv, as_s, as_r)
    await_send(b_send, b_recv, bs_s, bs_r)
    await_send(b_ret, b_back, br_s, br_r)
    await_send(a_ret, a_back, ar_s, ar_r)
    for copy in q_out + pt_out:
        copy.wait_send()
    for dz in (1, 3, 2):
        st_out[dz].wait_send()


def unpack(a_back, b_back, g_q, g_p, outq_hbm, outp_hbm, q_buf, p_buf, sem):
    copies = []
    for j in range(PW // CT):
        got = tn(g_p[...], b_back[:, j * CT : (j + 1) * CT]).astype(BF16)
        for h in range(2):
            columns = slice(h * PW + j * CT, h * PW + (j + 1) * CT)
            p_buf[:, columns] = got[h * 128 : (h + 1) * 128, :]
            copy = pltpu.make_async_copy(
                p_buf.at[:, columns], outp_hbm.at[:, columns], sem.at[2 * j + h]
            )
            copy.start()
            copies.append(copy)
    back = tn(g_q[...], a_back[...]).astype(BF16)
    for e in range(8):
        q_buf[:, e * QW : (e + 1) * QW] = back[e * 32 : (e + 1) * 32, :]
    copy = pltpu.make_async_copy(q_buf, outq_hbm, sem.at[8])
    copy.start()
    for c in copies + [copy]:
        c.wait()


def per_device(queries, passages, query_cluster, passage_cluster, allowed, positive):
    vm = pltpu.VMEM
    dma = pltpu.SemaphoreType.DMA
    hbm = pl.BlockSpec(memory_space=pl.ANY)
    res = pl.BlockSpec(memory_space=vm)
    landed = pl.pallas_call(
        kernel,
        out_shape=(
            pltpu.VMEM((512, QW), BF16),
            pltpu.VMEM((512, PW), BF16),
            pltpu.VMEM((512, 256), BF16),
            pltpu.VMEM((512, 256), BF16),
        ),
        in_specs=[pl.BlockSpec(memory_space=pltpu.HBM)] * 6,
        out_specs=(res,) * 4,
        scratch_shapes=[
            vm((512, QW + 128), BF16), vm((512, QW + 128), BF16),
            vm((512, PW), BF16), vm((512, PW), BF16),
            vm((512, QW), BF16), vm((512, PW), BF16),
            vm((256, QW), BF16), vm((256, PW), BF16), vm((512, QW), BF16),
            vm((512, 512), BF16),
            vm((16, 256), I32), vm((128, 256), BF16),
            vm((1, 32), I32), vm((1, 32), I32), vm((1, 128), I32),
            vm((256, 128), BF16),
            vm((256, D + 128), BF16), vm((256, D), BF16), vm((256, 256), F32),
            vm((256, D), BF16), vm((2, 64, PW), BF16), vm((2, 64, D), BF16),
            vm((8, 256), F32), vm((3, 8, 256), F32),
        ]
        + [dma((NB,))] * 8
        + [dma((6,))] * 2
        + [dma((3,))] * 2
        + [dma((6,))] * 2
        + [dma((14,))],
        compiler_params=pltpu.CompilerParams(
            collective_id=0, has_side_effects=True, vmem_limit_bytes=54 * 1024 * 1024
        ),
        name="contrastive",
    )(
        queries,
        passages,
        query_cluster.reshape(1, -1),
        positive.reshape(1, -1),
        passage_cluster.reshape(1, -1),
        allowed.T,
    )
    return pl.pallas_call(
        unpack,
        out_shape=(
            jax.ShapeDtypeStruct(queries.shape, BF16),
            jax.ShapeDtypeStruct(passages.shape, BF16),
        ),
        in_specs=[res] * 4,
        out_specs=(hbm, hbm),
        scratch_shapes=[vm((32, D), BF16), vm((128, D), BF16), dma((9,))],
        compiler_params=pltpu.CompilerParams(vmem_limit_bytes=16 * 1024 * 1024),
        name="unpack",
    )(*landed)


def solution(mesh):
    rows = P(("pb", "pa"), None)
    flat = P(("pb", "pa"))
    return jax.shard_map(
        per_device,
        mesh=mesh,
        in_specs=(rows, rows, flat, flat, P(), flat),
        out_specs=(rows, rows),
        check_vma=False,
    )
```

```python
import functools

import jax
import jax.numpy as jnp
from jax import lax
from jax.experimental import pallas as pl
from jax.experimental.pallas import tpu as pltpu
from jax.sharding import PartitionSpec as P

MESH = pl.DeviceIdType.MESH
F32, BF16, I32 = jnp.float32, jnp.bfloat16, jnp.int32
D = 4096
NB = 32
NZ = 4
QW = 512
PW = 2048
CT = 512
SCALE = 50.0
FILL = -1e30


def iota(shape, dim):
    return lax.broadcasted_iota(I32, shape, dim)


def shr(a, n):
    return lax.shift_right_logical(a, jnp.full(a.shape, n, I32))


def hot(cond):
    return jnp.where(cond, 1.0, 0.0).astype(BF16)


def nn(a, b):
    return lax.dot_general(a, b, (((1,), (0,)), ((), ())), preferred_element_type=F32)


def nt(a, b):
    return lax.dot_general(a, b, (((1,), (1,)), ((), ())), preferred_element_type=F32)


def tn(a, b):
    return lax.dot_general(a, b, (((0,), (0,)), ((), ())), preferred_element_type=F32)


def cols(j, width=CT):
    return pl.ds(pl.multiple_of(j * width, width), width)


def rows16(i):
    return pl.ds(pl.multiple_of(i * 16, 16), 16)


def kernel(
    q_hbm, p_hbm, qc_hbm, pos_hbm, pc_hbm, allowed_hbm,
    a_back, b_back, g_q, g_p,
    a_send, a_recv, b_send, b_recv, a_ret, b_ret,
    q_stack, p_stack, gq_stack, sel_q, allow_int, allow_buf, qc_buf, pos_buf, pc_buf, p_meta,
    q_all, p_all, score, live, target, gs, part, relay_in, part_in, stat, stat_in,
    as_s, as_r, bs_s, bs_r, ar_s, ar_r, br_s, br_r, zq_s, zq_r, zs_s, zs_r, zg_s, zg_r, in_sem,
):
    me = lax.axis_index("pb")
    z = lax.axis_index("pa")
    x, y, c = me // 8, (me // 2) % 4, me % 2

    def offset(i):
        j = i % 16
        dx = j % 4
        return dx, (dx + 4 - j // 4) % 4, i // 16

    def partner(i):
        dx, dy, dc = offset(i)
        return ((x + dx) % 4) * 8 + ((y + dy) % 4) * 2 + (c + dc) % 2

    def origin(i):
        dx, dy, dc = offset(i)
        return ((x + 4 - dx) % 4) * 8 + ((y + 4 - dy) % 4) * 2 + (c + dc) % 2

    loads = [
        pltpu.make_async_copy(qc_hbm, qc_buf, in_sem.at[0]),
        pltpu.make_async_copy(pos_hbm, pos_buf, in_sem.at[1]),
        pltpu.make_async_copy(pc_hbm, pc_buf, in_sem.at[2]),
        pltpu.make_async_copy(allowed_hbm, allow_int, in_sem.at[3]),
    ]
    for e in range(8):
        loads.append(
            pltpu.make_async_copy(
                q_hbm.at[:, e * QW : (e + 1) * QW],
                q_stack.at[e * 32 : (e + 1) * 32, :],
                in_sem.at[4 + e],
            )
        )
    for h in range(2):
        loads.append(
            pltpu.make_async_copy(
                p_hbm.at[:, h * PW : (h + 1) * PW],
                p_stack.at[h * 128 : (h + 1) * 128, :],
                in_sem.at[12 + h],
            )
        )
    for load in loads:
        load.start()

    barrier = pltpu.get_barrier_semaphore()

    def greet(i, carry):
        pl.semaphore_signal(barrier, inc=1, device_id=(partner(i), z), device_id_type=MESH)
        return carry

    lax.fori_loop(1, NB, greet, 0)
    for dz in range(1, NZ):
        pl.semaphore_signal(barrier, inc=1, device_id=(me, (z + dz) % NZ), device_id_type=MESH)

    for load in loads[:4]:
        load.wait()
    qc_row, pos_row, pc_row = qc_buf[...], pos_buf[...], pc_buf[...]
    lane32, sub32 = iota((32, 32), 1), iota((32, 32), 0)
    qc_col = jnp.sum(jnp.where(lane32 == sub32, qc_row, 0), axis=1, keepdims=True)
    pos_col = jnp.sum(jnp.where(lane32 == sub32, pos_row, 0), axis=1, keepdims=True)
    qb_row, qb_col = shr(qc_row, 3), shr(qc_col, 3)
    q_before = jnp.where((qb_col == qb_row) & (sub32 < lane32), 1, 0)
    q_slot = qb_row * 2 + jnp.sum(q_before, axis=0, keepdims=True)
    lane128, sub128 = iota((128, 128), 1), iota((128, 128), 0)
    pc_col = jnp.sum(jnp.where(lane128 == sub128, pc_row, 0), axis=1, keepdims=True)
    pb_row, pb_col = shr(pc_row, 2), shr(pc_col, 2)
    p_before = jnp.where((pb_col == pb_row) & (sub128 < lane128), 1, 0)
    p_slot = pb_row * 2 + jnp.sum(p_before, axis=0, keepdims=True)

    spread = hot(iota((32, 256), 0) == (iota((32, 256), 1) & 31))
    q_slot8 = nn(jnp.broadcast_to(q_slot, (8, 32)).astype(F32).astype(BF16), spread)[0:1, :]
    big_r, big_c = iota((512, 256), 0), iota((512, 256), 1)
    g_q[...] = hot(
        (q_slot8 == shr(big_r, 3).astype(F32)) & (shr(big_c, 5) == (big_r & 7))
    )
    half_r = iota((512, 128), 0)
    here = p_slot == shr(half_r, 4) * 8 + (half_r & 7)
    g_p[:, 0:128] = hot(here & ((half_r & 8) == 0))
    g_p[:, 128:256] = hot(here & ((half_r & 8) == 8))

    allow_buf[...] = jnp.zeros_like(allow_buf)
    allow_buf[0:16, :] = allow_int[...].astype(F32).astype(BF16)
    l256c = iota((32, 256), 1)
    reach = nt(hot(l256c == qc_col), allow_buf[...])
    l32 = iota((32, 128), 1)
    q_num = jnp.where(l32 < 16, reach, 0.0)
    q_num = jnp.where(l32 == 16, (pos_col & 127).astype(F32) + 1.0, q_num)
    q_num = jnp.where(l32 == 17, shr(pos_col, 7).astype(F32), q_num).astype(BF16)
    p_num = jnp.where((lane128 < 16) & ((pc_col & 15) == lane128), 1.0, 0.0)
    p_num = jnp.where(lane128 == 16, sub128.astype(F32) + 1.0, p_num).astype(BF16)
    mr_p, mr_q = iota((512, 128), 0), iota((512, 32), 0)
    gm_p = hot((p_slot == shr(mr_p, 4) * 8 + (mr_p & 15)) & ((mr_p & 15) < 8))
    gm_q = hot((q_slot == shr(mr_q, 4) * 2 + (mr_q & 15) - 8) & (shr(mr_q & 15, 1) == 4))
    a_send[:, QW:] = (nn(gm_p, p_num) + nn(gm_q, q_num)).astype(BF16)
    for load in loads[4:12]:
        load.wait()
    a_send[:, 0:QW] = nn(g_q[...], q_stack[...]).astype(BF16)

    pl.semaphore_wait(barrier, NB - 1 + NZ - 1)

    def out_copy(src, dst, send, recv, i):
        d = partner(i)
        return pltpu.make_async_remote_copy(
            src_ref=src.at[rows16(d), :],
            dst_ref=dst.at[rows16(i), :],
            send_sem=send.at[i],
            recv_sem=recv.at[i],
            device_id=(d, z),
            device_id_type=MESH,
        )

    def back_copy(src, dst, send, recv, i, place):
        return pltpu.make_async_remote_copy(
            src_ref=src.at[rows16(i), :],
            dst_ref=dst.at[rows16(place), :],
            send_sem=send.at[i],
            recv_sem=recv.at[i],
            device_id=(origin(i), z),
            device_id_type=MESH,
        )

    def steps(lo, hi, act):
        def body(i, carry):
            act(i)
            return carry

        lax.fori_loop(lo, hi, body, 0)

    a_out = functools.partial(out_copy, a_send, a_recv, as_s, as_r)
    b_out = functools.partial(out_copy, b_send, b_recv, bs_s, bs_r)
    a_home = functools.partial(back_copy, a_ret, a_back, ar_s, ar_r)
    b_home = functools.partial(back_copy, b_ret, b_back, br_s, br_r)

    def z_copy(src, dst, send, recv, dz, k=None):
        k = dz - 1 if k is None else k
        return pltpu.make_async_remote_copy(
            src_ref=src,
            dst_ref=dst,
            send_sem=send.at[k],
            recv_sem=recv.at[k],
            device_id=(me, (z + dz) % NZ),
            device_id_type=MESH,
        )

    def block_rows(dz):
        return pl.ds(pl.multiple_of(((z + dz) % NZ) * 64, 64), 64)

    mine = rows16(me)
    steps(1, NB, lambda i: a_out(i).start())
    a_recv[0:16, :] = a_send[mine, :]

    for load in loads[12:]:
        load.wait()

    def pack_p(j, carry):
        b_send[:, cols(j)] = nn(g_p[...], p_stack[:, cols(j)]).astype(BF16)
        return carry

    lax.fori_loop(0, PW // CT, pack_p, 0)
    steps(1, NB, lambda i: b_out(i).start())
    b_recv[0:16, :] = b_send[mine, :]

    sr, sc = iota((512, 512), 0), iota((512, 512), 1)
    sel_q[...] = hot((shr(sr, 6) == (sc & 7)) & ((sr & 63) == shr(sc, 3)))
    hr, hc = iota((256, 512), 0), iota((256, 512), 1)
    half = (shr(hr, 3) == shr(hc, 4)) & ((hr & 7) == (hc & 7))
    sel_m = hot(half & ((hc & 8) == 0))
    nr, nc = iota((64, 512), 0), iota((64, 512), 1)
    sel_n = hot((shr(nr, 1) == shr(nc, 4)) & ((nc & 15) == 8 + (nr & 1)))

    steps(1, NB, lambda i: a_out(i).wait_recv())
    zrows = pl.ds(pl.multiple_of(z * 64, 64), 64)
    whole = nn(sel_q[...], a_recv[:, 0:QW]).astype(BF16)
    for e in range(8):
        q_all[zrows, e * QW : (e + 1) * QW] = whole[e * 64 : (e + 1) * 64, :]
    q_all[zrows, D:] = nn(sel_n, a_recv[:, QW:]).astype(BF16)
    left, right = slice(0, PW), slice(PW, D + 128)

    def q_hop(dz_block, columns, dz, k):
        piece = q_all.at[block_rows(dz_block), columns]
        return z_copy(piece, piece, zq_s, zq_r, dz, k)

    q_out = [
        q_hop(0, left, 1, 0), q_hop(0, right, 3, 3), q_hop(0, right, 1, 1), q_hop(0, left, 3, 4),
        q_hop(3, left, 1, 2), q_hop(1, right, 3, 5),
    ]
    for copy in q_out[:4]:
        copy.start()
    p_meta[...] = nn(sel_m, a_recv[:, QW:]).astype(BF16)
    q_hop(3, left, 1, 0).wait_recv()
    q_out[4].start()
    q_hop(1, right, 3, 3).wait_recv()
    q_out[5].start()

    ur, uc = iota((64, 128), 0), iota((64, 128), 1)
    pair = (shr(ur, 3) == shr(uc, 4)) & ((ur & 7) == (uc & 7))
    sel_u = [hot(pair & ((uc & 8) == 8 * h)) for h in range(2)]

    def arrive(g, lo):
        steps(lo, 8 * (g + 1), lambda i: b_out(i).wait_recv())
        for j in range(PW // CT):
            got = b_recv[g * 128 : (g + 1) * 128, j * CT : (j + 1) * CT]
            for h in range(2):
                columns = slice(h * PW + j * CT, h * PW + (j + 1) * CT)
                p_all[g * 64 : (g + 1) * 64, columns] = nn(sel_u[h], got).astype(BF16)

    def score_rows(lo, hi):
        acc = nt(p_all[lo:hi, 0:CT], q_all[:, 0:CT])
        for j in range(1, D // CT):
            acc = acc + nt(p_all[lo:hi, j * CT : (j + 1) * CT], q_all[:, j * CT : (j + 1) * CT])
        score[lo:hi, :] = acc * SCALE

    for g in range(3):
        arrive(g, max(1, 8 * g))

    q_hop(3, right, 1, 1).wait_recv()
    q_hop(1, left, 3, 4).wait_recv()
    q_hop(2, left, 1, 2).wait_recv()
    q_hop(2, right, 3, 5).wait_recv()

    qm, pm = q_all[:, D:], p_meta[...]
    l256 = iota((256, 128), 1)
    reached = nt(jnp.where(l256 < 16, pm.astype(F32), 0.0).astype(BF16), qm)
    live[...] = jnp.where(reached > 0.5, 1.0, 0.0)
    er, el = iota((8, 128), 0), iota((8, 128), 1)
    q_dig = nt(hot((er < 2) & (el == 16 + er)), qm)
    q_lo, q_hi = q_dig[0:1, :], q_dig[1:2, :]
    q_code = jnp.where(q_lo > 0.5, q_hi * 256.0 + q_lo, -2.0)
    p_lo = pm[:, 16:17].astype(F32)
    slot = shr(iota((256, 1), 0), 3)
    dx, dc = slot & 3, shr(slot, 4)
    dy = (dx - shr(slot & 15, 2)) & 3
    p_dev = (((x - dx) & 3) * 8 + ((y - dy) & 3) * 2 + ((c + dc) & 1)) * NZ + z
    p_code = jnp.where(p_lo > 0.5, p_dev.astype(F32) * 256.0 + p_lo, -1.0)
    target[...] = jnp.where(p_code == q_code, 1.0, 0.0)

    score_rows(0, 192)
    arrive(3, 24)
    score_rows(192, 256)

    s = score[...]
    permitted = live[...] > 0.5
    top = jnp.max(jnp.where(permitted, s, FILL), axis=0, keepdims=True)
    total = jnp.sum(jnp.where(permitted, jnp.exp(s - top), 0.0), axis=0, keepdims=True)
    stat[0:1, :] = top
    stat[1:2, :] = total
    stat[2:8, :] = jnp.zeros((6, 256), F32)
    st_out = {dz: z_copy(stat, stat_in.at[dz - 1], zs_s, zs_r, dz) for dz in (1, 3, 2)}
    for dz in (2, 1, 3):
        st_out[dz].start()
    for dz in (1, 3, 2):
        st_out[dz].wait_recv()
    tops = [top] + [stat_in[i, 0:1, :] for i in range(3)]
    sums = [total] + [stat_in[i, 1:2, :] for i in range(3)]
    row_top = jnp.maximum(jnp.maximum(tops[0], tops[1]), jnp.maximum(tops[2], tops[3]))
    row_total = sum(l * jnp.exp(m - row_top) for m, l in zip(tops, sums))
    prob = jnp.where(permitted, jnp.exp(s - row_top), 0.0)
    prob = prob / jnp.where(row_total > 0.0, row_total, 1.0)
    gs_f = (prob - target[...]) * SCALE
    gs[...] = gs_f.astype(BF16)

    dr, dq = iota((128, 64), 0), iota((128, 64), 1)
    same = (shr(dr, 4) == shr(dq, 3)) & ((dr & 7) == (dq & 7))
    dup = [hot(same & ((dr & 8) == 8 * h)) for h in range(2)]

    def send_home(g):
        part_gs = gs[g * 64 : (g + 1) * 64, :]
        halves = [nn(dup[h], part_gs).astype(BF16) for h in range(2)]
        for j in range(PW // CT):
            acc = nn(halves[0], q_all[:, j * CT : (j + 1) * CT])
            acc = acc + nn(halves[1], q_all[:, PW + j * CT : PW + (j + 1) * CT])
            b_ret[g * 128 : (g + 1) * 128, j * CT : (j + 1) * CT] = acc.astype(BF16)
        steps(max(1, 8 * g), 8 * (g + 1), lambda i: b_home(i, me).start())

    send_home(0)

    gs_t = jnp.transpose(gs_f).astype(BF16)

    def part_step(j, carry):
        part[:, cols(j)] = nn(gs_t, p_all[:, cols(j)]).astype(BF16)
        return carry

    lax.fori_loop(0, D // CT, part_step, 0)
    low, high = slice(0, PW), slice(PW, D)

    def part_hop(dz_block, columns, dst, dz, k):
        return z_copy(part.at[block_rows(dz_block), columns], dst, zg_s, zg_r, dz, k)

    pt_out = [
        part_hop(2, low, relay_in.at[0], 1, 0),
        part_hop(2, high, relay_in.at[1], 3, 1),
        part_hop(1, high, part_in.at[0, :, high], 1, 2),
        part_hop(3, low, part_in.at[1, :, low], 3, 3),
        part_hop(1, low, part_in.at[0, :, low], 1, 4),
        part_hop(3, high, part_in.at[1, :, high], 3, 5),
    ]
    for copy in pt_out[:4]:
        copy.start()

    for g in range(1, 4):
        send_home(g)
    b_back[mine, :] = b_ret[0:16, :]

    pt_out[0].wait_recv()
    up = part[block_rows(1), low].astype(F32) + relay_in[0].astype(F32)
    part[block_rows(1), low] = up.astype(BF16)
    pt_out[4].start()
    pt_out[1].wait_recv()
    down = part[block_rows(3), high].astype(F32) + relay_in[1].astype(F32)
    part[block_rows(3), high] = down.astype(BF16)
    pt_out[5].start()
    for copy in pt_out[2:]:
        copy.wait_recv()
    for e in range(8):
        ec = slice(e * QW, (e + 1) * QW)
        acc = part[zrows, ec].astype(F32)
        for i in range(2):
            acc = acc + part_in[i, :, ec].astype(F32)
        gq_stack[e * 64 : (e + 1) * 64, :] = acc.astype(BF16)
    a_ret[...] = tn(sel_q[...], gq_stack[...]).astype(BF16)
    steps(1, NB, lambda i: a_home(i, me).start())
    a_back[mine, :] = a_ret[0:16, :]
    steps(1, NB, lambda i: b_home(i, partner(i)).wait_recv())
    steps(1, NB, lambda i: a_home(i, partner(i)).wait_recv())

    steps(1, NB, lambda i: a_out(i).wait_send())
    steps(1, NB, lambda i: b_out(i).wait_send())
    steps(1, NB, lambda i: b_home(i, me).wait_send())
    steps(1, NB, lambda i: a_home(i, me).wait_send())
    for copy in q_out + pt_out:
        copy.wait_send()
    for dz in (1, 3, 2):
        st_out[dz].wait_send()


def unpack(a_back, b_back, g_q, g_p, outq_hbm, outp_hbm, q_buf, p_buf, sem):
    copies = []
    for j in range(PW // CT):
        got = tn(g_p[...], b_back[:, j * CT : (j + 1) * CT]).astype(BF16)
        for h in range(2):
            columns = slice(h * PW + j * CT, h * PW + (j + 1) * CT)
            p_buf[:, columns] = got[h * 128 : (h + 1) * 128, :]
            copy = pltpu.make_async_copy(
                p_buf.at[:, columns], outp_hbm.at[:, columns], sem.at[2 * j + h]
            )
            copy.start()
            copies.append(copy)
    back = tn(g_q[...], a_back[...]).astype(BF16)
    for e in range(8):
        q_buf[:, e * QW : (e + 1) * QW] = back[e * 32 : (e + 1) * 32, :]
    copy = pltpu.make_async_copy(q_buf, outq_hbm, sem.at[8])
    copy.start()
    for c in copies + [copy]:
        c.wait()


def per_device(queries, passages, query_cluster, passage_cluster, allowed, positive):
    vm = pltpu.VMEM
    dma = pltpu.SemaphoreType.DMA
    hbm = pl.BlockSpec(memory_space=pl.ANY)
    res = pl.BlockSpec(memory_space=vm)
    landed = pl.pallas_call(
        kernel,
        out_shape=(
            pltpu.VMEM((512, QW), BF16),
            pltpu.VMEM((512, PW), BF16),
            pltpu.VMEM((512, 256), BF16),
            pltpu.VMEM((512, 256), BF16),
        ),
        in_specs=[pl.BlockSpec(memory_space=pltpu.HBM)] * 6,
        out_specs=(res,) * 4,
        scratch_shapes=[
            vm((512, QW + 128), BF16), vm((512, QW + 128), BF16),
            vm((512, PW), BF16), vm((512, PW), BF16),
            vm((512, QW), BF16), vm((512, PW), BF16),
            vm((256, QW), BF16), vm((256, PW), BF16), vm((512, QW), BF16),
            vm((512, 512), BF16),
            vm((16, 256), I32), vm((128, 256), BF16),
            vm((1, 32), I32), vm((1, 32), I32), vm((1, 128), I32),
            vm((256, 128), BF16),
            vm((256, D + 128), BF16), vm((256, D), BF16),
            vm((256, 256), F32), vm((256, 256), F32), vm((256, 256), F32),
            vm((256, 256), BF16),
            vm((256, D), BF16), vm((2, 64, PW), BF16), vm((2, 64, D), BF16),
            vm((8, 256), F32), vm((3, 8, 256), F32),
        ]
        + [dma((NB,))] * 8
        + [dma((6,))] * 2
        + [dma((3,))] * 2
        + [dma((6,))] * 2
        + [dma((14,))],
        compiler_params=pltpu.CompilerParams(
            collective_id=0, has_side_effects=True, vmem_limit_bytes=54 * 1024 * 1024
        ),
        name="contrastive",
    )(
        queries,
        passages,
        query_cluster.reshape(1, -1),
        positive.reshape(1, -1),
        passage_cluster.reshape(1, -1),
        allowed.T,
    )
    return pl.pallas_call(
        unpack,
        out_shape=(
            jax.ShapeDtypeStruct(queries.shape, BF16),
            jax.ShapeDtypeStruct(passages.shape, BF16),
        ),
        in_specs=[res] * 4,
        out_specs=(hbm, hbm),
        scratch_shapes=[vm((32, D), BF16), vm((128, D), BF16), dma((9,))],
        compiler_params=pltpu.CompilerParams(vmem_limit_bytes=16 * 1024 * 1024),
        name="unpack",
    )(*landed)


def solution(mesh):
    rows = P(("pb", "pa"), None)
    flat = P(("pb", "pa"))
    return jax.shard_map(
        per_device,
        mesh=mesh,
        in_specs=(rows, rows, flat, flat, P(), flat),
        out_specs=(rows, rows),
        check_vma=False,
    )
```

```python
import functools

import jax
import jax.numpy as jnp
from jax import lax
from jax.experimental import pallas as pl
from jax.experimental.pallas import tpu as pltpu
from jax.sharding import PartitionSpec as P

MESH = pl.DeviceIdType.MESH
F32, BF16, I32 = jnp.float32, jnp.bfloat16, jnp.int32
D = 4096
NB = 32
NZ = 4
QW = 512
PW = 2048
CT = 512
SCALE = 50.0
FILL = -1e30


def iota(shape, dim):
    return lax.broadcasted_iota(I32, shape, dim)


def shr(a, n):
    return lax.shift_right_logical(a, jnp.full(a.shape, n, I32))


def hot(cond):
    return jnp.where(cond, 1.0, 0.0).astype(BF16)


def nn(a, b):
    return lax.dot_general(a, b, (((1,), (0,)), ((), ())), preferred_element_type=F32)


def nt(a, b):
    return lax.dot_general(a, b, (((1,), (1,)), ((), ())), preferred_element_type=F32)


def tn(a, b):
    return lax.dot_general(a, b, (((0,), (0,)), ((), ())), preferred_element_type=F32)


def cols(j, width=CT):
    return pl.ds(pl.multiple_of(j * width, width), width)


def rows16(i):
    return pl.ds(pl.multiple_of(i * 16, 16), 16)


def offset(i):
    j = i % 16
    dx = j % 4
    return dx, (dx + 4 - j // 4) % 4, i // 16


def hops(i):
    dx, dy, _ = offset(i)
    return min(dx, 4 - dx) + min(dy, 4 - dy)


FAR_FIRST = sorted(range(1, NB), key=hops, reverse=True)


def kernel(
    q_hbm, p_hbm, qc_hbm, pos_hbm, pc_hbm, allowed_hbm,
    a_back, b_back, g_q, g_p,
    a_send, a_recv, b_send, b_recv, a_ret, b_ret,
    q_stack, p_stack, gq_stack, sel_q, allow_int, allow_buf, qc_buf, pos_buf, pc_buf, p_meta,
    q_all, q_t, p_all, score, live, target, gs, part, relay_in, part_in, stat, stat_in,
    as_s, as_r, bs_s, bs_r, ar_s, ar_r, br_s, br_r, zq_s, zq_r, zs_s, zs_r, zg_s, zg_r, in_sem,
):
    me = lax.axis_index("pb")
    z = lax.axis_index("pa")
    x, y, c = me // 8, (me // 2) % 4, me % 2

    def partner(i):
        dx, dy, dc = offset(i)
        return ((x + dx) % 4) * 8 + ((y + dy) % 4) * 2 + (c + dc) % 2

    def origin(i):
        dx, dy, dc = offset(i)
        return ((x + 4 - dx) % 4) * 8 + ((y + 4 - dy) % 4) * 2 + (c + dc) % 2

    barrier = pltpu.get_barrier_semaphore()
    for i in FAR_FIRST:
        pl.semaphore_signal(barrier, inc=1, device_id=(partner(i), z), device_id_type=MESH)
    for dz in (2, 1, 3):
        pl.semaphore_signal(barrier, inc=1, device_id=(me, (z + dz) % NZ), device_id_type=MESH)

    loads = [
        pltpu.make_async_copy(qc_hbm, qc_buf, in_sem.at[0]),
        pltpu.make_async_copy(pos_hbm, pos_buf, in_sem.at[1]),
        pltpu.make_async_copy(pc_hbm, pc_buf, in_sem.at[2]),
        pltpu.make_async_copy(allowed_hbm, allow_int, in_sem.at[3]),
    ]
    for e in range(8):
        loads.append(
            pltpu.make_async_copy(
                q_hbm.at[:, e * QW : (e + 1) * QW],
                q_stack.at[e * 32 : (e + 1) * 32, :],
                in_sem.at[4 + e],
            )
        )
    for h in range(2):
        loads.append(
            pltpu.make_async_copy(
                p_hbm.at[:, h * PW : (h + 1) * PW],
                p_stack.at[h * 128 : (h + 1) * 128, :],
                in_sem.at[12 + h],
            )
        )
    for load in loads:
        load.start()

    for load in loads[:4]:
        load.wait()
    qc_row, pos_row, pc_row = qc_buf[...], pos_buf[...], pc_buf[...]
    lane32, sub32 = iota((32, 32), 1), iota((32, 32), 0)
    qc_col = jnp.sum(jnp.where(lane32 == sub32, qc_row, 0), axis=1, keepdims=True)
    pos_col = jnp.sum(jnp.where(lane32 == sub32, pos_row, 0), axis=1, keepdims=True)
    qb_row, qb_col = shr(qc_row, 3), shr(qc_col, 3)
    q_before = jnp.where((qb_col == qb_row) & (sub32 < lane32), 1, 0)
    q_slot = qb_row * 2 + jnp.sum(q_before, axis=0, keepdims=True)
    lane128, sub128 = iota((128, 128), 1), iota((128, 128), 0)
    pc_col = jnp.sum(jnp.where(lane128 == sub128, pc_row, 0), axis=1, keepdims=True)
    pb_row, pb_col = shr(pc_row, 2), shr(pc_col, 2)
    p_before = jnp.where((pb_col == pb_row) & (sub128 < lane128), 1, 0)
    p_slot = pb_row * 2 + jnp.sum(p_before, axis=0, keepdims=True)

    spread = hot(iota((32, 256), 0) == (iota((32, 256), 1) & 31))
    q_slot8 = nn(jnp.broadcast_to(q_slot, (8, 32)).astype(F32).astype(BF16), spread)[0:1, :]
    big_r, big_c = iota((512, 256), 0), iota((512, 256), 1)
    g_q[...] = hot(
        (q_slot8 == shr(big_r, 3).astype(F32)) & (shr(big_c, 5) == (big_r & 7))
    )
    half_r = iota((512, 128), 0)
    here = p_slot == shr(half_r, 4) * 8 + (half_r & 7)
    g_p[:, 0:128] = hot(here & ((half_r & 8) == 0))
    g_p[:, 128:256] = hot(here & ((half_r & 8) == 8))

    allow_buf[...] = jnp.zeros_like(allow_buf)
    allow_buf[0:16, :] = allow_int[...].astype(F32).astype(BF16)
    l256c = iota((32, 256), 1)
    reach = nt(hot(l256c == qc_col), allow_buf[...])
    l32 = iota((32, 128), 1)
    q_num = jnp.where(l32 < 16, reach, 0.0)
    q_num = jnp.where(l32 == 16, (pos_col & 127).astype(F32) + 1.0, q_num)
    q_num = jnp.where(l32 == 17, shr(pos_col, 7).astype(F32), q_num).astype(BF16)
    p_num = jnp.where((lane128 < 16) & ((pc_col & 15) == lane128), 1.0, 0.0)
    p_num = jnp.where(lane128 == 16, sub128.astype(F32) + 1.0, p_num).astype(BF16)
    mr_p, mr_q = iota((512, 128), 0), iota((512, 32), 0)
    gm_p = hot((p_slot == shr(mr_p, 4) * 8 + (mr_p & 15)) & ((mr_p & 15) < 8))
    gm_q = hot((q_slot == shr(mr_q, 4) * 2 + (mr_q & 15) - 8) & (shr(mr_q & 15, 1) == 4))
    a_send[:, QW:] = (nn(gm_p, p_num) + nn(gm_q, q_num)).astype(BF16)
    for load in loads[4:12]:
        load.wait()
    a_send[:, 0:QW] = nn(g_q[...], q_stack[...]).astype(BF16)

    pl.semaphore_wait(barrier, NB - 1 + NZ - 1)

    def out_copy(src, dst, send, recv, i):
        d = partner(i)
        return pltpu.make_async_remote_copy(
            src_ref=src.at[rows16(d), :],
            dst_ref=dst.at[rows16(i), :],
            send_sem=send.at[i],
            recv_sem=recv.at[i],
            device_id=(d, z),
            device_id_type=MESH,
        )

    def back_copy(src, dst, send, recv, i, place):
        return pltpu.make_async_remote_copy(
            src_ref=src.at[rows16(i), :],
            dst_ref=dst.at[rows16(place), :],
            send_sem=send.at[i],
            recv_sem=recv.at[i],
            device_id=(origin(i), z),
            device_id_type=MESH,
        )

    def steps(lo, hi, act):
        def body(i, carry):
            act(i)
            return carry

        lax.fori_loop(lo, hi, body, 0)

    a_out = functools.partial(out_copy, a_send, a_recv, as_s, as_r)
    b_out = functools.partial(out_copy, b_send, b_recv, bs_s, bs_r)
    a_home = functools.partial(back_copy, a_ret, a_back, ar_s, ar_r)
    b_home = functools.partial(back_copy, b_ret, b_back, br_s, br_r)

    def z_copy(src, dst, send, recv, dz, k=None):
        k = dz - 1 if k is None else k
        return pltpu.make_async_remote_copy(
            src_ref=src,
            dst_ref=dst,
            send_sem=send.at[k],
            recv_sem=recv.at[k],
            device_id=(me, (z + dz) % NZ),
            device_id_type=MESH,
        )

    def block_rows(dz):
        return pl.ds(pl.multiple_of(((z + dz) % NZ) * 64, 64), 64)

    mine = rows16(me)
    steps(1, NB, lambda i: a_out(i).start())
    a_recv[0:16, :] = a_send[mine, :]

    for load in loads[12:]:
        load.wait()

    def pack_p(j, carry):
        b_send[:, cols(j)] = nn(g_p[...], p_stack[:, cols(j)]).astype(BF16)
        return carry

    lax.fori_loop(0, PW // CT, pack_p, 0)
    steps(1, NB, lambda i: b_out(i).start())
    b_recv[0:16, :] = b_send[mine, :]

    sr, sc = iota((512, 512), 0), iota((512, 512), 1)
    sel_q[...] = hot((shr(sr, 6) == (sc & 7)) & ((sr & 63) == shr(sc, 3)))
    hr, hc = iota((256, 512), 0), iota((256, 512), 1)
    half = (shr(hr, 3) == shr(hc, 4)) & ((hr & 7) == (hc & 7))
    sel_m = hot(half & ((hc & 8) == 0))
    nr, nc = iota((64, 512), 0), iota((64, 512), 1)
    sel_n = hot((shr(nr, 1) == shr(nc, 4)) & ((nc & 15) == 8 + (nr & 1)))

    steps(1, NB, lambda i: a_out(i).wait_recv())
    zrows = pl.ds(pl.multiple_of(z * 64, 64), 64)
    whole = nn(sel_q[...], a_recv[:, 0:QW]).astype(BF16)
    for e in range(8):
        q_all[zrows, e * QW : (e + 1) * QW] = whole[e * 64 : (e + 1) * 64, :]
    q_all[zrows, D:] = nn(sel_n, a_recv[:, QW:]).astype(BF16)
    left, right = slice(0, PW), slice(PW, D + 128)

    def q_hop(dz_block, columns, dz, k):
        piece = q_all.at[block_rows(dz_block), columns]
        return z_copy(piece, piece, zq_s, zq_r, dz, k)

    q_out = [
        q_hop(0, left, 1, 0), q_hop(0, right, 3, 3), q_hop(0, right, 1, 1), q_hop(0, left, 3, 4),
        q_hop(3, left, 1, 2), q_hop(1, right, 3, 5),
    ]
    for copy in q_out[:4]:
        copy.start()
    p_meta[...] = nn(sel_m, a_recv[:, QW:]).astype(BF16)
    q_hop(3, left, 1, 0).wait_recv()
    q_out[4].start()
    q_hop(1, right, 3, 3).wait_recv()
    q_out[5].start()

    ur, uc = iota((64, 128), 0), iota((64, 128), 1)
    pair = (shr(ur, 3) == shr(uc, 4)) & ((ur & 7) == (uc & 7))
    sel_u = [hot(pair & ((uc & 8) == 8 * h)) for h in range(2)]

    def arrive(g, lo):
        steps(lo, 8 * (g + 1), lambda i: b_out(i).wait_recv())
        for j in range(PW // CT):
            got = b_recv[g * 128 : (g + 1) * 128, j * CT : (j + 1) * CT]
            for h in range(2):
                columns = slice(h * PW + j * CT, h * PW + (j + 1) * CT)
                p_all[g * 64 : (g + 1) * 64, columns] = nn(sel_u[h], got).astype(BF16)

    def score_rows(lo, hi):
        acc = nn(p_all[lo:hi, 0:CT], q_t[0:CT, :])
        for j in range(1, D // CT):
            acc = acc + nn(p_all[lo:hi, j * CT : (j + 1) * CT], q_t[j * CT : (j + 1) * CT, :])
        return acc * SCALE

    def row_stats(s, lo, hi):
        permitted = live[lo:hi, :] > 0.5
        top = jnp.max(jnp.where(permitted, s, FILL), axis=0, keepdims=True)
        e = jnp.where(permitted, jnp.exp(s - top), 0.0)
        return top, jnp.sum(e, axis=0, keepdims=True), e

    for g in range(3):
        arrive(g, max(1, 8 * g))

    q_hop(3, right, 1, 1).wait_recv()
    q_hop(1, left, 3, 4).wait_recv()
    q_hop(2, left, 1, 2).wait_recv()
    q_hop(2, right, 3, 5).wait_recv()

    qm, pm = q_all[:, D:], p_meta[...]
    l256 = iota((256, 128), 1)
    reached = nt(jnp.where(l256 < 16, pm.astype(F32), 0.0).astype(BF16), qm)
    live[...] = jnp.where(reached > 0.5, 1.0, 0.0)
    er, el = iota((8, 128), 0), iota((8, 128), 1)
    q_dig = nt(hot((er < 2) & (el == 16 + er)), qm)
    q_lo, q_hi = q_dig[0:1, :], q_dig[1:2, :]
    q_code = jnp.where(q_lo > 0.5, q_hi * 256.0 + q_lo, -2.0)
    p_lo = pm[:, 16:17].astype(F32)
    slot = shr(iota((256, 1), 0), 3)
    dx, dc = slot & 3, shr(slot, 4)
    dy = (dx - shr(slot & 15, 2)) & 3
    p_dev = (((x - dx) & 3) * 8 + ((y - dy) & 3) * 2 + ((c + dc) & 1)) * NZ + z
    p_code = jnp.where(p_lo > 0.5, p_dev.astype(F32) * 256.0 + p_lo, -1.0)
    target[...] = jnp.where(p_code == q_code, SCALE, 0.0)

    def turn(j, carry):
        q_t[cols(j), :] = jnp.transpose(q_all[:, cols(j)].astype(F32)).astype(BF16)
        return carry

    lax.fori_loop(0, D // CT, turn, 0)
    top_a, total_a, e_a = row_stats(score_rows(0, 192), 0, 192)
    score[0:192, :] = e_a
    arrive(3, 24)
    top_b, total_b, e_b = row_stats(score_rows(192, 256), 192, 256)
    top = jnp.maximum(top_a, top_b)
    fix_a, fix_b = jnp.exp(top_a - top), jnp.exp(top_b - top)
    total = total_a * fix_a + total_b * fix_b

    stat[0:1, :] = top
    stat[1:2, :] = total
    stat[2:8, :] = jnp.zeros((6, 256), F32)
    st_out = {dz: z_copy(stat, stat_in.at[dz - 1], zs_s, zs_r, dz) for dz in (1, 3, 2)}
    for dz in (2, 1, 3):
        st_out[dz].start()
    score[192:256, :] = e_b
    for dz in (1, 3, 2):
        st_out[dz].wait_recv()
    tops = [top] + [stat_in[i, 0:1, :] for i in range(3)]
    sums = [total] + [stat_in[i, 1:2, :] for i in range(3)]
    row_top = jnp.maximum(jnp.maximum(tops[0], tops[1]), jnp.maximum(tops[2], tops[3]))
    row_total = sum(l * jnp.exp(m - row_top) for m, l in zip(tops, sums))
    share = SCALE * jnp.exp(top - row_top) / jnp.where(row_total > 0.0, row_total, 1.0)
    gs[0:192, :] = (score[0:192, :] * (share * fix_a) - target[0:192, :]).astype(BF16)
    gs[192:256, :] = (score[192:256, :] * (share * fix_b) - target[192:256, :]).astype(BF16)

    dr, dq = iota((128, 64), 0), iota((128, 64), 1)
    same = (shr(dr, 4) == shr(dq, 3)) & ((dr & 7) == (dq & 7))
    dup = [hot(same & ((dr & 8) == 8 * h)) for h in range(2)]

    def send_home(g):
        part_gs = gs[g * 64 : (g + 1) * 64, :]
        halves = [nn(dup[h], part_gs).astype(BF16) for h in range(2)]
        for j in range(PW // CT):
            acc = nn(halves[0], q_all[:, j * CT : (j + 1) * CT])
            acc = acc + nn(halves[1], q_all[:, PW + j * CT : PW + (j + 1) * CT])
            b_ret[g * 128 : (g + 1) * 128, j * CT : (j + 1) * CT] = acc.astype(BF16)
        steps(max(1, 8 * g), 8 * (g + 1), lambda i: b_home(i, me).start())

    send_home(0)

    gs_t = jnp.transpose(gs[...].astype(F32)).astype(BF16)

    def part_step(j, carry):
        part[:, cols(j)] = nn(gs_t, p_all[:, cols(j)]).astype(BF16)
        return carry

    lax.fori_loop(0, D // CT, part_step, 0)
    low, high = slice(0, PW), slice(PW, D)

    def part_hop(dz_block, columns, dst, dz, k):
        return z_copy(part.at[block_rows(dz_block), columns], dst, zg_s, zg_r, dz, k)

    pt_out = [
        part_hop(2, low, relay_in.at[0], 1, 0),
        part_hop(2, high, relay_in.at[1], 3, 1),
        part_hop(1, high, part_in.at[0, :, high], 1, 2),
        part_hop(3, low, part_in.at[1, :, low], 3, 3),
        part_hop(1, low, part_in.at[0, :, low], 1, 4),
        part_hop(3, high, part_in.at[1, :, high], 3, 5),
    ]
    for copy in pt_out[:4]:
        copy.start()

    for g in range(1, 4):
        send_home(g)
    b_back[mine, :] = b_ret[0:16, :]

    pt_out[0].wait_recv()
    up = part[block_rows(1), low].astype(F32) + relay_in[0].astype(F32)
    part[block_rows(1), low] = up.astype(BF16)
    pt_out[4].start()
    pt_out[1].wait_recv()
    down = part[block_rows(3), high].astype(F32) + relay_in[1].astype(F32)
    part[block_rows(3), high] = down.astype(BF16)
    pt_out[5].start()
    for copy in pt_out[2:]:
        copy.wait_recv()
    for e in range(8):
        ec = slice(e * QW, (e + 1) * QW)
        acc = part[zrows, ec].astype(F32)
        for i in range(2):
            acc = acc + part_in[i, :, ec].astype(F32)
        gq_stack[e * 64 : (e + 1) * 64, :] = acc.astype(BF16)
    a_ret[...] = tn(sel_q[...], gq_stack[...]).astype(BF16)
    steps(1, NB, lambda i: a_home(i, me).start())
    a_back[mine, :] = a_ret[0:16, :]
    steps(1, NB, lambda i: b_home(i, partner(i)).wait_recv())
    steps(1, NB, lambda i: a_home(i, partner(i)).wait_recv())

    steps(1, NB, lambda i: a_out(i).wait_send())
    steps(1, NB, lambda i: b_out(i).wait_send())
    steps(1, NB, lambda i: b_home(i, me).wait_send())
    steps(1, NB, lambda i: a_home(i, me).wait_send())
    for copy in q_out + pt_out:
        copy.wait_send()
    for dz in (1, 3, 2):
        st_out[dz].wait_send()


def unpack(a_back, b_back, g_q, g_p, outq_hbm, outp_hbm, q_buf, p_buf, sem):
    copies = []
    for j in range(PW // CT):
        got = tn(g_p[...], b_back[:, j * CT : (j + 1) * CT]).astype(BF16)
        for h in range(2):
            columns = slice(h * PW + j * CT, h * PW + (j + 1) * CT)
            p_buf[:, columns] = got[h * 128 : (h + 1) * 128, :]
            copy = pltpu.make_async_copy(
                p_buf.at[:, columns], outp_hbm.at[:, columns], sem.at[2 * j + h]
            )
            copy.start()
            copies.append(copy)
    back = tn(g_q[...], a_back[...]).astype(BF16)
    for e in range(8):
        q_buf[:, e * QW : (e + 1) * QW] = back[e * 32 : (e + 1) * 32, :]
    copy = pltpu.make_async_copy(q_buf, outq_hbm, sem.at[8])
    copy.start()
    for c in copies + [copy]:
        c.wait()


def per_device(queries, passages, query_cluster, passage_cluster, allowed, positive):
    vm = pltpu.VMEM
    dma = pltpu.SemaphoreType.DMA
    hbm = pl.BlockSpec(memory_space=pl.ANY)
    res = pl.BlockSpec(memory_space=vm)
    landed = pl.pallas_call(
        kernel,
        out_shape=(
            pltpu.VMEM((512, QW), BF16),
            pltpu.VMEM((512, PW), BF16),
            pltpu.VMEM((512, 256), BF16),
            pltpu.VMEM((512, 256), BF16),
        ),
        in_specs=[pl.BlockSpec(memory_space=pltpu.HBM)] * 6,
        out_specs=(res,) * 4,
        scratch_shapes=[
            vm((512, QW + 128), BF16), vm((512, QW + 128), BF16),
            vm((512, PW), BF16), vm((512, PW), BF16),
            vm((512, QW), BF16), vm((512, PW), BF16),
            vm((256, QW), BF16), vm((256, PW), BF16), vm((512, QW), BF16),
            vm((512, 512), BF16),
            vm((16, 256), I32), vm((128, 256), BF16),
            vm((1, 32), I32), vm((1, 32), I32), vm((1, 128), I32),
            vm((256, 128), BF16),
            vm((256, D + 128), BF16), vm((D, 256), BF16), vm((256, D), BF16),
            vm((256, 256), F32), vm((256, 256), F32), vm((256, 256), F32),
            vm((256, 256), BF16),
            vm((256, D), BF16), vm((2, 64, PW), BF16), vm((2, 64, D), BF16),
            vm((8, 256), F32), vm((3, 8, 256), F32),
        ]
        + [dma((NB,))] * 8
        + [dma((6,))] * 2
        + [dma((3,))] * 2
        + [dma((6,))] * 2
        + [dma((14,))],
        compiler_params=pltpu.CompilerParams(
            collective_id=0, has_side_effects=True, vmem_limit_bytes=54 * 1024 * 1024
        ),
        name="contrastive",
    )(
        queries,
        passages,
        query_cluster.reshape(1, -1),
        positive.reshape(1, -1),
        passage_cluster.reshape(1, -1),
        allowed.T,
    )
    return pl.pallas_call(
        unpack,
        out_shape=(
            jax.ShapeDtypeStruct(queries.shape, BF16),
            jax.ShapeDtypeStruct(passages.shape, BF16),
        ),
        in_specs=[res] * 4,
        out_specs=(hbm, hbm),
        scratch_shapes=[vm((32, D), BF16), vm((128, D), BF16), dma((9,))],
        compiler_params=pltpu.CompilerParams(vmem_limit_bytes=16 * 1024 * 1024),
        name="unpack",
    )(*landed)


def solution(mesh):
    rows = P(("pb", "pa"), None)
    flat = P(("pb", "pa"))
    return jax.shard_map(
        per_device,
        mesh=mesh,
        in_specs=(rows, rows, flat, flat, P(), flat),
        out_specs=(rows, rows),
        check_vma=False,
    )
```

```python
import functools

import jax
import jax.numpy as jnp
from jax import lax
from jax.experimental import pallas as pl
from jax.experimental.pallas import tpu as pltpu
from jax.sharding import PartitionSpec as P

MESH = pl.DeviceIdType.MESH
F32, BF16, I32 = jnp.float32, jnp.bfloat16, jnp.int32
D = 4096
NB = 32
NZ = 4
QW = 512
PW = 2048
CT = 512
SCALE = 50.0
FILL = -1e30


def iota(shape, dim):
    return lax.broadcasted_iota(I32, shape, dim)


def shr(a, n):
    return lax.shift_right_logical(a, jnp.full(a.shape, n, I32))


def hot(cond):
    return jnp.where(cond, 1.0, 0.0).astype(BF16)


def nn(a, b):
    return lax.dot_general(a, b, (((1,), (0,)), ((), ())), preferred_element_type=F32)


def nt(a, b):
    return lax.dot_general(a, b, (((1,), (1,)), ((), ())), preferred_element_type=F32)


def tn(a, b):
    return lax.dot_general(a, b, (((0,), (0,)), ((), ())), preferred_element_type=F32)


def cols(j, width=CT):
    return pl.ds(pl.multiple_of(j * width, width), width)


def rows16(i):
    return pl.ds(pl.multiple_of(i * 16, 16), 16)


def offset(i):
    j = i % 16
    dx = j % 4
    return dx, (dx + 4 - j // 4) % 4, i // 16


def hops(i):
    dx, dy, _ = offset(i)
    return min(dx, 4 - dx) + min(dy, 4 - dy)


FAR_FIRST = sorted(range(1, NB), key=hops, reverse=True)


def kernel(
    q_hbm, p_hbm, qc_hbm, pos_hbm, pc_hbm, allowed_hbm,
    a_back, p_grad, g_q,
    b_back, g_p, a_send, a_recv, b_send, b_recv, a_ret, b_ret,
    q_stack, p_stack, gq_stack, sel_q, allow_int, allow_buf, qc_buf, pos_buf, pc_buf, p_meta,
    q_all, q_t, p_all, score, live, target, gs, part, relay_in, part_in, stat, stat_in,
    as_s, as_r, bs_s, bs_r, ar_s, ar_r, br_s, br_r, zq_s, zq_r, zs_s, zs_r, zg_s, zg_r, in_sem,
):
    me = lax.axis_index("pb")
    z = lax.axis_index("pa")
    x, y, c = me // 8, (me // 2) % 4, me % 2

    def partner(i):
        dx, dy, dc = offset(i)
        return ((x + dx) % 4) * 8 + ((y + dy) % 4) * 2 + (c + dc) % 2

    def origin(i):
        dx, dy, dc = offset(i)
        return ((x + 4 - dx) % 4) * 8 + ((y + 4 - dy) % 4) * 2 + (c + dc) % 2

    barrier = pltpu.get_barrier_semaphore()
    for i in FAR_FIRST:
        pl.semaphore_signal(barrier, inc=1, device_id=(partner(i), z), device_id_type=MESH)
    for dz in (2, 1, 3):
        pl.semaphore_signal(barrier, inc=1, device_id=(me, (z + dz) % NZ), device_id_type=MESH)

    loads = [
        pltpu.make_async_copy(qc_hbm, qc_buf, in_sem.at[0]),
        pltpu.make_async_copy(pos_hbm, pos_buf, in_sem.at[1]),
        pltpu.make_async_copy(pc_hbm, pc_buf, in_sem.at[2]),
        pltpu.make_async_copy(allowed_hbm, allow_int, in_sem.at[3]),
    ]
    for e in range(8):
        loads.append(
            pltpu.make_async_copy(
                q_hbm.at[:, e * QW : (e + 1) * QW],
                q_stack.at[e * 32 : (e + 1) * 32, :],
                in_sem.at[4 + e],
            )
        )
    for h in range(2):
        loads.append(
            pltpu.make_async_copy(
                p_hbm.at[:, h * PW : (h + 1) * PW],
                p_stack.at[h * 128 : (h + 1) * 128, :],
                in_sem.at[12 + h],
            )
        )
    for load in loads:
        load.start()

    for load in loads[:4]:
        load.wait()
    qc_row, pos_row, pc_row = qc_buf[...], pos_buf[...], pc_buf[...]
    lane32, sub32 = iota((32, 32), 1), iota((32, 32), 0)
    qc_col = jnp.sum(jnp.where(lane32 == sub32, qc_row, 0), axis=1, keepdims=True)
    pos_col = jnp.sum(jnp.where(lane32 == sub32, pos_row, 0), axis=1, keepdims=True)
    qb_row, qb_col = shr(qc_row, 3), shr(qc_col, 3)
    q_before = jnp.where((qb_col == qb_row) & (sub32 < lane32), 1, 0)
    q_slot = qb_row * 2 + jnp.sum(q_before, axis=0, keepdims=True)
    lane128, sub128 = iota((128, 128), 1), iota((128, 128), 0)
    pc_col = jnp.sum(jnp.where(lane128 == sub128, pc_row, 0), axis=1, keepdims=True)
    pb_row, pb_col = shr(pc_row, 2), shr(pc_col, 2)
    p_before = jnp.where((pb_col == pb_row) & (sub128 < lane128), 1, 0)
    p_slot = pb_row * 2 + jnp.sum(p_before, axis=0, keepdims=True)

    spread = hot(iota((32, 256), 0) == (iota((32, 256), 1) & 31))
    q_slot8 = nn(jnp.broadcast_to(q_slot, (8, 32)).astype(F32).astype(BF16), spread)[0:1, :]
    big_r, big_c = iota((512, 256), 0), iota((512, 256), 1)
    g_q[...] = hot(
        (q_slot8 == shr(big_r, 3).astype(F32)) & (shr(big_c, 5) == (big_r & 7))
    )
    half_r = iota((512, 128), 0)
    here = p_slot == shr(half_r, 4) * 8 + (half_r & 7)
    g_p[:, 0:128] = hot(here & ((half_r & 8) == 0))
    g_p[:, 128:256] = hot(here & ((half_r & 8) == 8))

    allow_buf[...] = jnp.zeros_like(allow_buf)
    allow_buf[0:16, :] = allow_int[...].astype(F32).astype(BF16)
    l256c = iota((32, 256), 1)
    reach = nt(hot(l256c == qc_col), allow_buf[...])
    l32 = iota((32, 128), 1)
    q_num = jnp.where(l32 < 16, reach, 0.0)
    q_num = jnp.where(l32 == 16, (pos_col & 127).astype(F32) + 1.0, q_num)
    q_num = jnp.where(l32 == 17, shr(pos_col, 7).astype(F32), q_num).astype(BF16)
    p_num = jnp.where((lane128 < 16) & ((pc_col & 15) == lane128), 1.0, 0.0)
    p_num = jnp.where(lane128 == 16, sub128.astype(F32) + 1.0, p_num).astype(BF16)
    mr_p, mr_q = iota((512, 128), 0), iota((512, 32), 0)
    gm_p = hot((p_slot == shr(mr_p, 4) * 8 + (mr_p & 15)) & ((mr_p & 15) < 8))
    gm_q = hot((q_slot == shr(mr_q, 4) * 2 + (mr_q & 15) - 8) & (shr(mr_q & 15, 1) == 4))
    a_send[:, QW:] = (nn(gm_p, p_num) + nn(gm_q, q_num)).astype(BF16)
    for load in loads[4:12]:
        load.wait()
    a_send[:, 0:QW] = nn(g_q[...], q_stack[...]).astype(BF16)

    pl.semaphore_wait(barrier, NB - 1 + NZ - 1)

    def out_copy(src, dst, send, recv, i):
        d = partner(i)
        return pltpu.make_async_remote_copy(
            src_ref=src.at[rows16(d), :],
            dst_ref=dst.at[rows16(i), :],
            send_sem=send.at[i],
            recv_sem=recv.at[i],
            device_id=(d, z),
            device_id_type=MESH,
        )

    def back_copy(src, dst, send, recv, i, place):
        return pltpu.make_async_remote_copy(
            src_ref=src.at[rows16(i), :],
            dst_ref=dst.at[rows16(place), :],
            send_sem=send.at[i],
            recv_sem=recv.at[i],
            device_id=(origin(i), z),
            device_id_type=MESH,
        )

    def steps(lo, hi, act):
        def body(i, carry):
            act(i)
            return carry

        lax.fori_loop(lo, hi, body, 0)

    a_out = functools.partial(out_copy, a_send, a_recv, as_s, as_r)
    b_out = functools.partial(out_copy, b_send, b_recv, bs_s, bs_r)
    a_home = functools.partial(back_copy, a_ret, a_back, ar_s, ar_r)
    b_home = functools.partial(back_copy, b_ret, b_back, br_s, br_r)

    def z_copy(src, dst, send, recv, dz, k=None):
        k = dz - 1 if k is None else k
        return pltpu.make_async_remote_copy(
            src_ref=src,
            dst_ref=dst,
            send_sem=send.at[k],
            recv_sem=recv.at[k],
            device_id=(me, (z + dz) % NZ),
            device_id_type=MESH,
        )

    def block_rows(dz):
        return pl.ds(pl.multiple_of(((z + dz) % NZ) * 64, 64), 64)

    mine = rows16(me)
    steps(1, NB, lambda i: a_out(i).start())
    a_recv[0:16, :] = a_send[mine, :]

    for load in loads[12:]:
        load.wait()

    def pack_p(j, carry):
        b_send[:, cols(j)] = nn(g_p[...], p_stack[:, cols(j)]).astype(BF16)
        return carry

    lax.fori_loop(0, PW // CT, pack_p, 0)
    steps(1, NB, lambda i: b_out(i).start())
    b_recv[0:16, :] = b_send[mine, :]

    sr, sc = iota((512, 512), 0), iota((512, 512), 1)
    sel_q[...] = hot((shr(sr, 6) == (sc & 7)) & ((sr & 63) == shr(sc, 3)))
    hr, hc = iota((256, 512), 0), iota((256, 512), 1)
    half = (shr(hr, 3) == shr(hc, 4)) & ((hr & 7) == (hc & 7))
    sel_m = hot(half & ((hc & 8) == 0))
    wr, wc = iota((128, 128), 0), iota((128, 128), 1)
    sel_w = hot((shr(wr, 4) == (wc & 7)) & ((wr & 15) == shr(wc, 3)))
    nr, nc = iota((16, 128), 0), iota((16, 128), 1)
    sel_n = hot((shr(nr, 1) == shr(nc, 4)) & ((nc & 15) == 8 + (nr & 1)))

    left, right = slice(0, PW), slice(PW, D + 128)

    def group_rows(dz, g):
        return pl.ds(pl.multiple_of(((z + dz) % NZ) * 64 + g * 16, 16), 16)

    def q_hop(dz_block, columns, dz, k, g):
        piece = q_all.at[group_rows(dz_block, g), columns]
        return z_copy(piece, piece, zq_s, zq_r, dz, g * 6 + k)

    q_out = []

    def send_on(copy):
        copy.start()
        q_out.append(copy)

    def relay(g):
        q_hop(3, left, 1, 0, g).wait_recv()
        send_on(q_hop(3, left, 1, 2, g))
        q_hop(1, right, 3, 3, g).wait_recv()
        send_on(q_hop(1, right, 3, 5, g))

    for g in range(4):
        steps(max(1, 8 * g), 8 * (g + 1), lambda i: a_out(i).wait_recv())
        come = slice(128 * g, 128 * (g + 1))
        whole = nn(sel_w, a_recv[come, 0:QW]).astype(BF16)
        rows = group_rows(0, g)
        for e in range(8):
            q_all[rows, e * QW : (e + 1) * QW] = whole[e * 16 : (e + 1) * 16, :]
        q_all[rows, D:] = nn(sel_n, a_recv[come, QW:]).astype(BF16)
        send_on(q_hop(0, left, 1, 0, g))
        send_on(q_hop(0, right, 3, 3, g))
        send_on(q_hop(0, right, 1, 1, g))
        send_on(q_hop(0, left, 3, 4, g))
        if g:
            relay(g - 1)
    relay(3)
    p_meta[...] = nn(sel_m, a_recv[:, QW:]).astype(BF16)
    ur, uc = iota((64, 128), 0), iota((64, 128), 1)
    pair = (shr(ur, 3) == shr(uc, 4)) & ((ur & 7) == (uc & 7))
    sel_u = [hot(pair & ((uc & 8) == 8 * h)) for h in range(2)]

    def arrive(g, lo):
        steps(lo, 8 * (g + 1), lambda i: b_out(i).wait_recv())
        for j in range(PW // CT):
            got = b_recv[g * 128 : (g + 1) * 128, j * CT : (j + 1) * CT]
            for h in range(2):
                columns = slice(h * PW + j * CT, h * PW + (j + 1) * CT)
                p_all[g * 64 : (g + 1) * 64, columns] = nn(sel_u[h], got).astype(BF16)

    def score_rows(lo, hi):
        acc = nn(p_all[lo:hi, 0:CT], q_t[0:CT, :])
        for j in range(1, D // CT):
            acc = acc + nn(p_all[lo:hi, j * CT : (j + 1) * CT], q_t[j * CT : (j + 1) * CT, :])
        return acc * SCALE

    def row_stats(s, lo, hi):
        permitted = live[lo:hi, :] > 0.5
        top = jnp.max(jnp.where(permitted, s, FILL), axis=0, keepdims=True)
        e = jnp.where(permitted, jnp.exp(s - top), 0.0)
        return top, jnp.sum(e, axis=0, keepdims=True), e

    for g in range(3):
        arrive(g, max(1, 8 * g))

    for g in range(4):
        q_hop(3, right, 1, 1, g).wait_recv()
        q_hop(1, left, 3, 4, g).wait_recv()
        q_hop(2, left, 1, 2, g).wait_recv()
        q_hop(2, right, 3, 5, g).wait_recv()

    qm, pm = q_all[:, D:], p_meta[...]
    l256 = iota((256, 128), 1)
    reached = nt(jnp.where(l256 < 16, pm.astype(F32), 0.0).astype(BF16), qm)
    live[...] = jnp.where(reached > 0.5, 1.0, 0.0)
    er, el = iota((8, 128), 0), iota((8, 128), 1)
    q_dig = nt(hot((er < 2) & (el == 16 + er)), qm)
    q_lo, q_hi = q_dig[0:1, :], q_dig[1:2, :]
    q_code = jnp.where(q_lo > 0.5, q_hi * 256.0 + q_lo, -2.0)
    p_lo = pm[:, 16:17].astype(F32)
    slot = shr(iota((256, 1), 0), 3)
    dx, dc = slot & 3, shr(slot, 4)
    dy = (dx - shr(slot & 15, 2)) & 3
    p_dev = (((x - dx) & 3) * 8 + ((y - dy) & 3) * 2 + ((c + dc) & 1)) * NZ + z
    p_code = jnp.where(p_lo > 0.5, p_dev.astype(F32) * 256.0 + p_lo, -1.0)
    target[...] = jnp.where(p_code == q_code, SCALE, 0.0)

    def turn(j, carry):
        q_t[cols(j), :] = jnp.transpose(q_all[:, cols(j)].astype(F32)).astype(BF16)
        return carry

    lax.fori_loop(0, D // CT, turn, 0)
    top_a, total_a, e_a = row_stats(score_rows(0, 192), 0, 192)
    score[0:192, :] = e_a
    arrive(3, 24)
    top_b, total_b, e_b = row_stats(score_rows(192, 256), 192, 256)
    top = jnp.maximum(top_a, top_b)
    fix_a, fix_b = jnp.exp(top_a - top), jnp.exp(top_b - top)
    total = total_a * fix_a + total_b * fix_b

    stat[0:1, :] = top
    stat[1:2, :] = total
    stat[2:8, :] = jnp.zeros((6, 256), F32)
    st_out = {dz: z_copy(stat, stat_in.at[dz - 1], zs_s, zs_r, dz) for dz in (1, 3, 2)}
    for dz in (2, 1, 3):
        st_out[dz].start()
    score[192:256, :] = e_b
    for dz in (1, 3, 2):
        st_out[dz].wait_recv()
    tops = [top] + [stat_in[i, 0:1, :] for i in range(3)]
    sums = [total] + [stat_in[i, 1:2, :] for i in range(3)]
    row_top = jnp.maximum(jnp.maximum(tops[0], tops[1]), jnp.maximum(tops[2], tops[3]))
    row_total = sum(l * jnp.exp(m - row_top) for m, l in zip(tops, sums))
    share = SCALE * jnp.exp(top - row_top) / jnp.where(row_total > 0.0, row_total, 1.0)
    gs[0:192, :] = (score[0:192, :] * (share * fix_a) - target[0:192, :]).astype(BF16)
    gs[192:256, :] = (score[192:256, :] * (share * fix_b) - target[192:256, :]).astype(BF16)

    dr, dq = iota((128, 64), 0), iota((128, 64), 1)
    same = (shr(dr, 4) == shr(dq, 3)) & ((dr & 7) == (dq & 7))
    dup = [hot(same & ((dr & 8) == 8 * h)) for h in range(2)]

    def send_home(g):
        part_gs = gs[g * 64 : (g + 1) * 64, :]
        halves = [nn(dup[h], part_gs).astype(BF16) for h in range(2)]
        for j in range(PW // CT):
            acc = nn(halves[0], q_all[:, j * CT : (j + 1) * CT])
            acc = acc + nn(halves[1], q_all[:, PW + j * CT : PW + (j + 1) * CT])
            b_ret[g * 128 : (g + 1) * 128, j * CT : (j + 1) * CT] = acc.astype(BF16)
        steps(max(1, 8 * g), 8 * (g + 1), lambda i: b_home(i, me).start())

    send_home(0)

    gs_t = jnp.transpose(gs[...].astype(F32)).astype(BF16)

    def part_step(j, carry):
        part[:, cols(j)] = nn(gs_t, p_all[:, cols(j)]).astype(BF16)
        return carry

    lax.fori_loop(0, D // CT, part_step, 0)
    low, high = slice(0, PW), slice(PW, D)

    def part_hop(dz_block, columns, dst, dz, k):
        return z_copy(part.at[block_rows(dz_block), columns], dst, zg_s, zg_r, dz, k)

    pt_out = [
        part_hop(2, low, relay_in.at[0], 1, 0),
        part_hop(2, high, relay_in.at[1], 3, 1),
        part_hop(1, high, part_in.at[0, :, high], 1, 2),
        part_hop(3, low, part_in.at[1, :, low], 3, 3),
        part_hop(1, low, part_in.at[0, :, low], 1, 4),
        part_hop(3, high, part_in.at[1, :, high], 3, 5),
    ]
    for copy in pt_out[:4]:
        copy.start()

    for g in range(1, 4):
        send_home(g)
    b_back[mine, :] = b_ret[0:16, :]

    pt_out[0].wait_recv()
    up = part[block_rows(1), low].astype(F32) + relay_in[0].astype(F32)
    part[block_rows(1), low] = up.astype(BF16)
    pt_out[4].start()
    pt_out[1].wait_recv()
    down = part[block_rows(3), high].astype(F32) + relay_in[1].astype(F32)
    part[block_rows(3), high] = down.astype(BF16)
    pt_out[5].start()
    for copy in pt_out[2:]:
        copy.wait_recv()
    for e in range(8):
        ec = slice(e * QW, (e + 1) * QW)
        acc = part[block_rows(0), ec].astype(F32)
        for i in range(2):
            acc = acc + part_in[i, :, ec].astype(F32)
        gq_stack[e * 64 : (e + 1) * 64, :] = acc.astype(BF16)
    a_ret[...] = tn(sel_q[...], gq_stack[...]).astype(BF16)
    steps(1, NB, lambda i: a_home(i, me).start())
    a_back[mine, :] = a_ret[0:16, :]
    steps(1, NB, lambda i: b_home(i, partner(i)).wait_recv())
    for j in range(PW // CT):
        got = tn(g_p[...], b_back[:, j * CT : (j + 1) * CT]).astype(BF16)
        for h in range(2):
            columns = slice(h * PW + j * CT, h * PW + (j + 1) * CT)
            p_grad[:, columns] = got[h * 128 : (h + 1) * 128, :]
    steps(1, NB, lambda i: a_home(i, partner(i)).wait_recv())

    steps(1, NB, lambda i: a_out(i).wait_send())
    steps(1, NB, lambda i: b_out(i).wait_send())
    steps(1, NB, lambda i: b_home(i, me).wait_send())
    steps(1, NB, lambda i: a_home(i, me).wait_send())
    for copy in q_out + pt_out:
        copy.wait_send()
    for dz in (1, 3, 2):
        st_out[dz].wait_send()


def unpack(a_back, p_grad, g_q, outq_hbm, outp_hbm, q_buf, sem):
    copies = []
    for h in range(8):
        rows = slice(h * 16, (h + 1) * 16)
        copies.append(pltpu.make_async_copy(p_grad.at[rows, :], outp_hbm.at[rows, :], sem.at[h]))
        copies[-1].start()
    back = tn(g_q[...], a_back[...]).astype(BF16)
    for e in range(8):
        q_buf[:, e * QW : (e + 1) * QW] = back[e * 32 : (e + 1) * 32, :]
    for h in range(2):
        rows = slice(h * 16, (h + 1) * 16)
        copies.append(pltpu.make_async_copy(q_buf.at[rows, :], outq_hbm.at[rows, :], sem.at[8 + h]))
        copies[-1].start()
    for copy in copies:
        copy.wait()


def per_device(queries, passages, query_cluster, passage_cluster, allowed, positive):
    vm = pltpu.VMEM
    dma = pltpu.SemaphoreType.DMA
    hbm = pl.BlockSpec(memory_space=pl.ANY)
    res = pl.BlockSpec(memory_space=vm)
    landed = pl.pallas_call(
        kernel,
        out_shape=(
            pltpu.VMEM((512, QW), BF16),
            pltpu.VMEM((128, D), BF16),
            pltpu.VMEM((512, 256), BF16),
        ),
        in_specs=[pl.BlockSpec(memory_space=pltpu.HBM)] * 6,
        out_specs=(res,) * 3,
        scratch_shapes=[
            vm((512, PW), BF16), vm((512, 256), BF16),
            vm((512, QW + 128), BF16), vm((512, QW + 128), BF16),
            vm((512, PW), BF16), vm((512, PW), BF16),
            vm((512, QW), BF16), vm((512, PW), BF16),
            vm((256, QW), BF16), vm((256, PW), BF16), vm((512, QW), BF16),
            vm((512, 512), BF16),
            vm((16, 256), I32), vm((128, 256), BF16),
            vm((1, 32), I32), vm((1, 32), I32), vm((1, 128), I32),
            vm((256, 128), BF16),
            vm((256, D + 128), BF16), vm((D, 256), BF16), vm((256, D), BF16),
            vm((256, 256), F32), vm((256, 256), F32), vm((256, 256), F32),
            vm((256, 256), BF16),
            vm((256, D), BF16), vm((2, 64, PW), BF16), vm((2, 64, D), BF16),
            vm((8, 256), F32), vm((3, 8, 256), F32),
        ]
        + [dma((NB,))] * 8
        + [dma((24,))] * 2
        + [dma((3,))] * 2
        + [dma((6,))] * 2
        + [dma((14,))],
        compiler_params=pltpu.CompilerParams(
            collective_id=0, has_side_effects=True, vmem_limit_bytes=54 * 1024 * 1024
        ),
        name="contrastive",
    )(
        queries,
        passages,
        query_cluster.reshape(1, -1),
        positive.reshape(1, -1),
        passage_cluster.reshape(1, -1),
        allowed.T,
    )
    return pl.pallas_call(
        unpack,
        out_shape=(
            jax.ShapeDtypeStruct(queries.shape, BF16),
            jax.ShapeDtypeStruct(passages.shape, BF16),
        ),
        in_specs=[res] * 3,
        out_specs=(hbm, hbm),
        scratch_shapes=[vm((32, D), BF16), dma((10,))],
        compiler_params=pltpu.CompilerParams(vmem_limit_bytes=16 * 1024 * 1024),
        name="unpack",
    )(*landed)


def solution(mesh):
    rows = P(("pb", "pa"), None)
    flat = P(("pb", "pa"))
    return jax.shard_map(
        per_device,
        mesh=mesh,
        in_specs=(rows, rows, flat, flat, P(), flat),
        out_specs=(rows, rows),
        check_vma=False,
    )
```

```python
import functools

import jax
import jax.numpy as jnp
from jax import lax
from jax.experimental import pallas as pl
from jax.experimental.pallas import tpu as pltpu
from jax.sharding import PartitionSpec as P

MESH = pl.DeviceIdType.MESH
F32, BF16, I32 = jnp.float32, jnp.bfloat16, jnp.int32
D = 4096
NB = 32
NZ = 4
QW = 512
PW = 2048
CT = 512
SCALE = 50.0
FILL = -1e30


def iota(shape, dim):
    return lax.broadcasted_iota(I32, shape, dim)


def shr(a, n):
    return lax.shift_right_logical(a, jnp.full(a.shape, n, I32))


def hot(cond):
    return jnp.where(cond, 1.0, 0.0).astype(BF16)


def nn(a, b):
    return lax.dot_general(a, b, (((1,), (0,)), ((), ())), preferred_element_type=F32)


def nt(a, b):
    return lax.dot_general(a, b, (((1,), (1,)), ((), ())), preferred_element_type=F32)


def tn(a, b):
    return lax.dot_general(a, b, (((0,), (0,)), ((), ())), preferred_element_type=F32)


def cols(j, width=CT):
    return pl.ds(pl.multiple_of(j * width, width), width)


def rows16(i):
    return pl.ds(pl.multiple_of(i * 16, 16), 16)


def offset(i):
    j = i % 16
    dx = j % 4
    return dx, (dx + 4 - j // 4) % 4, i // 16


def hops(i):
    dx, dy, _ = offset(i)
    return min(dx, 4 - dx) + min(dy, 4 - dy)


FAR_FIRST = sorted(range(1, NB), key=hops, reverse=True)


def kernel(
    q_hbm, p_hbm, qc_hbm, pos_hbm, pc_hbm, allowed_hbm,
    a_back, p_grad, g_q,
    b_back, g_p, a_send, a_recv, b_send, b_recv, a_ret, b_ret,
    q_stack, p_stack, gq_stack, sel_q, allow_int, allow_buf, qc_buf, pos_buf, pc_buf, m_send, m_recv, m_flat,
    q_all, q_t, p_all, score, live, target, gs, part, relay_in, part_in, stat, stat_in,
    as_s, as_r, ms_s, ms_r, bs_s, bs_r, ar_s, ar_r, br_s, br_r, zq_s, zq_r, zs_s, zs_r, zg_s, zg_r, in_sem,
):
    me = lax.axis_index("pb")
    z = lax.axis_index("pa")
    x, y, c = me // 8, (me // 2) % 4, me % 2

    def partner(i):
        dx, dy, dc = offset(i)
        return ((x + dx) % 4) * 8 + ((y + dy) % 4) * 2 + (c + dc) % 2

    def origin(i):
        dx, dy, dc = offset(i)
        return ((x + 4 - dx) % 4) * 8 + ((y + 4 - dy) % 4) * 2 + (c + dc) % 2

    barrier = pltpu.get_barrier_semaphore()
    for i in FAR_FIRST:
        pl.semaphore_signal(barrier, inc=1, device_id=(partner(i), z), device_id_type=MESH)
    for dz in (2, 1, 3):
        pl.semaphore_signal(barrier, inc=1, device_id=(me, (z + dz) % NZ), device_id_type=MESH)

    loads = [
        pltpu.make_async_copy(qc_hbm, qc_buf, in_sem.at[0]),
        pltpu.make_async_copy(pos_hbm, pos_buf, in_sem.at[1]),
        pltpu.make_async_copy(pc_hbm, pc_buf, in_sem.at[2]),
        pltpu.make_async_copy(allowed_hbm, allow_int, in_sem.at[3]),
    ]
    for e in range(8):
        loads.append(
            pltpu.make_async_copy(
                q_hbm.at[:, e * QW : (e + 1) * QW],
                q_stack.at[e * 32 : (e + 1) * 32, :],
                in_sem.at[4 + e],
            )
        )
    for h in range(2):
        loads.append(
            pltpu.make_async_copy(
                p_hbm.at[:, h * PW : (h + 1) * PW],
                p_stack.at[h * 128 : (h + 1) * 128, :],
                in_sem.at[12 + h],
            )
        )
    for load in loads:
        load.start()

    for load in loads[:4]:
        load.wait()
    qc_row, pos_row, pc_row = qc_buf[...], pos_buf[...], pc_buf[...]
    lane32, sub32 = iota((32, 32), 1), iota((32, 32), 0)
    qc_col = jnp.sum(jnp.where(lane32 == sub32, qc_row, 0), axis=1, keepdims=True)
    pos_col = jnp.sum(jnp.where(lane32 == sub32, pos_row, 0), axis=1, keepdims=True)
    qb_row, qb_col = shr(qc_row, 3), shr(qc_col, 3)
    q_before = jnp.where((qb_col == qb_row) & (sub32 < lane32), 1, 0)
    q_slot = qb_row * 2 + jnp.sum(q_before, axis=0, keepdims=True)
    lane128, sub128 = iota((128, 128), 1), iota((128, 128), 0)
    pc_col = jnp.sum(jnp.where(lane128 == sub128, pc_row, 0), axis=1, keepdims=True)
    pb_row, pb_col = shr(pc_row, 2), shr(pc_col, 2)
    p_before = jnp.where((pb_col == pb_row) & (sub128 < lane128), 1, 0)
    p_slot = pb_row * 2 + jnp.sum(p_before, axis=0, keepdims=True)

    spread = hot(iota((32, 256), 0) == (iota((32, 256), 1) & 31))
    q_slot8 = nn(jnp.broadcast_to(q_slot, (8, 32)).astype(F32).astype(BF16), spread)[0:1, :]
    big_r, big_c = iota((512, 256), 0), iota((512, 256), 1)
    g_q[...] = hot(
        (q_slot8 == shr(big_r, 3).astype(F32)) & (shr(big_c, 5) == (big_r & 7))
    )
    half_r = iota((512, 128), 0)
    here = p_slot == shr(half_r, 4) * 8 + (half_r & 7)
    g_p[:, 0:128] = hot(here & ((half_r & 8) == 0))
    g_p[:, 128:256] = hot(here & ((half_r & 8) == 8))

    allow_buf[...] = jnp.zeros_like(allow_buf)
    table = allow_int[...].astype(F32).astype(BF16)
    allow_buf[16:32, :] = table
    allow_buf[32:48, :] = table
    reach = nt(hot(iota((32, 256), 1) == qc_col), allow_buf[...])
    q_slot_col = jnp.sum(jnp.where(lane32 == sub32, q_slot, 0), axis=1, keepdims=True)
    p_slot_col = jnp.sum(jnp.where(lane128 == sub128, p_slot, 0), axis=1, keepdims=True)
    l32 = iota((32, 128), 1)
    second = q_slot_col & 1
    q_num = jnp.where(shr(l32, 4) == 1 + second, reach, 0.0)
    q_num = jnp.where(l32 == 48 + second, (pos_col & 127).astype(F32) + 1.0, q_num)
    q_num = jnp.where(l32 == 50 + second, shr(pos_col, 7).astype(F32), q_num).astype(BF16)
    kth = p_slot_col & 7
    p_num = jnp.where(lane128 == kth, sub128.astype(F32) + 1.0, 0.0)
    p_num = jnp.where(lane128 == 8 + kth, (pc_col & 15).astype(F32), p_num).astype(BF16)
    to_q = hot(shr(q_slot, 1) == iota((32, 32), 0))
    to_p = hot(shr(p_slot, 3) == iota((32, 128), 0))
    m_flat[...] = nn(to_p, p_num) + nn(to_q, q_num)

    def spread_rows(i, carry):
        m_send[i] = m_flat[pl.ds(i, 1), :]
        return carry

    lax.fori_loop(0, NB, spread_rows, 0)
    m_flat[...] = jnp.zeros_like(m_flat)
    for load in loads[4:12]:
        load.wait()
    a_send[...] = nn(g_q[...], q_stack[...]).astype(BF16)

    pl.semaphore_wait(barrier, NB - 1 + NZ - 1)

    def out_copy(src, dst, send, recv, i):
        d = partner(i)
        return pltpu.make_async_remote_copy(
            src_ref=src.at[rows16(d), :],
            dst_ref=dst.at[rows16(i), :],
            send_sem=send.at[i],
            recv_sem=recv.at[i],
            device_id=(d, z),
            device_id_type=MESH,
        )

    def m_out(i):
        d = partner(i)
        return pltpu.make_async_remote_copy(
            src_ref=m_send.at[d],
            dst_ref=m_recv.at[i],
            send_sem=ms_s.at[i],
            recv_sem=ms_r.at[i],
            device_id=(d, z),
            device_id_type=MESH,
        )

    def back_copy(src, dst, send, recv, i, place):
        return pltpu.make_async_remote_copy(
            src_ref=src.at[rows16(i), :],
            dst_ref=dst.at[rows16(place), :],
            send_sem=send.at[i],
            recv_sem=recv.at[i],
            device_id=(origin(i), z),
            device_id_type=MESH,
        )

    def steps(lo, hi, act):
        def body(i, carry):
            act(i)
            return carry

        lax.fori_loop(lo, hi, body, 0)

    a_out = functools.partial(out_copy, a_send, a_recv, as_s, as_r)
    b_out = functools.partial(out_copy, b_send, b_recv, bs_s, bs_r)
    a_home = functools.partial(back_copy, a_ret, a_back, ar_s, ar_r)
    b_home = functools.partial(back_copy, b_ret, b_back, br_s, br_r)

    def z_copy(src, dst, send, recv, dz, k=None):
        k = dz - 1 if k is None else k
        return pltpu.make_async_remote_copy(
            src_ref=src,
            dst_ref=dst,
            send_sem=send.at[k],
            recv_sem=recv.at[k],
            device_id=(me, (z + dz) % NZ),
            device_id_type=MESH,
        )

    def block_rows(dz):
        return pl.ds(pl.multiple_of(((z + dz) % NZ) * 64, 64), 64)

    mine = rows16(me)
    def send_queries(i):
        a_out(i).start()
        m_out(i).start()

    steps(1, NB, send_queries)
    a_recv[0:16, :] = a_send[mine, :]
    m_recv[0] = m_send[me]

    for load in loads[12:]:
        load.wait()

    def pack_p(j, carry):
        b_send[:, cols(j)] = nn(g_p[...], p_stack[:, cols(j)]).astype(BF16)
        return carry

    lax.fori_loop(0, PW // CT, pack_p, 0)
    steps(1, NB, lambda i: b_out(i).start())
    b_recv[0:16, :] = b_send[mine, :]

    sr, sc = iota((512, 512), 0), iota((512, 512), 1)
    sel_q[...] = hot((shr(sr, 6) == (sc & 7)) & ((sr & 63) == shr(sc, 3)))
    wr, wc = iota((128, 128), 0), iota((128, 128), 1)
    sel_w = hot((shr(wr, 4) == (wc & 7)) & ((wr & 15) == shr(wc, 3)))
    fr, fc = iota((128, 128), 0), iota((128, 128), 1)
    pick = [
        hot(
            ((fr == 16 + 16 * r + fc) & (fc < 16))
            | ((fr == 48 + r) & (fc == 16))
            | ((fr == 50 + r) & (fc == 17))
        )
        for r in range(2)
    ]
    first = (iota((16, 128), 0) & 1) == 0

    left, right = slice(0, PW), slice(PW, D + 128)

    def group_rows(dz, g):
        return pl.ds(pl.multiple_of(((z + dz) % NZ) * 64 + g * 16, 16), 16)

    def q_hop(dz_block, columns, dz, k, g):
        piece = q_all.at[group_rows(dz_block, g), columns]
        return z_copy(piece, piece, zq_s, zq_r, dz, g * 6 + k)

    q_out = []

    def send_on(copy):
        copy.start()
        q_out.append(copy)

    def relay(g):
        q_hop(3, left, 1, 0, g).wait_recv()
        send_on(q_hop(3, left, 1, 2, g))
        q_hop(1, right, 3, 3, g).wait_recv()
        send_on(q_hop(1, right, 3, 5, g))

    for g in range(4):
        def take(i):
            m_flat[pl.ds(i, 1), :] = m_recv[i]

        def await_queries(i):
            a_out(i).wait_recv()
            m_out(i).wait_recv()

        steps(max(1, 8 * g), 8 * (g + 1), await_queries)
        steps(8 * g, 8 * (g + 1), take)
        come = slice(128 * g, 128 * (g + 1))
        whole = nn(sel_w, a_recv[come, :]).astype(BF16)
        rows = group_rows(0, g)
        for e in range(8):
            q_all[rows, e * QW : (e + 1) * QW] = whole[e * 16 : (e + 1) * 16, :]
        twice = hot(iota((16, 32), 1) == 8 * g + shr(iota((16, 32), 0), 1))
        nums = nn(twice, m_flat[...].astype(BF16)).astype(BF16)
        q_all[rows, D:] = jnp.where(first, nn(nums, pick[0]), nn(nums, pick[1])).astype(BF16)
        send_on(q_hop(0, left, 1, 0, g))
        send_on(q_hop(0, right, 3, 3, g))
        send_on(q_hop(0, right, 1, 1, g))
        send_on(q_hop(0, left, 3, 4, g))
        if g:
            relay(g - 1)
    relay(3)
    ur, uc = iota((64, 128), 0), iota((64, 128), 1)
    pair = (shr(ur, 3) == shr(uc, 4)) & ((ur & 7) == (uc & 7))
    sel_u = [hot(pair & ((uc & 8) == 8 * h)) for h in range(2)]

    def arrive(g, lo):
        steps(lo, 8 * (g + 1), lambda i: b_out(i).wait_recv())
        for j in range(PW // CT):
            got = b_recv[g * 128 : (g + 1) * 128, j * CT : (j + 1) * CT]
            for h in range(2):
                columns = slice(h * PW + j * CT, h * PW + (j + 1) * CT)
                p_all[g * 64 : (g + 1) * 64, columns] = nn(sel_u[h], got).astype(BF16)

    def score_rows(lo, hi):
        acc = nn(p_all[lo:hi, 0:CT], q_t[0:CT, :])
        for j in range(1, D // CT):
            acc = acc + nn(p_all[lo:hi, j * CT : (j + 1) * CT], q_t[j * CT : (j + 1) * CT, :])
        return acc * SCALE

    def row_stats(s, lo, hi):
        permitted = live[lo:hi, :] > 0.5
        top = jnp.max(jnp.where(permitted, s, FILL), axis=0, keepdims=True)
        e = jnp.where(permitted, jnp.exp(s - top), 0.0)
        return top, jnp.sum(e, axis=0, keepdims=True), e

    for g in range(3):
        arrive(g, max(1, 8 * g))

    for g in range(4):
        q_hop(3, right, 1, 1, g).wait_recv()
        q_hop(1, left, 3, 4, g).wait_recv()
        q_hop(2, left, 1, 2, g).wait_recv()
        q_hop(2, right, 3, 5, g).wait_recv()

    qm = q_all[:, D:]
    eightfold = hot(iota((256, 32), 1) == shr(iota((256, 32), 0), 3))
    p_nums = nn(eightfold, m_flat[...].astype(BF16))
    l256, k256 = iota((256, 128), 1), iota((256, 128), 0) & 7
    p_lo = jnp.sum(jnp.where(l256 == k256, p_nums, 0.0), axis=1, keepdims=True)
    p_cl = jnp.sum(jnp.where(l256 == 8 + k256, p_nums, 0.0), axis=1, keepdims=True)
    reached = nt(hot((l256.astype(F32) == p_cl) & (p_lo > 0.5)), qm)
    live[...] = jnp.where(reached > 0.5, 1.0, 0.0)
    er, el = iota((8, 128), 0), iota((8, 128), 1)
    q_dig = nt(hot((er < 2) & (el == 16 + er)), qm)
    q_lo, q_hi = q_dig[0:1, :], q_dig[1:2, :]
    q_code = jnp.where(q_lo > 0.5, q_hi * 256.0 + q_lo, -2.0)
    slot = shr(iota((256, 1), 0), 3)
    dx, dc = slot & 3, shr(slot, 4)
    dy = (dx - shr(slot & 15, 2)) & 3
    p_dev = (((x - dx) & 3) * 8 + ((y - dy) & 3) * 2 + ((c + dc) & 1)) * NZ + z
    p_code = jnp.where(p_lo > 0.5, p_dev.astype(F32) * 256.0 + p_lo, -1.0)
    target[...] = jnp.where(p_code == q_code, SCALE, 0.0)

    def turn(j, carry):
        q_t[cols(j), :] = jnp.transpose(q_all[:, cols(j)].astype(F32)).astype(BF16)
        return carry

    lax.fori_loop(0, D // CT, turn, 0)
    top_a, total_a, e_a = row_stats(score_rows(0, 192), 0, 192)
    score[0:192, :] = e_a
    arrive(3, 24)
    top_b, total_b, e_b = row_stats(score_rows(192, 256), 192, 256)
    top = jnp.maximum(top_a, top_b)
    fix_a, fix_b = jnp.exp(top_a - top), jnp.exp(top_b - top)
    total = total_a * fix_a + total_b * fix_b

    stat[0:1, :] = top
    stat[1:2, :] = total
    stat[2:8, :] = jnp.zeros((6, 256), F32)
    st_out = {dz: z_copy(stat, stat_in.at[dz - 1], zs_s, zs_r, dz) for dz in (1, 3, 2)}
    for dz in (2, 1, 3):
        st_out[dz].start()
    score[192:256, :] = e_b
    for dz in (1, 3, 2):
        st_out[dz].wait_recv()
    tops = [top] + [stat_in[i, 0:1, :] for i in range(3)]
    sums = [total] + [stat_in[i, 1:2, :] for i in range(3)]
    row_top = jnp.maximum(jnp.maximum(tops[0], tops[1]), jnp.maximum(tops[2], tops[3]))
    row_total = sum(l * jnp.exp(m - row_top) for m, l in zip(tops, sums))
    share = SCALE * jnp.exp(top - row_top) / jnp.where(row_total > 0.0, row_total, 1.0)
    gs[0:192, :] = (score[0:192, :] * (share * fix_a) - target[0:192, :]).astype(BF16)
    gs[192:256, :] = (score[192:256, :] * (share * fix_b) - target[192:256, :]).astype(BF16)

    dr, dq = iota((128, 64), 0), iota((128, 64), 1)
    same = (shr(dr, 4) == shr(dq, 3)) & ((dr & 7) == (dq & 7))
    dup = [hot(same & ((dr & 8) == 8 * h)) for h in range(2)]

    def send_home(g):
        part_gs = gs[g * 64 : (g + 1) * 64, :]
        halves = [nn(dup[h], part_gs).astype(BF16) for h in range(2)]
        for j in range(PW // CT):
            acc = nn(halves[0], q_all[:, j * CT : (j + 1) * CT])
            acc = acc + nn(halves[1], q_all[:, PW + j * CT : PW + (j + 1) * CT])
            b_ret[g * 128 : (g + 1) * 128, j * CT : (j + 1) * CT] = acc.astype(BF16)
        steps(max(1, 8 * g), 8 * (g + 1), lambda i: b_home(i, me).start())

    send_home(0)

    gs_t = jnp.transpose(gs[...].astype(F32)).astype(BF16)

    def part_step(j, carry):
        part[:, cols(j)] = nn(gs_t, p_all[:, cols(j)]).astype(BF16)
        return carry

    lax.fori_loop(0, D // CT, part_step, 0)
    low, high = slice(0, PW), slice(PW, D)

    def part_hop(dz_block, columns, dst, dz, k):
        return z_copy(part.at[block_rows(dz_block), columns], dst, zg_s, zg_r, dz, k)

    pt_out = [
        part_hop(2, low, relay_in.at[0], 1, 0),
        part_hop(2, high, relay_in.at[1], 3, 1),
        part_hop(1, high, part_in.at[0, :, high], 1, 2),
        part_hop(3, low, part_in.at[1, :, low], 3, 3),
        part_hop(1, low, part_in.at[0, :, low], 1, 4),
        part_hop(3, high, part_in.at[1, :, high], 3, 5),
    ]
    for copy in pt_out[:4]:
        copy.start()

    for g in range(1, 4):
        send_home(g)
    b_back[mine, :] = b_ret[0:16, :]

    pt_out[0].wait_recv()
    up = part[block_rows(1), low].astype(F32) + relay_in[0].astype(F32)
    part[block_rows(1), low] = up.astype(BF16)
    pt_out[4].start()
    pt_out[1].wait_recv()
    down = part[block_rows(3), high].astype(F32) + relay_in[1].astype(F32)
    part[block_rows(3), high] = down.astype(BF16)
    pt_out[5].start()
    for copy in pt_out[2:]:
        copy.wait_recv()
    for e in range(8):
        ec = slice(e * QW, (e + 1) * QW)
        acc = part[block_rows(0), ec].astype(F32)
        for i in range(2):
            acc = acc + part_in[i, :, ec].astype(F32)
        gq_stack[e * 64 : (e + 1) * 64, :] = acc.astype(BF16)
    a_ret[...] = tn(sel_q[...], gq_stack[...]).astype(BF16)
    steps(1, NB, lambda i: a_home(i, me).start())
    a_back[mine, :] = a_ret[0:16, :]
    steps(1, NB, lambda i: b_home(i, partner(i)).wait_recv())
    for j in range(PW // CT):
        got = tn(g_p[...], b_back[:, j * CT : (j + 1) * CT]).astype(BF16)
        for h in range(2):
            columns = slice(h * PW + j * CT, h * PW + (j + 1) * CT)
            p_grad[:, columns] = got[h * 128 : (h + 1) * 128, :]
    steps(1, NB, lambda i: a_home(i, partner(i)).wait_recv())

    steps(1, NB, lambda i: a_out(i).wait_send())
    steps(1, NB, lambda i: m_out(i).wait_send())
    steps(1, NB, lambda i: b_out(i).wait_send())
    steps(1, NB, lambda i: b_home(i, me).wait_send())
    steps(1, NB, lambda i: a_home(i, me).wait_send())
    for copy in q_out + pt_out:
        copy.wait_send()
    for dz in (1, 3, 2):
        st_out[dz].wait_send()


def unpack(a_back, p_grad, g_q, outq_hbm, outp_hbm, q_buf, sem):
    copies = []
    for h in range(8):
        rows = slice(h * 16, (h + 1) * 16)
        copies.append(pltpu.make_async_copy(p_grad.at[rows, :], outp_hbm.at[rows, :], sem.at[h]))
        copies[-1].start()
    back = tn(g_q[...], a_back[...]).astype(BF16)
    for e in range(8):
        q_buf[:, e * QW : (e + 1) * QW] = back[e * 32 : (e + 1) * 32, :]
    for h in range(2):
        rows = slice(h * 16, (h + 1) * 16)
        copies.append(pltpu.make_async_copy(q_buf.at[rows, :], outq_hbm.at[rows, :], sem.at[8 + h]))
        copies[-1].start()
    for copy in copies:
        copy.wait()


def per_device(queries, passages, query_cluster, passage_cluster, allowed, positive):
    vm = pltpu.VMEM
    dma = pltpu.SemaphoreType.DMA
    hbm = pl.BlockSpec(memory_space=pl.ANY)
    res = pl.BlockSpec(memory_space=vm)
    landed = pl.pallas_call(
        kernel,
        out_shape=(
            pltpu.VMEM((512, QW), BF16),
            pltpu.VMEM((128, D), BF16),
            pltpu.VMEM((512, 256), BF16),
        ),
        in_specs=[pl.BlockSpec(memory_space=pltpu.HBM)] * 6,
        out_specs=(res,) * 3,
        scratch_shapes=[
            vm((512, PW), BF16), vm((512, 256), BF16),
            vm((512, QW), BF16), vm((512, QW), BF16),
            vm((512, PW), BF16), vm((512, PW), BF16),
            vm((512, QW), BF16), vm((512, PW), BF16),
            vm((256, QW), BF16), vm((256, PW), BF16), vm((512, QW), BF16),
            vm((512, 512), BF16),
            vm((16, 256), I32), vm((128, 256), BF16),
            vm((1, 32), I32), vm((1, 32), I32), vm((1, 128), I32),
            vm((NB, 1, 128), F32), vm((NB, 1, 128), F32), vm((NB, 128), F32),
            vm((256, D + 128), BF16), vm((D, 256), BF16), vm((256, D), BF16),
            vm((256, 256), F32), vm((256, 256), F32), vm((256, 256), F32),
            vm((256, 256), BF16),
            vm((256, D), BF16), vm((2, 64, PW), BF16), vm((2, 64, D), BF16),
            vm((8, 256), F32), vm((3, 8, 256), F32),
        ]
        + [dma((NB,))] * 10
        + [dma((24,))] * 2
        + [dma((3,))] * 2
        + [dma((6,))] * 2
        + [dma((14,))],
        compiler_params=pltpu.CompilerParams(
            collective_id=0, has_side_effects=True, vmem_limit_bytes=54 * 1024 * 1024
        ),
        name="contrastive",
    )(
        queries,
        passages,
        query_cluster.reshape(1, -1),
        positive.reshape(1, -1),
        passage_cluster.reshape(1, -1),
        allowed.T,
    )
    return pl.pallas_call(
        unpack,
        out_shape=(
            jax.ShapeDtypeStruct(queries.shape, BF16),
            jax.ShapeDtypeStruct(passages.shape, BF16),
        ),
        in_specs=[res] * 3,
        out_specs=(hbm, hbm),
        scratch_shapes=[vm((32, D), BF16), dma((10,))],
        compiler_params=pltpu.CompilerParams(vmem_limit_bytes=16 * 1024 * 1024),
        name="unpack",
    )(*landed)


def solution(mesh):
    rows = P(("pb", "pa"), None)
    flat = P(("pb", "pa"))
    return jax.shard_map(
        per_device,
        mesh=mesh,
        in_specs=(rows, rows, flat, flat, P(), flat),
        out_specs=(rows, rows),
        check_vma=False,
    )
```

```python
import functools

import jax
import jax.numpy as jnp
from jax import lax
from jax.experimental import pallas as pl
from jax.experimental.pallas import tpu as pltpu
from jax.sharding import PartitionSpec as P

MESH = pl.DeviceIdType.MESH
F32, BF16, I32 = jnp.float32, jnp.bfloat16, jnp.int32
D = 4096
NB = 32
NZ = 4
QW = 512
PW = 2048
CT = 512
SCALE = 50.0
FILL = -1e30


def iota(shape, dim):
    return lax.broadcasted_iota(I32, shape, dim)


def shr(a, n):
    return lax.shift_right_logical(a, jnp.full(a.shape, n, I32))


def hot(cond):
    return jnp.where(cond, 1.0, 0.0).astype(BF16)


def nn(a, b):
    return lax.dot_general(a, b, (((1,), (0,)), ((), ())), preferred_element_type=F32)


def nt(a, b):
    return lax.dot_general(a, b, (((1,), (1,)), ((), ())), preferred_element_type=F32)


def tn(a, b):
    return lax.dot_general(a, b, (((0,), (0,)), ((), ())), preferred_element_type=F32)


def cols(j, width=CT):
    return pl.ds(pl.multiple_of(j * width, width), width)


def rows16(i):
    return pl.ds(pl.multiple_of(i * 16, 16), 16)


def offset(i):
    dc = ((i + 15) // 16) % 2
    j = (i + 15 * dc) % 16
    dx = j % 4
    return dx, (dx + 4 - j // 4) % 4, dc


def hops(i):
    dx, dy, _ = offset(i)
    return min(dx, 4 - dx) + min(dy, 4 - dy)


FAR_FIRST = sorted(range(1, NB), key=hops, reverse=True)


def kernel(
    q_hbm, p_hbm, qc_hbm, pos_hbm, pc_hbm, allowed_hbm,
    a_back, p_grad, g_q,
    b_back, g_p, a_send, a_recv, b_send, b_recv, a_ret, b_ret,
    q_stack, p_stack, gq_stack, sel_q, allow_int, allow_buf, qc_buf, pos_buf, pc_buf, m_send, m_recv, m_flat,
    q_all, q_t, p_all, score, live, target, gs, part, relay_in, part_in, stat, stat_in,
    as_s, as_r, ms_s, ms_r, bs_s, bs_r, ar_s, ar_r, br_s, br_r, zq_s, zq_r, zs_s, zs_r, zg_s, zg_r, in_sem,
):
    me = lax.axis_index("pb")
    z = lax.axis_index("pa")
    x, y, c = me // 8, (me // 2) % 4, me % 2

    def partner(i):
        dx, dy, dc = offset(i)
        return ((x + dx) % 4) * 8 + ((y + dy) % 4) * 2 + (c + dc) % 2

    def origin(i):
        dx, dy, dc = offset(i)
        return ((x + 4 - dx) % 4) * 8 + ((y + 4 - dy) % 4) * 2 + (c + dc) % 2

    barrier = pltpu.get_barrier_semaphore()
    for i in FAR_FIRST:
        pl.semaphore_signal(barrier, inc=1, device_id=(partner(i), z), device_id_type=MESH)
    for dz in (2, 1, 3):
        pl.semaphore_signal(barrier, inc=1, device_id=(me, (z + dz) % NZ), device_id_type=MESH)

    loads = [
        pltpu.make_async_copy(qc_hbm, qc_buf, in_sem.at[0]),
        pltpu.make_async_copy(pos_hbm, pos_buf, in_sem.at[1]),
        pltpu.make_async_copy(pc_hbm, pc_buf, in_sem.at[2]),
        pltpu.make_async_copy(allowed_hbm, allow_int, in_sem.at[3]),
    ]
    for e in range(8):
        loads.append(
            pltpu.make_async_copy(
                q_hbm.at[:, e * QW : (e + 1) * QW],
                q_stack.at[e * 32 : (e + 1) * 32, :],
                in_sem.at[4 + e],
            )
        )
    for h in range(2):
        loads.append(
            pltpu.make_async_copy(
                p_hbm.at[:, h * PW : (h + 1) * PW],
                p_stack.at[h * 128 : (h + 1) * 128, :],
                in_sem.at[12 + h],
            )
        )
    for load in loads:
        load.start()

    for load in loads[:4]:
        load.wait()
    qc_row, pos_row, pc_row = qc_buf[...], pos_buf[...], pc_buf[...]
    lane32, sub32 = iota((32, 32), 1), iota((32, 32), 0)
    qc_col = jnp.sum(jnp.where(lane32 == sub32, qc_row, 0), axis=1, keepdims=True)
    pos_col = jnp.sum(jnp.where(lane32 == sub32, pos_row, 0), axis=1, keepdims=True)
    qb_row, qb_col = shr(qc_row, 3), shr(qc_col, 3)
    q_before = jnp.where((qb_col == qb_row) & (sub32 < lane32), 1, 0)
    q_slot = qb_row * 2 + jnp.sum(q_before, axis=0, keepdims=True)
    lane128, sub128 = iota((128, 128), 1), iota((128, 128), 0)
    pc_col = jnp.sum(jnp.where(lane128 == sub128, pc_row, 0), axis=1, keepdims=True)
    pb_row, pb_col = shr(pc_row, 2), shr(pc_col, 2)
    p_before = jnp.where((pb_col == pb_row) & (sub128 < lane128), 1, 0)
    p_slot = pb_row * 2 + jnp.sum(p_before, axis=0, keepdims=True)

    spread = hot(iota((32, 256), 0) == (iota((32, 256), 1) & 31))
    q_slot8 = nn(jnp.broadcast_to(q_slot, (8, 32)).astype(F32).astype(BF16), spread)[0:1, :]
    big_r, big_c = iota((512, 256), 0), iota((512, 256), 1)
    g_q[...] = hot(
        (q_slot8 == shr(big_r, 3).astype(F32)) & (shr(big_c, 5) == (big_r & 7))
    )
    half_r = iota((512, 128), 0)
    here = p_slot == shr(half_r, 4) * 8 + (half_r & 7)
    g_p[:, 0:128] = hot(here & ((half_r & 8) == 0))
    g_p[:, 128:256] = hot(here & ((half_r & 8) == 8))

    allow_buf[...] = jnp.zeros_like(allow_buf)
    table = allow_int[...].astype(F32).astype(BF16)
    allow_buf[16:32, :] = table
    allow_buf[32:48, :] = table
    reach = nt(hot(iota((32, 256), 1) == qc_col), allow_buf[...])
    q_slot_col = jnp.sum(jnp.where(lane32 == sub32, q_slot, 0), axis=1, keepdims=True)
    p_slot_col = jnp.sum(jnp.where(lane128 == sub128, p_slot, 0), axis=1, keepdims=True)
    l32 = iota((32, 128), 1)
    second = q_slot_col & 1
    q_num = jnp.where(shr(l32, 4) == 1 + second, reach, 0.0)
    q_num = jnp.where(l32 == 48 + second, (pos_col & 127).astype(F32) + 1.0, q_num)
    q_num = jnp.where(l32 == 50 + second, shr(pos_col, 7).astype(F32), q_num).astype(BF16)
    kth = p_slot_col & 7
    p_num = jnp.where(lane128 == kth, sub128.astype(F32) + 1.0, 0.0)
    p_num = jnp.where(lane128 == 8 + kth, (pc_col & 15).astype(F32), p_num).astype(BF16)
    to_q = hot(shr(q_slot, 1) == iota((32, 32), 0))
    to_p = hot(shr(p_slot, 3) == iota((32, 128), 0))
    m_flat[...] = nn(to_p, p_num) + nn(to_q, q_num)

    def spread_rows(i, carry):
        m_send[i] = m_flat[pl.ds(i, 1), :]
        return carry

    lax.fori_loop(0, NB, spread_rows, 0)
    m_flat[...] = jnp.zeros_like(m_flat)
    for load in loads[4:12]:
        load.wait()
    a_send[...] = nn(g_q[...], q_stack[...]).astype(BF16)

    for load in loads[12:]:
        load.wait()

    def pack_p(j, carry):
        b_send[:, cols(j)] = nn(g_p[...], p_stack[:, cols(j)]).astype(BF16)
        return carry

    lax.fori_loop(0, 2, pack_p, 0)
    pl.semaphore_wait(barrier, NB - 1 + NZ - 1)

    def out_copy(src, dst, send, recv, i):
        d = partner(i)
        return pltpu.make_async_remote_copy(
            src_ref=src.at[rows16(d), :],
            dst_ref=dst.at[rows16(i), :],
            send_sem=send.at[i],
            recv_sem=recv.at[i],
            device_id=(d, z),
            device_id_type=MESH,
        )

    def m_out(i):
        d = partner(i)
        return pltpu.make_async_remote_copy(
            src_ref=m_send.at[d],
            dst_ref=m_recv.at[i],
            send_sem=ms_s.at[i],
            recv_sem=ms_r.at[i],
            device_id=(d, z),
            device_id_type=MESH,
        )

    def back_copy(src, dst, send, recv, i, place):
        return pltpu.make_async_remote_copy(
            src_ref=src.at[rows16(i), :],
            dst_ref=dst.at[rows16(place), :],
            send_sem=send.at[i],
            recv_sem=recv.at[i],
            device_id=(origin(i), z),
            device_id_type=MESH,
        )

    def steps(lo, hi, act):
        def body(i, carry):
            act(i)
            return carry

        lax.fori_loop(lo, hi, body, 0)

    a_out = functools.partial(out_copy, a_send, a_recv, as_s, as_r)
    b_out = functools.partial(out_copy, b_send, b_recv, bs_s, bs_r)
    a_home = functools.partial(back_copy, a_ret, a_back, ar_s, ar_r)
    b_home = functools.partial(back_copy, b_ret, b_back, br_s, br_r)

    def z_copy(src, dst, send, recv, dz, k=None):
        k = dz - 1 if k is None else k
        return pltpu.make_async_remote_copy(
            src_ref=src,
            dst_ref=dst,
            send_sem=send.at[k],
            recv_sem=recv.at[k],
            device_id=(me, (z + dz) % NZ),
            device_id_type=MESH,
        )

    def block_rows(dz):
        return pl.ds(pl.multiple_of(((z + dz) % NZ) * 64, 64), 64)

    mine = rows16(me)
    def send_queries(i):
        a_out(i).start()
        m_out(i).start()

    steps(1, NB, send_queries)
    lax.fori_loop(2, PW // CT, pack_p, 0)
    steps(1, NB, lambda i: b_out(i).start())
    a_recv[0:16, :] = a_send[mine, :]
    m_recv[0] = m_send[me]
    b_recv[0:16, :] = b_send[mine, :]

    sr, sc = iota((512, 512), 0), iota((512, 512), 1)
    sel_q[...] = hot((shr(sr, 6) == (sc & 7)) & ((sr & 63) == shr(sc, 3)))
    wr, wc = iota((128, 128), 0), iota((128, 128), 1)
    sel_w = hot((shr(wr, 4) == (wc & 7)) & ((wr & 15) == shr(wc, 3)))
    fr, fc = iota((128, 128), 0), iota((128, 128), 1)
    pick = [
        hot(
            ((fr == 16 + 16 * r + fc) & (fc < 16))
            | ((fr == 48 + r) & (fc == 16))
            | ((fr == 50 + r) & (fc == 17))
        )
        for r in range(2)
    ]
    first = (iota((16, 128), 0) & 1) == 0

    left, right = slice(0, PW), slice(PW, D + 128)

    def group_rows(dz, g):
        return pl.ds(pl.multiple_of(((z + dz) % NZ) * 64 + g * 16, 16), 16)

    def q_hop(dz_block, columns, dz, k, g):
        piece = q_all.at[group_rows(dz_block, g), columns]
        return z_copy(piece, piece, zq_s, zq_r, dz, g * 6 + k)

    q_out = []

    def send_on(copy):
        copy.start()
        q_out.append(copy)

    def relay(g):
        q_hop(3, left, 1, 0, g).wait_recv()
        send_on(q_hop(3, left, 1, 2, g))
        q_hop(1, right, 3, 3, g).wait_recv()
        send_on(q_hop(1, right, 3, 5, g))

    for g in range(4):
        def take(i):
            m_flat[pl.ds(i, 1), :] = m_recv[i]

        def await_queries(i):
            a_out(i).wait_recv()
            m_out(i).wait_recv()

        steps(max(1, 8 * g), 8 * (g + 1), await_queries)
        steps(8 * g, 8 * (g + 1), take)
        come = slice(128 * g, 128 * (g + 1))
        whole = nn(sel_w, a_recv[come, :]).astype(BF16)
        rows = group_rows(0, g)
        for e in range(8):
            q_all[rows, e * QW : (e + 1) * QW] = whole[e * 16 : (e + 1) * 16, :]
        twice = hot(iota((16, 32), 1) == 8 * g + shr(iota((16, 32), 0), 1))
        nums = nn(twice, m_flat[...].astype(BF16)).astype(BF16)
        q_all[rows, D:] = jnp.where(first, nn(nums, pick[0]), nn(nums, pick[1])).astype(BF16)
        send_on(q_hop(0, left, 1, 0, g))
        send_on(q_hop(0, right, 3, 3, g))
        send_on(q_hop(0, right, 1, 1, g))
        send_on(q_hop(0, left, 3, 4, g))
        if g:
            relay(g - 1)
    relay(3)
    ur, uc = iota((64, 128), 0), iota((64, 128), 1)
    pair = (shr(ur, 3) == shr(uc, 4)) & ((ur & 7) == (uc & 7))
    sel_u = [hot(pair & ((uc & 8) == 8 * h)) for h in range(2)]

    def arrive(g, lo):
        steps(lo, 8 * (g + 1), lambda i: b_out(i).wait_recv())
        for j in range(PW // CT):
            got = b_recv[g * 128 : (g + 1) * 128, j * CT : (j + 1) * CT]
            for h in range(2):
                columns = slice(h * PW + j * CT, h * PW + (j + 1) * CT)
                p_all[g * 64 : (g + 1) * 64, columns] = nn(sel_u[h], got).astype(BF16)

    def score_rows(lo, hi):
        acc = nn(p_all[lo:hi, 0:CT], q_t[0:CT, :])
        for j in range(1, D // CT):
            acc = acc + nn(p_all[lo:hi, j * CT : (j + 1) * CT], q_t[j * CT : (j + 1) * CT, :])
        return acc * SCALE

    def row_stats(s, lo, hi):
        permitted = live[lo:hi, :] > 0.5
        top = jnp.max(jnp.where(permitted, s, FILL), axis=0, keepdims=True)
        e = jnp.where(permitted, jnp.exp(s - top), 0.0)
        return top, jnp.sum(e, axis=0, keepdims=True), e

    for g in range(3):
        arrive(g, max(1, 8 * g))

    for g in range(4):
        q_hop(3, right, 1, 1, g).wait_recv()
        q_hop(1, left, 3, 4, g).wait_recv()
        q_hop(2, left, 1, 2, g).wait_recv()
        q_hop(2, right, 3, 5, g).wait_recv()

    qm = q_all[:, D:]
    eightfold = hot(iota((256, 32), 1) == shr(iota((256, 32), 0), 3))
    p_nums = nn(eightfold, m_flat[...].astype(BF16))
    l256, k256 = iota((256, 128), 1), iota((256, 128), 0) & 7
    p_lo = jnp.sum(jnp.where(l256 == k256, p_nums, 0.0), axis=1, keepdims=True)
    p_cl = jnp.sum(jnp.where(l256 == 8 + k256, p_nums, 0.0), axis=1, keepdims=True)
    reached = nt(hot((l256.astype(F32) == p_cl) & (p_lo > 0.5)), qm)
    live[...] = jnp.where(reached > 0.5, 1.0, 0.0)
    er, el = iota((8, 128), 0), iota((8, 128), 1)
    q_dig = nt(hot((er < 2) & (el == 16 + er)), qm)
    q_lo, q_hi = q_dig[0:1, :], q_dig[1:2, :]
    q_code = jnp.where(q_lo > 0.5, q_hi * 256.0 + q_lo, -2.0)
    slot = shr(iota((256, 1), 0), 3)
    dc = shr(slot + 15, 4) & 1
    j = (slot + 15 * dc) & 15
    dx = j & 3
    dy = (dx - shr(j, 2)) & 3
    p_dev = (((x - dx) & 3) * 8 + ((y - dy) & 3) * 2 + ((c + dc) & 1)) * NZ + z
    p_code = jnp.where(p_lo > 0.5, p_dev.astype(F32) * 256.0 + p_lo, -1.0)
    target[...] = jnp.where(p_code == q_code, SCALE, 0.0)

    def turn(j, carry):
        q_t[cols(j), :] = jnp.transpose(q_all[:, cols(j)].astype(F32)).astype(BF16)
        return carry

    lax.fori_loop(0, D // CT, turn, 0)
    top_a, total_a, e_a = row_stats(score_rows(0, 192), 0, 192)
    score[0:192, :] = e_a
    arrive(3, 24)
    top_b, total_b, e_b = row_stats(score_rows(192, 256), 192, 256)
    top = jnp.maximum(top_a, top_b)
    fix_a, fix_b = jnp.exp(top_a - top), jnp.exp(top_b - top)
    total = total_a * fix_a + total_b * fix_b

    stat[0:1, :] = top
    stat[1:2, :] = total
    stat[2:8, :] = jnp.zeros((6, 256), F32)
    st_out = {dz: z_copy(stat, stat_in.at[dz - 1], zs_s, zs_r, dz) for dz in (1, 3, 2)}
    for dz in (2, 1, 3):
        st_out[dz].start()
    score[192:256, :] = e_b
    for dz in (1, 3, 2):
        st_out[dz].wait_recv()
    tops = [top] + [stat_in[i, 0:1, :] for i in range(3)]
    sums = [total] + [stat_in[i, 1:2, :] for i in range(3)]
    row_top = jnp.maximum(jnp.maximum(tops[0], tops[1]), jnp.maximum(tops[2], tops[3]))
    row_total = sum(l * jnp.exp(m - row_top) for m, l in zip(tops, sums))
    share = SCALE * jnp.exp(top - row_top) / jnp.where(row_total > 0.0, row_total, 1.0)
    gs[0:192, :] = (score[0:192, :] * (share * fix_a) - target[0:192, :]).astype(BF16)
    gs[192:256, :] = (score[192:256, :] * (share * fix_b) - target[192:256, :]).astype(BF16)

    dr, dq = iota((128, 64), 0), iota((128, 64), 1)
    same = (shr(dr, 4) == shr(dq, 3)) & ((dr & 7) == (dq & 7))
    dup = [hot(same & ((dr & 8) == 8 * h)) for h in range(2)]

    def send_home(g):
        part_gs = gs[g * 64 : (g + 1) * 64, :]
        halves = [nn(dup[h], part_gs).astype(BF16) for h in range(2)]
        for j in range(PW // CT):
            acc = nn(halves[0], q_all[:, j * CT : (j + 1) * CT])
            acc = acc + nn(halves[1], q_all[:, PW + j * CT : PW + (j + 1) * CT])
            b_ret[g * 128 : (g + 1) * 128, j * CT : (j + 1) * CT] = acc.astype(BF16)
        steps(max(1, 8 * g), 8 * (g + 1), lambda i: b_home(i, me).start())

    send_home(0)

    gs_t = jnp.transpose(gs[...].astype(F32)).astype(BF16)

    def part_step(j, carry):
        part[:, cols(j)] = nn(gs_t, p_all[:, cols(j)]).astype(BF16)
        return carry

    lax.fori_loop(0, D // CT, part_step, 0)
    low, high = slice(0, PW), slice(PW, D)

    def part_hop(dz_block, columns, dst, dz, k):
        return z_copy(part.at[block_rows(dz_block), columns], dst, zg_s, zg_r, dz, k)

    pt_out = [
        part_hop(2, low, relay_in.at[0], 1, 0),
        part_hop(2, high, relay_in.at[1], 3, 1),
        part_hop(1, high, part_in.at[0, :, high], 1, 2),
        part_hop(3, low, part_in.at[1, :, low], 3, 3),
        part_hop(1, low, part_in.at[0, :, low], 1, 4),
        part_hop(3, high, part_in.at[1, :, high], 3, 5),
    ]
    for copy in pt_out[:4]:
        copy.start()

    for g in range(1, 4):
        send_home(g)
    b_back[mine, :] = b_ret[0:16, :]

    pt_out[0].wait_recv()
    up = part[block_rows(1), low].astype(F32) + relay_in[0].astype(F32)
    part[block_rows(1), low] = up.astype(BF16)
    pt_out[4].start()
    pt_out[1].wait_recv()
    down = part[block_rows(3), high].astype(F32) + relay_in[1].astype(F32)
    part[block_rows(3), high] = down.astype(BF16)
    pt_out[5].start()
    for copy in pt_out[2:]:
        copy.wait_recv()
    for e in range(8):
        ec = slice(e * QW, (e + 1) * QW)
        acc = part[block_rows(0), ec].astype(F32)
        for i in range(2):
            acc = acc + part_in[i, :, ec].astype(F32)
        gq_stack[e * 64 : (e + 1) * 64, :] = acc.astype(BF16)
    a_ret[...] = tn(sel_q[...], gq_stack[...]).astype(BF16)
    steps(1, NB, lambda i: a_home(i, me).start())
    a_back[mine, :] = a_ret[0:16, :]
    steps(1, NB, lambda i: b_home(i, partner(i)).wait_recv())
    for j in range(PW // CT):
        got = tn(g_p[...], b_back[:, j * CT : (j + 1) * CT]).astype(BF16)
        for h in range(2):
            columns = slice(h * PW + j * CT, h * PW + (j + 1) * CT)
            p_grad[:, columns] = got[h * 128 : (h + 1) * 128, :]
    steps(1, NB, lambda i: a_home(i, partner(i)).wait_recv())

    steps(1, NB, lambda i: a_out(i).wait_send())
    steps(1, NB, lambda i: m_out(i).wait_send())
    steps(1, NB, lambda i: b_out(i).wait_send())
    steps(1, NB, lambda i: b_home(i, me).wait_send())
    steps(1, NB, lambda i: a_home(i, me).wait_send())
    for copy in q_out + pt_out:
        copy.wait_send()
    for dz in (1, 3, 2):
        st_out[dz].wait_send()


def unpack(a_back, p_grad, g_q, outq_hbm, outp_hbm, q_buf, sem):
    copies = []
    for h in range(8):
        rows = slice(h * 16, (h + 1) * 16)
        copies.append(pltpu.make_async_copy(p_grad.at[rows, :], outp_hbm.at[rows, :], sem.at[h]))
        copies[-1].start()
    back = tn(g_q[...], a_back[...]).astype(BF16)
    for e in range(8):
        q_buf[:, e * QW : (e + 1) * QW] = back[e * 32 : (e + 1) * 32, :]
    for h in range(2):
        rows = slice(h * 16, (h + 1) * 16)
        copies.append(pltpu.make_async_copy(q_buf.at[rows, :], outq_hbm.at[rows, :], sem.at[8 + h]))
        copies[-1].start()
    for copy in copies:
        copy.wait()


def per_device(queries, passages, query_cluster, passage_cluster, allowed, positive):
    vm = pltpu.VMEM
    dma = pltpu.SemaphoreType.DMA
    hbm = pl.BlockSpec(memory_space=pl.ANY)
    res = pl.BlockSpec(memory_space=vm)
    landed = pl.pallas_call(
        kernel,
        out_shape=(
            pltpu.VMEM((512, QW), BF16),
            pltpu.VMEM((128, D), BF16),
            pltpu.VMEM((512, 256), BF16),
        ),
        in_specs=[pl.BlockSpec(memory_space=pltpu.HBM)] * 6,
        out_specs=(res,) * 3,
        scratch_shapes=[
            vm((512, PW), BF16), vm((512, 256), BF16),
            vm((512, QW), BF16), vm((512, QW), BF16),
            vm((512, PW), BF16), vm((512, PW), BF16),
            vm((512, QW), BF16), vm((512, PW), BF16),
            vm((256, QW), BF16), vm((256, PW), BF16), vm((512, QW), BF16),
            vm((512, 512), BF16),
            vm((16, 256), I32), vm((128, 256), BF16),
            vm((1, 32), I32), vm((1, 32), I32), vm((1, 128), I32),
            vm((NB, 1, 128), F32), vm((NB, 1, 128), F32), vm((NB, 128), F32),
            vm((256, D + 128), BF16), vm((D, 256), BF16), vm((256, D), BF16),
            vm((256, 256), F32), vm((256, 256), F32), vm((256, 256), F32),
            vm((256, 256), BF16),
            vm((256, D), BF16), vm((2, 64, PW), BF16), vm((2, 64, D), BF16),
            vm((8, 256), F32), vm((3, 8, 256), F32),
        ]
        + [dma((NB,))] * 10
        + [dma((24,))] * 2
        + [dma((3,))] * 2
        + [dma((6,))] * 2
        + [dma((14,))],
        compiler_params=pltpu.CompilerParams(
            collective_id=0, has_side_effects=True, vmem_limit_bytes=54 * 1024 * 1024
        ),
        name="contrastive",
    )(
        queries,
        passages,
        query_cluster.reshape(1, -1),
        positive.reshape(1, -1),
        passage_cluster.reshape(1, -1),
        allowed.T,
    )
    return pl.pallas_call(
        unpack,
        out_shape=(
            jax.ShapeDtypeStruct(queries.shape, BF16),
            jax.ShapeDtypeStruct(passages.shape, BF16),
        ),
        in_specs=[res] * 3,
        out_specs=(hbm, hbm),
        scratch_shapes=[vm((32, D), BF16), dma((10,))],
        compiler_params=pltpu.CompilerParams(vmem_limit_bytes=16 * 1024 * 1024),
        name="unpack",
    )(*landed)


def solution(mesh):
    rows = P(("pb", "pa"), None)
    flat = P(("pb", "pa"))
    return jax.shard_map(
        per_device,
        mesh=mesh,
        in_specs=(rows, rows, flat, flat, P(), flat),
        out_specs=(rows, rows),
        check_vma=False,
    )
```

```python
import functools

import jax
import jax.numpy as jnp
from jax import lax
from jax.experimental import pallas as pl
from jax.experimental.pallas import tpu as pltpu
from jax.sharding import PartitionSpec as P

MESH = pl.DeviceIdType.MESH
F32, BF16, I32 = jnp.float32, jnp.bfloat16, jnp.int32
D = 4096
NB = 32
NZ = 4
QW = 512
PW = 2048
CT = 512
SCALE = 50.0
FILL = -1e30


def iota(shape, dim):
    return lax.broadcasted_iota(I32, shape, dim)


def shr(a, n):
    return lax.shift_right_logical(a, jnp.full(a.shape, n, I32))


def hot(cond):
    return jnp.where(cond, 1.0, 0.0).astype(BF16)


def nn(a, b):
    return lax.dot_general(a, b, (((1,), (0,)), ((), ())), preferred_element_type=F32)


def nt(a, b):
    return lax.dot_general(a, b, (((1,), (1,)), ((), ())), preferred_element_type=F32)


def tn(a, b):
    return lax.dot_general(a, b, (((0,), (0,)), ((), ())), preferred_element_type=F32)


def cols(j, width=CT):
    return pl.ds(pl.multiple_of(j * width, width), width)


def rows16(i):
    return pl.ds(pl.multiple_of(i * 16, 16), 16)


def offset(i):
    dc = ((i + 15) // 16) % 2
    j = (i + 15 * dc) % 16
    dx = j % 4
    return dx, (dx + 4 - j // 4) % 4, dc


def hops(i):
    dx, dy, _ = offset(i)
    return min(dx, 4 - dx) + min(dy, 4 - dy)


FAR_FIRST = sorted(range(1, NB), key=hops, reverse=True)


def kernel(
    q_hbm, p_hbm, qc_hbm, pos_hbm, pc_hbm, allowed_hbm,
    a_back, p_grad, g_q,
    b_back, g_p, a_send, a_recv, b_send, b_recv, a_ret, b_ret,
    q_stack, p_stack, gq_stack, sel_q, allow_int, allow_buf, qc_buf, pos_buf, pc_buf, m_send, m_recv, m_flat,
    q_all, q_t, p_all, score, live, target, gs, part, relay_in, part_in, stat, stat_in,
    as_s, as_r, ms_s, ms_r, bs_s, bs_r, ar_s, ar_r, br_s, br_r, zq_s, zq_r, zs_s, zs_r, zg_s, zg_r, in_sem,
):
    me = lax.axis_index("pb")
    z = lax.axis_index("pa")
    x, y, c = me // 8, (me // 2) % 4, me % 2

    def partner(i):
        dx, dy, dc = offset(i)
        return ((x + dx) % 4) * 8 + ((y + dy) % 4) * 2 + (c + dc) % 2

    def origin(i):
        dx, dy, dc = offset(i)
        return ((x + 4 - dx) % 4) * 8 + ((y + 4 - dy) % 4) * 2 + (c + dc) % 2

    barrier = pltpu.get_barrier_semaphore()
    for i in FAR_FIRST:
        pl.semaphore_signal(barrier, inc=1, device_id=(partner(i), z), device_id_type=MESH)
    for dz in (2, 1, 3):
        pl.semaphore_signal(barrier, inc=1, device_id=(me, (z + dz) % NZ), device_id_type=MESH)

    loads = [
        pltpu.make_async_copy(qc_hbm, qc_buf, in_sem.at[0]),
        pltpu.make_async_copy(pos_hbm, pos_buf, in_sem.at[1]),
        pltpu.make_async_copy(pc_hbm, pc_buf, in_sem.at[2]),
        pltpu.make_async_copy(allowed_hbm, allow_int, in_sem.at[3]),
    ]
    for e in range(8):
        loads.append(
            pltpu.make_async_copy(
                q_hbm.at[:, e * QW : (e + 1) * QW],
                q_stack.at[e * 32 : (e + 1) * 32, :],
                in_sem.at[4 + e],
            )
        )
    for h in range(2):
        loads.append(
            pltpu.make_async_copy(
                p_hbm.at[:, h * PW : (h + 1) * PW],
                p_stack.at[h * 128 : (h + 1) * 128, :],
                in_sem.at[12 + h],
            )
        )
    for load in loads:
        load.start()

    for load in loads[:4]:
        load.wait()
    qc_row, pos_row, pc_row = qc_buf[...], pos_buf[...], pc_buf[...]
    lane32, sub32 = iota((32, 32), 1), iota((32, 32), 0)
    qc_col = jnp.sum(jnp.where(lane32 == sub32, qc_row, 0), axis=1, keepdims=True)
    pos_col = jnp.sum(jnp.where(lane32 == sub32, pos_row, 0), axis=1, keepdims=True)
    qb_row, qb_col = shr(qc_row, 3), shr(qc_col, 3)
    q_before = jnp.where((qb_col == qb_row) & (sub32 < lane32), 1, 0)
    q_slot = qb_row * 2 + jnp.sum(q_before, axis=0, keepdims=True)
    lane128, sub128 = iota((128, 128), 1), iota((128, 128), 0)
    pc_col = jnp.sum(jnp.where(lane128 == sub128, pc_row, 0), axis=1, keepdims=True)
    pb_row, pb_col = shr(pc_row, 2), shr(pc_col, 2)
    p_before = jnp.where((pb_col == pb_row) & (sub128 < lane128), 1, 0)
    p_slot = pb_row * 2 + jnp.sum(p_before, axis=0, keepdims=True)

    spread = hot(iota((32, 256), 0) == (iota((32, 256), 1) & 31))
    q_slot8 = nn(jnp.broadcast_to(q_slot, (8, 32)).astype(F32).astype(BF16), spread)[0:1, :]
    big_r, big_c = iota((512, 256), 0), iota((512, 256), 1)
    g_q[...] = hot(
        (q_slot8 == shr(big_r, 3).astype(F32)) & (shr(big_c, 5) == (big_r & 7))
    )
    half_r = iota((512, 128), 0)
    here = p_slot == shr(half_r, 4) * 8 + (half_r & 7)
    g_p[:, 0:128] = hot(here & ((half_r & 8) == 0))
    g_p[:, 128:256] = hot(here & ((half_r & 8) == 8))

    allow_buf[...] = jnp.zeros_like(allow_buf)
    table = allow_int[...].astype(F32).astype(BF16)
    allow_buf[16:32, :] = table
    allow_buf[32:48, :] = table
    reach = nt(hot(iota((32, 256), 1) == qc_col), allow_buf[...])
    q_slot_col = jnp.sum(jnp.where(lane32 == sub32, q_slot, 0), axis=1, keepdims=True)
    p_slot_col = jnp.sum(jnp.where(lane128 == sub128, p_slot, 0), axis=1, keepdims=True)
    l32 = iota((32, 128), 1)
    second = q_slot_col & 1
    q_num = jnp.where(shr(l32, 4) == 1 + second, reach, 0.0)
    q_num = jnp.where(l32 == 48 + second, (pos_col & 127).astype(F32) + 1.0, q_num)
    q_num = jnp.where(l32 == 50 + second, shr(pos_col, 7).astype(F32), q_num).astype(BF16)
    kth = p_slot_col & 7
    p_num = jnp.where(lane128 == kth, sub128.astype(F32) + 1.0, 0.0)
    p_num = jnp.where(lane128 == 8 + kth, (pc_col & 15).astype(F32), p_num).astype(BF16)
    to_q = hot(shr(q_slot, 1) == iota((32, 32), 0))
    to_p = hot(shr(p_slot, 3) == iota((32, 128), 0))
    m_flat[...] = nn(to_p, p_num) + nn(to_q, q_num)

    def spread_rows(i, carry):
        m_send[i] = m_flat[pl.ds(i, 1), :]
        return carry

    lax.fori_loop(0, NB, spread_rows, 0)
    m_flat[...] = jnp.zeros_like(m_flat)
    for load in loads[4:12]:
        load.wait()
    a_send[...] = nn(g_q[...], q_stack[...]).astype(BF16)

    for load in loads[12:]:
        load.wait()

    def pack_p(j, carry):
        b_send[:, cols(j)] = nn(g_p[...], p_stack[:, cols(j)]).astype(BF16)
        return carry

    lax.fori_loop(0, 2, pack_p, 0)
    pl.semaphore_wait(barrier, NB - 1 + NZ - 1)

    def out_copy(src, dst, send, recv, i):
        d = partner(i)
        return pltpu.make_async_remote_copy(
            src_ref=src.at[rows16(d), :],
            dst_ref=dst.at[rows16(i), :],
            send_sem=send.at[i],
            recv_sem=recv.at[i],
            device_id=(d, z),
            device_id_type=MESH,
        )

    def m_out(i):
        d = partner(i)
        return pltpu.make_async_remote_copy(
            src_ref=m_send.at[d],
            dst_ref=m_recv.at[i],
            send_sem=ms_s.at[i],
            recv_sem=ms_r.at[i],
            device_id=(d, z),
            device_id_type=MESH,
        )

    def back_copy(src, dst, send, recv, i, place):
        return pltpu.make_async_remote_copy(
            src_ref=src.at[rows16(i), :],
            dst_ref=dst.at[rows16(place), :],
            send_sem=send.at[i],
            recv_sem=recv.at[i],
            device_id=(origin(i), z),
            device_id_type=MESH,
        )

    def steps(lo, hi, act):
        def body(i, carry):
            act(i)
            return carry

        lax.fori_loop(lo, hi, body, 0)

    a_out = functools.partial(out_copy, a_send, a_recv, as_s, as_r)
    b_out = functools.partial(out_copy, b_send, b_recv, bs_s, bs_r)
    a_home = functools.partial(back_copy, a_ret, a_back, ar_s, ar_r)
    b_home = functools.partial(back_copy, b_ret, b_back, br_s, br_r)

    def z_copy(src, dst, send, recv, dz, k=None):
        k = dz - 1 if k is None else k
        return pltpu.make_async_remote_copy(
            src_ref=src,
            dst_ref=dst,
            send_sem=send.at[k],
            recv_sem=recv.at[k],
            device_id=(me, (z + dz) % NZ),
            device_id_type=MESH,
        )

    def block_rows(dz):
        return pl.ds(pl.multiple_of(((z + dz) % NZ) * 64, 64), 64)

    mine = rows16(me)
    def send_queries(i):
        a_out(i).start()
        m_out(i).start()

    steps(1, NB, send_queries)
    lax.fori_loop(2, PW // CT, pack_p, 0)
    steps(1, NB, lambda i: b_out(i).start())
    a_recv[0:16, :] = a_send[mine, :]
    m_recv[0] = m_send[me]
    b_recv[0:16, :] = b_send[mine, :]

    sr, sc = iota((512, 512), 0), iota((512, 512), 1)
    sel_q[...] = hot((shr(sr, 6) == (sc & 7)) & ((sr & 63) == shr(sc, 3)))
    wr, wc = iota((128, 128), 0), iota((128, 128), 1)
    sel_w = hot((shr(wr, 4) == (wc & 7)) & ((wr & 15) == shr(wc, 3)))
    fr, fc = iota((128, 128), 0), iota((128, 128), 1)
    pick = [
        hot(
            ((fr == 16 + 16 * r + fc) & (fc < 16))
            | ((fr == 48 + r) & (fc == 16))
            | ((fr == 50 + r) & (fc == 17))
        )
        for r in range(2)
    ]
    first = (iota((16, 128), 0) & 1) == 0

    left, right = slice(0, PW), slice(PW, D + 128)

    def group_rows(dz, g):
        return pl.ds(pl.multiple_of(((z + dz) % NZ) * 64 + g * 16, 16), 16)

    def q_hop(dz_block, columns, dz, k, g):
        piece = q_all.at[group_rows(dz_block, g), columns]
        return z_copy(piece, piece, zq_s, zq_r, dz, g * 6 + k)

    q_out = []

    def send_on(copy):
        copy.start()
        q_out.append(copy)

    def relay(g):
        q_hop(3, left, 1, 0, g).wait_recv()
        send_on(q_hop(3, left, 1, 2, g))
        q_hop(1, right, 3, 3, g).wait_recv()
        send_on(q_hop(1, right, 3, 5, g))

    for g in range(4):
        def take(i):
            m_flat[pl.ds(i, 1), :] = m_recv[i]

        def await_queries(i):
            a_out(i).wait_recv()
            m_out(i).wait_recv()

        steps(max(1, 8 * g), 8 * (g + 1), await_queries)
        steps(8 * g, 8 * (g + 1), take)
        come = slice(128 * g, 128 * (g + 1))
        whole = nn(sel_w, a_recv[come, :]).astype(BF16)
        rows = group_rows(0, g)
        for e in range(8):
            q_all[rows, e * QW : (e + 1) * QW] = whole[e * 16 : (e + 1) * 16, :]
        twice = hot(iota((16, 32), 1) == 8 * g + shr(iota((16, 32), 0), 1))
        nums = nn(twice, m_flat[...].astype(BF16)).astype(BF16)
        q_all[rows, D:] = jnp.where(first, nn(nums, pick[0]), nn(nums, pick[1])).astype(BF16)
        send_on(q_hop(0, left, 1, 0, g))
        send_on(q_hop(0, right, 3, 3, g))
        send_on(q_hop(0, right, 1, 1, g))
        send_on(q_hop(0, left, 3, 4, g))
        if g:
            relay(g - 1)
    relay(3)
    ur, uc = iota((64, 128), 0), iota((64, 128), 1)
    pair = (shr(ur, 3) == shr(uc, 4)) & ((ur & 7) == (uc & 7))
    sel_u = [hot(pair & ((uc & 8) == 8 * h)) for h in range(2)]

    def arrive(g, lo):
        steps(lo, 8 * (g + 1), lambda i: b_out(i).wait_recv())
        for j in range(PW // CT):
            got = b_recv[g * 128 : (g + 1) * 128, j * CT : (j + 1) * CT]
            for h in range(2):
                columns = slice(h * PW + j * CT, h * PW + (j + 1) * CT)
                p_all[g * 64 : (g + 1) * 64, columns] = nn(sel_u[h], got).astype(BF16)

    def score_rows(lo, hi):
        acc = nn(p_all[lo:hi, 0:CT], q_t[0:CT, :])
        for j in range(1, D // CT):
            acc = acc + nn(p_all[lo:hi, j * CT : (j + 1) * CT], q_t[j * CT : (j + 1) * CT, :])
        return acc * SCALE

    def row_stats(s, lo, hi):
        permitted = live[lo:hi, :] > 0.5
        top = jnp.max(jnp.where(permitted, s, FILL), axis=0, keepdims=True)
        e = jnp.where(permitted, jnp.exp(s - top), 0.0)
        return top, jnp.sum(e, axis=0, keepdims=True), e

    for g in range(3):
        arrive(g, max(1, 8 * g))

    for g in range(4):
        q_hop(3, right, 1, 1, g).wait_recv()
        q_hop(1, left, 3, 4, g).wait_recv()
        q_hop(2, left, 1, 2, g).wait_recv()
        q_hop(2, right, 3, 5, g).wait_recv()

    qm = q_all[:, D:]
    eightfold = hot(iota((256, 32), 1) == shr(iota((256, 32), 0), 3))
    p_nums = nn(eightfold, m_flat[...].astype(BF16))
    l256, k256 = iota((256, 128), 1), iota((256, 128), 0) & 7
    p_lo = jnp.sum(jnp.where(l256 == k256, p_nums, 0.0), axis=1, keepdims=True)
    p_cl = jnp.sum(jnp.where(l256 == 8 + k256, p_nums, 0.0), axis=1, keepdims=True)
    reached = nt(hot((l256.astype(F32) == p_cl) & (p_lo > 0.5)), qm)
    live[...] = jnp.where(reached > 0.5, 1.0, 0.0)
    er, el = iota((8, 128), 0), iota((8, 128), 1)
    q_dig = nt(hot((er < 2) & (el == 16 + er)), qm)
    q_lo, q_hi = q_dig[0:1, :], q_dig[1:2, :]
    q_code = jnp.where(q_lo > 0.5, q_hi * 256.0 + q_lo, -2.0)
    slot = shr(iota((256, 1), 0), 3)
    dc = shr(slot + 15, 4) & 1
    j = (slot + 15 * dc) & 15
    dx = j & 3
    dy = (dx - shr(j, 2)) & 3
    p_dev = (((x - dx) & 3) * 8 + ((y - dy) & 3) * 2 + ((c + dc) & 1)) * NZ + z
    p_code = jnp.where(p_lo > 0.5, p_dev.astype(F32) * 256.0 + p_lo, -1.0)
    target[...] = jnp.where(p_code == q_code, SCALE, 0.0)

    def turn(j, carry):
        q_t[cols(j), :] = jnp.transpose(q_all[:, cols(j)].astype(F32)).astype(BF16)
        return carry

    lax.fori_loop(0, D // CT, turn, 0)
    top_a, total_a, e_a = row_stats(score_rows(0, 192), 0, 192)
    score[0:192, :] = e_a
    arrive(3, 24)
    top_b, total_b, e_b = row_stats(score_rows(192, 256), 192, 256)
    top = jnp.maximum(top_a, top_b)
    fix_a, fix_b = jnp.exp(top_a - top), jnp.exp(top_b - top)
    total = total_a * fix_a + total_b * fix_b

    stat[0:1, :] = top
    stat[1:2, :] = total
    stat[2:8, :] = jnp.zeros((6, 256), F32)
    st_out = {dz: z_copy(stat, stat_in.at[dz - 1], zs_s, zs_r, dz) for dz in (1, 3, 2)}
    for dz in (2, 1, 3):
        st_out[dz].start()
    score[192:256, :] = e_b
    for dz in (1, 3, 2):
        st_out[dz].wait_recv()
    tops = [top] + [stat_in[i, 0:1, :] for i in range(3)]
    sums = [total] + [stat_in[i, 1:2, :] for i in range(3)]
    row_top = jnp.maximum(jnp.maximum(tops[0], tops[1]), jnp.maximum(tops[2], tops[3]))
    row_total = sum(l * jnp.exp(m - row_top) for m, l in zip(tops, sums))
    share = SCALE * jnp.exp(top - row_top) / jnp.where(row_total > 0.0, row_total, 1.0)
    gs[0:192, :] = (score[0:192, :] * (share * fix_a) - target[0:192, :]).astype(BF16)
    gs[192:256, :] = (score[192:256, :] * (share * fix_b) - target[192:256, :]).astype(BF16)

    dr, dq = iota((128, 64), 0), iota((128, 64), 1)
    same = (shr(dr, 4) == shr(dq, 3)) & ((dr & 7) == (dq & 7))
    dup = [hot(same & ((dr & 8) == 8 * h)) for h in range(2)]

    def send_home(g):
        part_gs = gs[g * 64 : (g + 1) * 64, :]
        halves = [nn(dup[h], part_gs).astype(BF16) for h in range(2)]
        for j in range(PW // CT):
            acc = nn(halves[0], q_all[:, j * CT : (j + 1) * CT])
            acc = acc + nn(halves[1], q_all[:, PW + j * CT : PW + (j + 1) * CT])
            b_ret[g * 128 : (g + 1) * 128, j * CT : (j + 1) * CT] = acc.astype(BF16)
        steps(max(1, 8 * g), 8 * (g + 1), lambda i: b_home(i, me).start())

    send_home(0)

    gs_t = jnp.transpose(gs[...].astype(F32)).astype(BF16)

    def part_step(j, carry):
        part[:, cols(j)] = nn(gs_t, p_all[:, cols(j)]).astype(BF16)
        return carry

    lax.fori_loop(0, D // CT, part_step, 0)
    low, high = slice(0, PW), slice(PW, D)

    def part_hop(dz_block, columns, dst, dz, k):
        return z_copy(part.at[block_rows(dz_block), columns], dst, zg_s, zg_r, dz, k)

    pt_out = [
        part_hop(2, low, relay_in.at[0], 1, 0),
        part_hop(2, high, relay_in.at[1], 3, 1),
        part_hop(1, high, part_in.at[0, :, high], 1, 2),
        part_hop(3, low, part_in.at[1, :, low], 3, 3),
        part_hop(1, low, part_in.at[0, :, low], 1, 4),
        part_hop(3, high, part_in.at[1, :, high], 3, 5),
    ]
    for copy in pt_out[:4]:
        copy.start()

    for g in range(1, 4):
        send_home(g)
    b_back[mine, :] = b_ret[0:16, :]

    steps(1, NB, lambda i: a_out(i).wait_send())
    steps(1, NB, lambda i: m_out(i).wait_send())
    steps(1, NB, lambda i: b_out(i).wait_send())
    for copy in q_out:
        copy.wait_send()
    for dz in (1, 3, 2):
        st_out[dz].wait_send()

    pt_out[0].wait_recv()
    up = part[block_rows(1), low].astype(F32) + relay_in[0].astype(F32)
    part[block_rows(1), low] = up.astype(BF16)
    pt_out[4].start()
    pt_out[1].wait_recv()
    down = part[block_rows(3), high].astype(F32) + relay_in[1].astype(F32)
    part[block_rows(3), high] = down.astype(BF16)
    pt_out[5].start()
    for copy in pt_out[2:]:
        copy.wait_recv()
    for e in range(8):
        ec = slice(e * QW, (e + 1) * QW)
        acc = part[block_rows(0), ec].astype(F32)
        for i in range(2):
            acc = acc + part_in[i, :, ec].astype(F32)
        gq_stack[e * 64 : (e + 1) * 64, :] = acc.astype(BF16)
    a_ret[...] = tn(sel_q[...], gq_stack[...]).astype(BF16)
    steps(1, NB, lambda i: a_home(i, me).start())
    a_back[mine, :] = a_ret[0:16, :]
    for copy in pt_out:
        copy.wait_send()
    steps(1, NB, lambda i: b_home(i, partner(i)).wait_recv())
    for j in range(PW // CT):
        got = tn(g_p[...], b_back[:, j * CT : (j + 1) * CT]).astype(BF16)
        for h in range(2):
            columns = slice(h * PW + j * CT, h * PW + (j + 1) * CT)
            p_grad[:, columns] = got[h * 128 : (h + 1) * 128, :]
    steps(1, NB, lambda i: b_home(i, me).wait_send())
    steps(1, NB, lambda i: a_home(i, me).wait_send())
    steps(1, NB, lambda i: a_home(i, partner(i)).wait_recv())


def unpack(a_back, p_grad, g_q, outq_hbm, outp_hbm, q_buf, sem):
    copies = []
    for h in range(8):
        rows = slice(h * 16, (h + 1) * 16)
        copies.append(pltpu.make_async_copy(p_grad.at[rows, :], outp_hbm.at[rows, :], sem.at[h]))
        copies[-1].start()
    back = tn(g_q[...], a_back[...]).astype(BF16)
    for e in range(8):
        q_buf[:, e * QW : (e + 1) * QW] = back[e * 32 : (e + 1) * 32, :]
    for h in range(2):
        rows = slice(h * 16, (h + 1) * 16)
        copies.append(pltpu.make_async_copy(q_buf.at[rows, :], outq_hbm.at[rows, :], sem.at[8 + h]))
        copies[-1].start()
    for copy in copies:
        copy.wait()


def per_device(queries, passages, query_cluster, passage_cluster, allowed, positive):
    vm = pltpu.VMEM
    dma = pltpu.SemaphoreType.DMA
    hbm = pl.BlockSpec(memory_space=pl.ANY)
    res = pl.BlockSpec(memory_space=vm)
    landed = pl.pallas_call(
        kernel,
        out_shape=(
            pltpu.VMEM((512, QW), BF16),
            pltpu.VMEM((128, D), BF16),
            pltpu.VMEM((512, 256), BF16),
        ),
        in_specs=[pl.BlockSpec(memory_space=pltpu.HBM)] * 6,
        out_specs=(res,) * 3,
        scratch_shapes=[
            vm((512, PW), BF16), vm((512, 256), BF16),
            vm((512, QW), BF16), vm((512, QW), BF16),
            vm((512, PW), BF16), vm((512, PW), BF16),
            vm((512, QW), BF16), vm((512, PW), BF16),
            vm((256, QW), BF16), vm((256, PW), BF16), vm((512, QW), BF16),
            vm((512, 512), BF16),
            vm((16, 256), I32), vm((128, 256), BF16),
            vm((1, 32), I32), vm((1, 32), I32), vm((1, 128), I32),
            vm((NB, 1, 128), F32), vm((NB, 1, 128), F32), vm((NB, 128), F32),
            vm((256, D + 128), BF16), vm((D, 256), BF16), vm((256, D), BF16),
            vm((256, 256), F32), vm((256, 256), F32), vm((256, 256), F32),
            vm((256, 256), BF16),
            vm((256, D), BF16), vm((2, 64, PW), BF16), vm((2, 64, D), BF16),
            vm((8, 256), F32), vm((3, 8, 256), F32),
        ]
        + [dma((NB,))] * 10
        + [dma((24,))] * 2
        + [dma((3,))] * 2
        + [dma((6,))] * 2
        + [dma((14,))],
        compiler_params=pltpu.CompilerParams(
            collective_id=0, has_side_effects=True, vmem_limit_bytes=54 * 1024 * 1024
        ),
        name="contrastive",
    )(
        queries,
        passages,
        query_cluster.reshape(1, -1),
        positive.reshape(1, -1),
        passage_cluster.reshape(1, -1),
        allowed.T,
    )
    return pl.pallas_call(
        unpack,
        out_shape=(
            jax.ShapeDtypeStruct(queries.shape, BF16),
            jax.ShapeDtypeStruct(passages.shape, BF16),
        ),
        in_specs=[res] * 3,
        out_specs=(hbm, hbm),
        scratch_shapes=[vm((32, D), BF16), dma((10,))],
        compiler_params=pltpu.CompilerParams(vmem_limit_bytes=16 * 1024 * 1024),
        name="unpack",
    )(*landed)


def solution(mesh):
    rows = P(("pb", "pa"), None)
    flat = P(("pb", "pa"))
    return jax.shard_map(
        per_device,
        mesh=mesh,
        in_specs=(rows, rows, flat, flat, P(), flat),
        out_specs=(rows, rows),
        check_vma=False,
    )
```

```python
import functools

import jax
import jax.numpy as jnp
from jax import lax
from jax.experimental import pallas as pl
from jax.experimental.pallas import tpu as pltpu
from jax.sharding import PartitionSpec as P

MESH = pl.DeviceIdType.MESH
F32, BF16, I32 = jnp.float32, jnp.bfloat16, jnp.int32
D = 4096
NB = 32
NZ = 4
QW = 512
PW = 2048
CT = 512
SCALE = 50.0
FILL = -1e30


def iota(shape, dim):
    return lax.broadcasted_iota(I32, shape, dim)


def shr(a, n):
    return lax.shift_right_logical(a, jnp.full(a.shape, n, I32))


def hot(cond):
    return jnp.where(cond, 1.0, 0.0).astype(BF16)


def nn(a, b):
    return lax.dot_general(a, b, (((1,), (0,)), ((), ())), preferred_element_type=F32)


def nt(a, b):
    return lax.dot_general(a, b, (((1,), (1,)), ((), ())), preferred_element_type=F32)


def tn(a, b):
    return lax.dot_general(a, b, (((0,), (0,)), ((), ())), preferred_element_type=F32)


def cols(j, width=CT):
    return pl.ds(pl.multiple_of(j * width, width), width)


def rows16(i):
    return pl.ds(pl.multiple_of(i * 16, 16), 16)


def offset(i):
    div, rem = (int.__floordiv__, int.__mod__) if isinstance(i, int) else (lax.div, lax.rem)
    dc = rem(div(i + 15, 16), 2)
    j = rem(i + 15 * dc, 16)
    dx = rem(j, 4)
    return dx, rem(dx + 4 - div(j, 4), 4), dc


def hops(i):
    dx, dy, _ = offset(i)
    return min(dx, 4 - dx) + min(dy, 4 - dy)


FAR_FIRST = sorted(range(1, NB), key=hops, reverse=True)


def kernel(
    q_hbm, p_hbm, qc_hbm, pos_hbm, pc_hbm, allowed_hbm,
    a_back, p_grad, g_q,
    b_back, g_p, a_send, a_recv, b_send, b_recv, a_ret, b_ret,
    q_stack, p_stack, gq_stack, sel_q, allow_int, allow_buf, qc_buf, pos_buf, pc_buf, m_send, m_recv, m_flat,
    q_all, q_t, p_all, score, live, target, gs, part, relay_in, part_in, stat, stat_in,
    as_s, as_r, ms_s, ms_r, bs_s, bs_r, ar_s, ar_r, br_s, br_r, zq_s, zq_r, zs_s, zs_r, zg_s, zg_r, in_sem,
):
    me = lax.axis_index("pb")
    z = lax.axis_index("pa")
    x, y, c = me // 8, (me // 2) % 4, me % 2

    def partner(i):
        dx, dy, dc = offset(i)
        return lax.rem(x + dx, 4) * 8 + lax.rem(y + dy, 4) * 2 + lax.rem(c + dc, 2)

    def origin(i):
        dx, dy, dc = offset(i)
        return lax.rem(x + 4 - dx, 4) * 8 + lax.rem(y + 4 - dy, 4) * 2 + lax.rem(c + dc, 2)

    barrier = pltpu.get_barrier_semaphore()
    for i in FAR_FIRST:
        pl.semaphore_signal(barrier, inc=1, device_id=(partner(i), z), device_id_type=MESH)
    for dz in (2, 1, 3):
        pl.semaphore_signal(barrier, inc=1, device_id=(me, (z + dz) % NZ), device_id_type=MESH)

    loads = [
        pltpu.make_async_copy(qc_hbm, qc_buf, in_sem.at[0]),
        pltpu.make_async_copy(pos_hbm, pos_buf, in_sem.at[1]),
        pltpu.make_async_copy(pc_hbm, pc_buf, in_sem.at[2]),
        pltpu.make_async_copy(allowed_hbm, allow_int, in_sem.at[3]),
    ]
    for e in range(8):
        loads.append(
            pltpu.make_async_copy(
                q_hbm.at[:, e * QW : (e + 1) * QW],
                q_stack.at[e * 32 : (e + 1) * 32, :],
                in_sem.at[4 + e],
            )
        )
    for h in range(2):
        loads.append(
            pltpu.make_async_copy(
                p_hbm.at[:, h * PW : (h + 1) * PW],
                p_stack.at[h * 128 : (h + 1) * 128, :],
                in_sem.at[12 + h],
            )
        )
    for load in loads:
        load.start()

    for load in loads[:4]:
        load.wait()
    qc_row, pos_row, pc_row = qc_buf[...], pos_buf[...], pc_buf[...]
    lane32, sub32 = iota((32, 32), 1), iota((32, 32), 0)
    qc_col = jnp.sum(jnp.where(lane32 == sub32, qc_row, 0), axis=1, keepdims=True)
    pos_col = jnp.sum(jnp.where(lane32 == sub32, pos_row, 0), axis=1, keepdims=True)
    qb_row, qb_col = shr(qc_row, 3), shr(qc_col, 3)
    q_before = jnp.where((qb_col == qb_row) & (sub32 < lane32), 1, 0)
    q_slot = qb_row * 2 + jnp.sum(q_before, axis=0, keepdims=True)
    lane128, sub128 = iota((128, 128), 1), iota((128, 128), 0)
    pc_col = jnp.sum(jnp.where(lane128 == sub128, pc_row, 0), axis=1, keepdims=True)
    pb_row, pb_col = shr(pc_row, 2), shr(pc_col, 2)
    p_before = jnp.where((pb_col == pb_row) & (sub128 < lane128), 1, 0)
    p_slot = pb_row * 2 + jnp.sum(p_before, axis=0, keepdims=True)

    spread = hot(iota((32, 256), 0) == (iota((32, 256), 1) & 31))
    q_slot8 = nn(jnp.broadcast_to(q_slot, (8, 32)).astype(F32).astype(BF16), spread)[0:1, :]
    big_r, big_c = iota((512, 256), 0), iota((512, 256), 1)
    g_q[...] = hot(
        (q_slot8 == shr(big_r, 3).astype(F32)) & (shr(big_c, 5) == (big_r & 7))
    )
    half_r = iota((512, 128), 0)
    here = p_slot == shr(half_r, 4) * 8 + (half_r & 7)
    g_p[:, 0:128] = hot(here & ((half_r & 8) == 0))
    g_p[:, 128:256] = hot(here & ((half_r & 8) == 8))

    allow_buf[...] = jnp.zeros_like(allow_buf)
    table = allow_int[...].astype(F32).astype(BF16)
    allow_buf[16:32, :] = table
    allow_buf[32:48, :] = table
    reach = nt(hot(iota((32, 256), 1) == qc_col), allow_buf[...])
    q_slot_col = jnp.sum(jnp.where(lane32 == sub32, q_slot, 0), axis=1, keepdims=True)
    p_slot_col = jnp.sum(jnp.where(lane128 == sub128, p_slot, 0), axis=1, keepdims=True)
    l32 = iota((32, 128), 1)
    second = q_slot_col & 1
    q_num = jnp.where(shr(l32, 4) == 1 + second, reach, 0.0)
    q_num = jnp.where(l32 == 48 + second, (pos_col & 127).astype(F32) + 1.0, q_num)
    q_num = jnp.where(l32 == 50 + second, shr(pos_col, 7).astype(F32), q_num).astype(BF16)
    kth = p_slot_col & 7
    p_num = jnp.where(lane128 == kth, sub128.astype(F32) + 1.0, 0.0)
    p_num = jnp.where(lane128 == 8 + kth, (pc_col & 15).astype(F32), p_num).astype(BF16)
    to_q = hot(shr(q_slot, 1) == iota((32, 32), 0))
    to_p = hot(shr(p_slot, 3) == iota((32, 128), 0))
    m_flat[...] = nn(to_p, p_num) + nn(to_q, q_num)

    def spread_rows(i, carry):
        m_send[i] = m_flat[pl.ds(i, 1), :]
        return carry

    lax.fori_loop(0, NB, spread_rows, 0)
    m_flat[...] = jnp.zeros_like(m_flat)
    for load in loads[4:12]:
        load.wait()
    a_send[...] = nn(g_q[...], q_stack[...]).astype(BF16)

    for load in loads[12:]:
        load.wait()

    def pack_p(j, carry):
        b_send[:, cols(j)] = nn(g_p[...], p_stack[:, cols(j)]).astype(BF16)
        return carry

    lax.fori_loop(0, 2, pack_p, 0)
    pl.semaphore_wait(barrier, NB - 1 + NZ - 1)

    def out_copy(src, dst, send, recv, i):
        d = partner(i)
        return pltpu.make_async_remote_copy(
            src_ref=src.at[rows16(d), :],
            dst_ref=dst.at[rows16(i), :],
            send_sem=send.at[i],
            recv_sem=recv.at[i],
            device_id=(d, z),
            device_id_type=MESH,
        )

    def m_out(i):
        d = partner(i)
        return pltpu.make_async_remote_copy(
            src_ref=m_send.at[d],
            dst_ref=m_recv.at[i],
            send_sem=ms_s.at[i],
            recv_sem=ms_r.at[i],
            device_id=(d, z),
            device_id_type=MESH,
        )

    def back_copy(src, dst, send, recv, i, place):
        return pltpu.make_async_remote_copy(
            src_ref=src.at[rows16(i), :],
            dst_ref=dst.at[rows16(place), :],
            send_sem=send.at[i],
            recv_sem=recv.at[i],
            device_id=(origin(i), z),
            device_id_type=MESH,
        )

    def steps(lo, hi, act):
        def body(i, carry):
            act(i)
            return carry

        lax.fori_loop(lo, hi, body, 0)

    a_out = functools.partial(out_copy, a_send, a_recv, as_s, as_r)
    b_out = functools.partial(out_copy, b_send, b_recv, bs_s, bs_r)
    a_home = functools.partial(back_copy, a_ret, a_back, ar_s, ar_r)
    b_home = functools.partial(back_copy, b_ret, b_back, br_s, br_r)

    def z_copy(src, dst, send, recv, dz, k=None):
        k = dz - 1 if k is None else k
        return pltpu.make_async_remote_copy(
            src_ref=src,
            dst_ref=dst,
            send_sem=send.at[k],
            recv_sem=recv.at[k],
            device_id=(me, (z + dz) % NZ),
            device_id_type=MESH,
        )

    def block_rows(dz):
        return pl.ds(pl.multiple_of(((z + dz) % NZ) * 64, 64), 64)

    mine = rows16(me)
    def send_queries(i):
        a_out(i).start()
        m_out(i).start()

    steps(1, NB, send_queries)
    lax.fori_loop(2, PW // CT, pack_p, 0)
    steps(1, NB, lambda i: b_out(i).start())
    a_recv[0:16, :] = a_send[mine, :]
    m_recv[0] = m_send[me]
    b_recv[0:16, :] = b_send[mine, :]

    sr, sc = iota((512, 512), 0), iota((512, 512), 1)
    sel_q[...] = hot((shr(sr, 6) == (sc & 7)) & ((sr & 63) == shr(sc, 3)))
    wr, wc = iota((128, 128), 0), iota((128, 128), 1)
    sel_w = hot((shr(wr, 4) == (wc & 7)) & ((wr & 15) == shr(wc, 3)))
    fr, fc = iota((128, 128), 0), iota((128, 128), 1)
    pick = [
        hot(
            ((fr == 16 + 16 * r + fc) & (fc < 16))
            | ((fr == 48 + r) & (fc == 16))
            | ((fr == 50 + r) & (fc == 17))
        )
        for r in range(2)
    ]
    first = (iota((16, 128), 0) & 1) == 0

    left, right = slice(0, PW), slice(PW, D + 128)

    def group_rows(dz, g):
        return pl.ds(pl.multiple_of(((z + dz) % NZ) * 64 + g * 16, 16), 16)

    def q_hop(dz_block, columns, dz, k, g):
        piece = q_all.at[group_rows(dz_block, g), columns]
        return z_copy(piece, piece, zq_s, zq_r, dz, g * 6 + k)

    q_out = []

    def send_on(copy):
        copy.start()
        q_out.append(copy)

    def relay(g):
        q_hop(3, left, 1, 0, g).wait_recv()
        send_on(q_hop(3, left, 1, 2, g))
        q_hop(1, right, 3, 3, g).wait_recv()
        send_on(q_hop(1, right, 3, 5, g))

    for g in range(4):
        def take(i):
            m_flat[pl.ds(i, 1), :] = m_recv[i]

        def await_queries(i):
            a_out(i).wait_recv()
            m_out(i).wait_recv()

        steps(max(1, 8 * g), 8 * (g + 1), await_queries)
        steps(8 * g, 8 * (g + 1), take)
        come = slice(128 * g, 128 * (g + 1))
        whole = nn(sel_w, a_recv[come, :]).astype(BF16)
        rows = group_rows(0, g)
        for e in range(8):
            q_all[rows, e * QW : (e + 1) * QW] = whole[e * 16 : (e + 1) * 16, :]
        twice = hot(iota((16, 32), 1) == 8 * g + shr(iota((16, 32), 0), 1))
        nums = nn(twice, m_flat[...].astype(BF16)).astype(BF16)
        q_all[rows, D:] = jnp.where(first, nn(nums, pick[0]), nn(nums, pick[1])).astype(BF16)
        send_on(q_hop(0, left, 1, 0, g))
        send_on(q_hop(0, right, 3, 3, g))
        send_on(q_hop(0, right, 1, 1, g))
        send_on(q_hop(0, left, 3, 4, g))
        if g:
            relay(g - 1)
    relay(3)
    ur, uc = iota((64, 128), 0), iota((64, 128), 1)
    pair = (shr(ur, 3) == shr(uc, 4)) & ((ur & 7) == (uc & 7))
    sel_u = [hot(pair & ((uc & 8) == 8 * h)) for h in range(2)]

    def arrive(g, lo):
        steps(lo, 8 * (g + 1), lambda i: b_out(i).wait_recv())
        for j in range(PW // CT):
            got = b_recv[g * 128 : (g + 1) * 128, j * CT : (j + 1) * CT]
            for h in range(2):
                columns = slice(h * PW + j * CT, h * PW + (j + 1) * CT)
                p_all[g * 64 : (g + 1) * 64, columns] = nn(sel_u[h], got).astype(BF16)

    def score_rows(lo, hi):
        acc = nn(p_all[lo:hi, 0:CT], q_t[0:CT, :])
        for j in range(1, D // CT):
            acc = acc + nn(p_all[lo:hi, j * CT : (j + 1) * CT], q_t[j * CT : (j + 1) * CT, :])
        return acc * SCALE

    def row_stats(s, lo, hi):
        permitted = live[lo:hi, :] > 0.5
        top = jnp.max(jnp.where(permitted, s, FILL), axis=0, keepdims=True)
        e = jnp.where(permitted, jnp.exp(s - top), 0.0)
        return top, jnp.sum(e, axis=0, keepdims=True), e

    for g in range(3):
        arrive(g, max(1, 8 * g))

    for g in range(4):
        q_hop(3, right, 1, 1, g).wait_recv()
        q_hop(1, left, 3, 4, g).wait_recv()
        q_hop(2, left, 1, 2, g).wait_recv()
        q_hop(2, right, 3, 5, g).wait_recv()

    qm = q_all[:, D:]
    eightfold = hot(iota((256, 32), 1) == shr(iota((256, 32), 0), 3))
    p_nums = nn(eightfold, m_flat[...].astype(BF16))
    l256, k256 = iota((256, 128), 1), iota((256, 128), 0) & 7
    p_lo = jnp.sum(jnp.where(l256 == k256, p_nums, 0.0), axis=1, keepdims=True)
    p_cl = jnp.sum(jnp.where(l256 == 8 + k256, p_nums, 0.0), axis=1, keepdims=True)
    reached = nt(hot((l256.astype(F32) == p_cl) & (p_lo > 0.5)), qm)
    live[...] = jnp.where(reached > 0.5, 1.0, 0.0)
    er, el = iota((8, 128), 0), iota((8, 128), 1)
    q_dig = nt(hot((er < 2) & (el == 16 + er)), qm)
    q_lo, q_hi = q_dig[0:1, :], q_dig[1:2, :]
    q_code = jnp.where(q_lo > 0.5, q_hi * 256.0 + q_lo, -2.0)
    slot = shr(iota((256, 1), 0), 3)
    dc = shr(slot + 15, 4) & 1
    j = (slot + 15 * dc) & 15
    dx = j & 3
    dy = (dx - shr(j, 2)) & 3
    p_dev = (((x - dx) & 3) * 8 + ((y - dy) & 3) * 2 + ((c + dc) & 1)) * NZ + z
    p_code = jnp.where(p_lo > 0.5, p_dev.astype(F32) * 256.0 + p_lo, -1.0)
    target[...] = jnp.where(p_code == q_code, SCALE, 0.0)

    def turn(j, carry):
        q_t[cols(j), :] = jnp.transpose(q_all[:, cols(j)].astype(F32)).astype(BF16)
        return carry

    lax.fori_loop(0, D // CT, turn, 0)
    top_a, total_a, e_a = row_stats(score_rows(0, 192), 0, 192)
    score[0:192, :] = e_a
    arrive(3, 24)
    top_b, total_b, e_b = row_stats(score_rows(192, 256), 192, 256)
    top = jnp.maximum(top_a, top_b)
    fix_a, fix_b = jnp.exp(top_a - top), jnp.exp(top_b - top)
    total = total_a * fix_a + total_b * fix_b

    stat[0:1, :] = top
    stat[1:2, :] = total
    stat[2:8, :] = jnp.zeros((6, 256), F32)
    st_out = {dz: z_copy(stat, stat_in.at[dz - 1], zs_s, zs_r, dz) for dz in (1, 3, 2)}
    for dz in (2, 1, 3):
        st_out[dz].start()
    score[192:256, :] = e_b
    for dz in (1, 3, 2):
        st_out[dz].wait_recv()
    tops = [top] + [stat_in[i, 0:1, :] for i in range(3)]
    sums = [total] + [stat_in[i, 1:2, :] for i in range(3)]
    row_top = jnp.maximum(jnp.maximum(tops[0], tops[1]), jnp.maximum(tops[2], tops[3]))
    row_total = sum(l * jnp.exp(m - row_top) for m, l in zip(tops, sums))
    share = SCALE * jnp.exp(top - row_top) / jnp.where(row_total > 0.0, row_total, 1.0)
    gs[0:192, :] = (score[0:192, :] * (share * fix_a) - target[0:192, :]).astype(BF16)
    gs[192:256, :] = (score[192:256, :] * (share * fix_b) - target[192:256, :]).astype(BF16)

    dr, dq = iota((128, 64), 0), iota((128, 64), 1)
    same = (shr(dr, 4) == shr(dq, 3)) & ((dr & 7) == (dq & 7))
    dup = [hot(same & ((dr & 8) == 8 * h)) for h in range(2)]

    def send_home(g):
        part_gs = gs[g * 64 : (g + 1) * 64, :]
        halves = [nn(dup[h], part_gs).astype(BF16) for h in range(2)]
        for j in range(PW // CT):
            acc = nn(halves[0], q_all[:, j * CT : (j + 1) * CT])
            acc = acc + nn(halves[1], q_all[:, PW + j * CT : PW + (j + 1) * CT])
            b_ret[g * 128 : (g + 1) * 128, j * CT : (j + 1) * CT] = acc.astype(BF16)
        steps(max(1, 8 * g), 8 * (g + 1), lambda i: b_home(i, me).start())

    send_home(0)

    gs_t = jnp.transpose(gs[...].astype(F32)).astype(BF16)

    def part_step(j, carry):
        part[:, cols(j)] = nn(gs_t, p_all[:, cols(j)]).astype(BF16)
        return carry

    lax.fori_loop(0, D // CT, part_step, 0)
    low, high = slice(0, PW), slice(PW, D)

    def part_hop(dz_block, columns, dst, dz, k):
        return z_copy(part.at[block_rows(dz_block), columns], dst, zg_s, zg_r, dz, k)

    pt_out = [
        part_hop(2, low, relay_in.at[0], 1, 0),
        part_hop(2, high, relay_in.at[1], 3, 1),
        part_hop(1, high, part_in.at[0, :, high], 1, 2),
        part_hop(3, low, part_in.at[1, :, low], 3, 3),
        part_hop(1, low, part_in.at[0, :, low], 1, 4),
        part_hop(3, high, part_in.at[1, :, high], 3, 5),
    ]
    for copy in pt_out[:4]:
        copy.start()

    for g in range(1, 4):
        send_home(g)
    b_back[mine, :] = b_ret[0:16, :]

    steps(1, NB, lambda i: a_out(i).wait_send())
    steps(1, NB, lambda i: m_out(i).wait_send())
    steps(1, NB, lambda i: b_out(i).wait_send())
    for copy in q_out:
        copy.wait_send()
    for dz in (1, 3, 2):
        st_out[dz].wait_send()

    pt_out[0].wait_recv()
    up = part[block_rows(1), low].astype(F32) + relay_in[0].astype(F32)
    part[block_rows(1), low] = up.astype(BF16)
    pt_out[4].start()
    pt_out[1].wait_recv()
    down = part[block_rows(3), high].astype(F32) + relay_in[1].astype(F32)
    part[block_rows(3), high] = down.astype(BF16)
    pt_out[5].start()
    for copy in pt_out[2:]:
        copy.wait_recv()
    for e in range(8):
        ec = slice(e * QW, (e + 1) * QW)
        acc = part[block_rows(0), ec].astype(F32)
        for i in range(2):
            acc = acc + part_in[i, :, ec].astype(F32)
        gq_stack[e * 64 : (e + 1) * 64, :] = acc.astype(BF16)
    a_ret[...] = tn(sel_q[...], gq_stack[...]).astype(BF16)
    steps(1, NB, lambda i: a_home(i, me).start())
    a_back[mine, :] = a_ret[0:16, :]
    for copy in pt_out:
        copy.wait_send()
    steps(1, NB, lambda i: b_home(i, partner(i)).wait_recv())
    for j in range(PW // CT):
        got = tn(g_p[...], b_back[:, j * CT : (j + 1) * CT]).astype(BF16)
        for h in range(2):
            columns = slice(h * PW + j * CT, h * PW + (j + 1) * CT)
            p_grad[:, columns] = got[h * 128 : (h + 1) * 128, :]
    steps(1, NB, lambda i: b_home(i, me).wait_send())
    steps(1, NB, lambda i: a_home(i, me).wait_send())
    steps(1, NB, lambda i: a_home(i, partner(i)).wait_recv())


def unpack(a_back, p_grad, g_q, outq_hbm, outp_hbm, q_buf, sem):
    copies = []
    for h in range(8):
        rows = slice(h * 16, (h + 1) * 16)
        copies.append(pltpu.make_async_copy(p_grad.at[rows, :], outp_hbm.at[rows, :], sem.at[h]))
        copies[-1].start()
    back = tn(g_q[...], a_back[...]).astype(BF16)
    for e in range(8):
        q_buf[:, e * QW : (e + 1) * QW] = back[e * 32 : (e + 1) * 32, :]
    for h in range(2):
        rows = slice(h * 16, (h + 1) * 16)
        copies.append(pltpu.make_async_copy(q_buf.at[rows, :], outq_hbm.at[rows, :], sem.at[8 + h]))
        copies[-1].start()
    for copy in copies:
        copy.wait()


def per_device(queries, passages, query_cluster, passage_cluster, allowed, positive):
    vm = pltpu.VMEM
    dma = pltpu.SemaphoreType.DMA
    hbm = pl.BlockSpec(memory_space=pl.ANY)
    res = pl.BlockSpec(memory_space=vm)
    landed = pl.pallas_call(
        kernel,
        out_shape=(
            pltpu.VMEM((512, QW), BF16),
            pltpu.VMEM((128, D), BF16),
            pltpu.VMEM((512, 256), BF16),
        ),
        in_specs=[pl.BlockSpec(memory_space=pltpu.HBM)] * 6,
        out_specs=(res,) * 3,
        scratch_shapes=[
            vm((512, PW), BF16), vm((512, 256), BF16),
            vm((512, QW), BF16), vm((512, QW), BF16),
            vm((512, PW), BF16), vm((512, PW), BF16),
            vm((512, QW), BF16), vm((512, PW), BF16),
            vm((256, QW), BF16), vm((256, PW), BF16), vm((512, QW), BF16),
            vm((512, 512), BF16),
            vm((16, 256), I32), vm((128, 256), BF16),
            vm((1, 32), I32), vm((1, 32), I32), vm((1, 128), I32),
            vm((NB, 1, 128), F32), vm((NB, 1, 128), F32), vm((NB, 128), F32),
            vm((256, D + 128), BF16), vm((D, 256), BF16), vm((256, D), BF16),
            vm((256, 256), F32), vm((256, 256), F32), vm((256, 256), F32),
            vm((256, 256), BF16),
            vm((256, D), BF16), vm((2, 64, PW), BF16), vm((2, 64, D), BF16),
            vm((8, 256), F32), vm((3, 8, 256), F32),
        ]
        + [dma((NB,))] * 10
        + [dma((24,))] * 2
        + [dma((3,))] * 2
        + [dma((6,))] * 2
        + [dma((14,))],
        compiler_params=pltpu.CompilerParams(
            collective_id=0, has_side_effects=True, vmem_limit_bytes=54 * 1024 * 1024
        ),
        name="contrastive",
    )(
        queries,
        passages,
        query_cluster.reshape(1, -1),
        positive.reshape(1, -1),
        passage_cluster.reshape(1, -1),
        allowed.T,
    )
    return pl.pallas_call(
        unpack,
        out_shape=(
            jax.ShapeDtypeStruct(queries.shape, BF16),
            jax.ShapeDtypeStruct(passages.shape, BF16),
        ),
        in_specs=[res] * 3,
        out_specs=(hbm, hbm),
        scratch_shapes=[vm((32, D), BF16), dma((10,))],
        compiler_params=pltpu.CompilerParams(vmem_limit_bytes=16 * 1024 * 1024),
        name="unpack",
    )(*landed)


def solution(mesh):
    rows = P(("pb", "pa"), None)
    flat = P(("pb", "pa"))
    return jax.shard_map(
        per_device,
        mesh=mesh,
        in_specs=(rows, rows, flat, flat, P(), flat),
        out_specs=(rows, rows),
        check_vma=False,
    )
```
